128 devices in a mesh: seg: 4 (over z), blk: 32 (over x, y, core).
Axes of the slice: x: 4, y: 4, z: 4, core: 2. Of those that a mesh axis runs over, the one named last changes fastest.
Arguments:
- records: float32 [12, 32768, 512], P('seg', 'blk'), may hold values from -600 to 600, as said below
- pairs: int32 [256, 8], P(('blk', 'seg')), may hold values from 0 to 1, as said below
Outputs:
- forward: float32 [256, 8, 65, 128], P(('blk', 'seg'))
- backward: float32 [256, 8, 65, 128], P(('blk', 'seg'))
The draws below stay inside these ranges and needn't reach their ends.
Inputs may be any that keep to these rules, and one draw needn't show every extreme that they name: records are finite. pairs is 0 where g + d >= 256; among the 16 entries of rows 2 * o to 2 * o + 1 at most 8 are 1, and exactly 8 for some o.
All inputs are finite; a program needn't handle non-finite values.
Results may differ from the reference program's by a relative error of at most 0.0041.
Values may be sent and summed in bfloat16 or wider, within the bound.
No kernel may reach another device: no remote copies, remote signals or barrier semaphores. Data moves between devices by JAX's collectives and lax.ppermute only.
A program may use at most 192 MiB of HBM per device.

```python
import math
import jax
import jax.numpy as jnp
from jax import lax

NF = 256
CB = 128
MAXLAG = 32
REACH = 8
SMOOTH = 32
BAND = 64
PAIR_CAP = 8
BPD = 2
NSEG = 12
NB = 256


def draw_records(key, part):
    key = jax.random.fold_in(key, 1)
    base_key, row_key, time_key = jax.random.split(key, 3)
    shape = (NSEG, NB * CB, 2 * NF)
    base = jnp.clip(jax.random.normal(base_key, shape, jnp.float32), -5.0, 5.0)
    rows = jnp.exp(jax.random.uniform(row_key, (1, NB * CB, 1), jnp.float32, 0.0, math.log(10.0)))
    times = jnp.exp(jax.random.uniform(time_key, (NSEG, 1, 2 * NF), jnp.float32, 0.0, math.log(10.0)))
    return base * rows * times


def draw_pairs(key, part):
    key = jax.random.fold_in(key, 2)
    count_key, chosen_key, score_key = jax.random.split(key, 3)
    owners = NB // BPD
    slots = BPD * REACH
    counts = jnp.minimum(jax.random.randint(count_key, (owners,), 1, 4), PAIR_CAP)
    chosen = jax.random.randint(chosen_key, (), 0, owners // 2)
    counts = jnp.where(jnp.arange(owners) == chosen, PAIR_CAP, counts)
    scores = jax.random.permutation(score_key, owners * slots).reshape(owners, slots)
    lower = jnp.arange(owners)[:, None] * BPD + jnp.arange(slots)[None, :] // REACH
    partner = lower + jnp.arange(slots)[None, :] % REACH + 1
    valid = partner < NB
    scores = jnp.where(valid, scores, scores + owners * slots)
    ranks = jnp.argsort(jnp.argsort(scores, axis=1), axis=1)
    live = (ranks < counts[:, None]) & valid
    return live.astype(jnp.int32).reshape(NB, REACH)


def setup_inputs(seed: int = 0) -> dict:
    key_of = jax.random.split(jax.random.key(seed), 3)
    records = draw_records(jax.random.fold_in(key_of[2], 71), 0)
    pairs = draw_pairs(jax.random.fold_in(key_of[2], 71), 0)
    return {"records": records, "pairs": pairs}


def smooth_table(length, half):
    rows = jnp.arange(length)[:, None]
    cols = jnp.arange(length)[None, :]
    inside = (jnp.abs(rows - cols) <= half).astype(jnp.float32)
    counted = lax.optimization_barrier(jnp.sum(inside, axis=0, keepdims=True))
    return inside / counted

def fourier_table(length, bins):
    times = jnp.arange(length)[:, None]
    freqs = jnp.arange(bins)[None, :]
    phase = (times * freqs % length).astype(jnp.float32) * (2.0 * jnp.pi / length)
    return jnp.concatenate([jnp.cos(phase), -jnp.sin(phase)], axis=1)

def lag_table(length, bins, most_lag):
    freqs = jnp.arange(bins)[:, None]
    shifts = jnp.arange(-most_lag, most_lag + 1)[None, :]
    phase = (freqs * shifts % length).astype(jnp.float32) * (2.0 * jnp.pi / length)
    return jnp.concatenate([jnp.cos(phase), -jnp.sin(phase)], axis=0)

def whiten(samples):
    length = samples.shape[-1]
    bins = length // 2
    flat = samples.reshape(-1, length)
    level = jnp.dot(jnp.abs(flat), smooth_table(length, SMOOTH), precision=lax.Precision.HIGHEST)
    normed = flat / (level + 1e-06)
    spectrum = jnp.dot(normed, fourier_table(length, bins), precision=lax.Precision.HIGHEST)
    square = spectrum * spectrum
    bands = bins // BAND
    power = square[:, :bins].reshape(-1, bands, BAND).sum(-1) + square[:, bins:].reshape(-1, bands, BAND).sum(-1)
    factor = 1.0 / jnp.sqrt(power / (2 * BAND) + 1e-05)
    factor = jnp.concatenate([factor, factor], axis=1)
    white = spectrum.reshape(-1, 2 * bands, BAND) * factor[:, :, None]
    return white.reshape(samples.shape).astype(jnp.bfloat16)

def correlate(own, other):
    bins = own.shape[-1] // 2
    segs = own.shape[0]
    own_re = own[..., :bins].astype(jnp.float32)
    own_im = own[..., bins:].astype(jnp.float32)
    far_re = other[..., :bins].astype(jnp.float32)
    far_im = other[..., bins:].astype(jnp.float32)
    form = 'sjcf,sjdcf->jdcf'
    real = jnp.einsum(form, own_re, far_re) + jnp.einsum(form, own_im, far_im)
    imag = jnp.einsum(form, own_re, far_im) - jnp.einsum(form, own_im, far_re)
    joined = jnp.concatenate([real, imag], axis=-1)
    scale = 1.0 / jnp.sqrt(jnp.float32(segs * bins))
    return jnp.einsum('jdcf,fl->jdlc', joined, lag_table(2 * bins, bins, MAXLAG), precision=lax.Precision.HIGHEST) * scale

def reference(records, pairs):
    white = lax.map(whiten, records)
    segs, _, length = white.shape
    white = white.reshape(segs, NB, CB, length)
    padded = jnp.concatenate([white, jnp.zeros((segs, REACH, CB, length), white.dtype)], axis=1)
    columns = []
    for offset in range(1, REACH + 1):
        other = padded[:, offset:offset + NB]
        columns.append(correlate(white, other[:, :, None])[:, 0])
    live = pairs.astype(jnp.float32)
    forward = jnp.stack(columns, axis=1) * live[:, :, None, None]
    lead = jnp.concatenate([jnp.zeros((REACH,) + forward.shape[1:], jnp.float32), forward], axis=0)
    backward = jnp.stack([lead[REACH - offset:REACH - offset + NB, offset - 1, ::-1] for offset in range(1, REACH + 1)], axis=1)
    return (forward, backward)
```

```python
import functools

import jax
import jax.numpy as jnp
import ml_dtypes
import numpy as np
from jax import lax
from jax.experimental import pallas as pl
from jax.experimental.pallas import tpu as pltpu
from jax.sharding import PartitionSpec as P

BINS = 256
LENGTH = 512
CHANS = 128
MAXLAG = 32
LAGS = 2 * MAXLAG + 1
REACH = 8
SMOOTH = 32
BAND = 64
GROUP = 8
HALF = GROUP // 2
ROWS = 256
SUB = 128
SLOTS = 13
BODY = 64
CHUNK = SLOTS * BODY + 16
SEND2 = 8 * BODY + 16
SEND3 = 4 * BODY + 16
VMEM_LIMIT = 56 * 1024 * 1024
BF = jnp.bfloat16
F32 = jnp.float32


def split(array):
    high = array.astype(ml_dtypes.bfloat16)
    low = (array - high.astype(np.float32)).astype(ml_dtypes.bfloat16)
    return high, low


def tables():
    times = np.arange(LENGTH)
    inside = (np.abs(times[:, None] - times[None, :]) <= SMOOTH).astype(np.float32)
    share = (1.0 / inside.sum(0, keepdims=True)).astype(np.float32)
    band = inside.astype(ml_dtypes.bfloat16)
    phase = (times[:, None] * np.arange(BINS)[None, :] % LENGTH) * (2.0 * np.pi / LENGTH)
    fourier = np.concatenate([np.cos(phase), -np.sin(phase)], axis=1).astype(np.float32)
    fhi, flo = split(fourier)
    which = np.arange(BINS) // BAND
    same = ((which[:, None] == which[None, :]) / (2.0 * BAND)).astype(ml_dtypes.bfloat16)
    return band, share, fhi, flo, same


def lag_rows(segments):
    shifts = np.arange(-MAXLAG, MAXLAG + 1)
    phase = (shifts[:, None] * np.arange(BINS)[None, :] % LENGTH) * (2.0 * np.pi / LENGTH)
    table = np.concatenate([np.cos(phase), -np.sin(phase)], axis=1) / np.sqrt(segments * BINS)
    table = np.concatenate([table, np.zeros((80 - LAGS, LENGTH))], axis=0).astype(np.float32)
    return np.concatenate(split(table), axis=0)


def dot(a, b):
    return jnp.dot(a, b, preferred_element_type=F32)


def dot_nt(a, b):
    return lax.dot_general(a, b, (((1,), (1,)), ((), ())), preferred_element_type=F32)


def halves(x):
    high = x.astype(BF)
    return high, (x - high.astype(F32)).astype(BF)


def whiten_body(half, records, band, share, fhi, flo, same, white):
    del half
    for part in range(ROWS // SUB):
        x = records[0, pl.ds(part * SUB, SUB), :]
        ahi, alo = halves(jnp.abs(x))
        level = (dot(ahi, band[...]) + dot(alo, band[...])) * share[...]
        nhi, nlo = halves(x / (level + 1e-06))
        spectrum = dot(nhi, fhi[...]) + dot(nlo, fhi[...]) + dot(nhi, flo[...])
        re = spectrum[:, :BINS]
        im = spectrum[:, BINS:]
        power = dot((re * re + im * im).astype(BF), same[...])
        factor = lax.rsqrt(power + 1e-05)
        white[part, 0, :, :BINS] = (re * factor).astype(BF)
        white[part, 0, :, BINS:] = (im * factor).astype(BF)


def whiten(half, records, consts):
    segs = records.shape[0]
    steps = HALF * CHANS // ROWS
    per = ROWS // CHANS

    def whole(array):
        return pl.BlockSpec(array.shape, lambda s, i, h: (0, 0))

    return pl.pallas_call(
        whiten_body,
        grid_spec=pltpu.PrefetchScalarGridSpec(
            num_scalar_prefetch=1,
            grid=(segs, steps),
            in_specs=[pl.BlockSpec((1, ROWS, LENGTH), lambda s, i, h: (s, h[0] * steps + i, 0))]
            + [whole(c) for c in consts],
            out_specs=pl.BlockSpec((per, 1, CHANS, LENGTH), lambda s, i, h: (i, s, 0, 0)),
        ),
        out_shape=jax.ShapeDtypeStruct((HALF, segs, CHANS, LENGTH), BF),
        compiler_params=pltpu.CompilerParams(vmem_limit_bytes=VMEM_LIMIT),
        cost_estimate=pl.CostEstimate(
            flops=segs * HALF * CHANS * LENGTH * LENGTH * 11,
            bytes_accessed=segs * HALF * CHANS * LENGTH * 6,
            transcendentals=0,
        ),
        name="whiten",
    )(half, records, *consts)


def row_of(b, p, total):
    return lax.rem(b * GROUP - HALF + p + total, total)


def correlate_body(
    meta, tab, own_ext, own_int, got_ext, got_int, lag, keep, out1, out2, out3, slots, win, stk, pq, cnt, sems
):
    b = meta[0]
    s = meta[1]
    core = meta[2]
    segs = win.shape[1]
    total = tab.shape[0] // REACH

    def load(k, source, quad):
        return pltpu.make_async_copy(source, win.at[pl.ds(quad * HALF, HALF)], sems.at[k])

    copies = [
        load(0, own_ext, 1 + core),
        load(1, own_int, 2 - core),
        load(2, got_ext, 3 * core),
        load(3, got_int, 3 - 3 * core),
    ]
    for copy in copies:
        copy.start()
    for k in range(4):
        cnt[k] = 0
    for copy in copies:
        copy.wait()

    def put(owner, entry, stack):
        n = cnt[owner]
        cnt[owner] = n + 1
        slots[entry] = n
        r = jnp.bitwise_and(owner - s, 3)
        stk[r, pl.ds(pl.multiple_of(n * BODY, BODY), BODY), :] = stack[:BODY]
        stk[r, pl.ds(SLOTS * BODY + n, 1), :] = stack[BODY:LAGS]

    def pair(p, d):
        q = p + d
        for chunk in range(CHANS // 16):
            rows = pl.ds(chunk * 16, 16)
            real = jnp.zeros((16, BINS), F32)
            imag = jnp.zeros((16, BINS), F32)
            for k in range(segs):
                are = win[p, k, rows, :BINS].astype(F32)
                aim = win[p, k, rows, BINS:].astype(F32)
                bre = win[q, k, rows, :BINS].astype(F32)
                bim = win[q, k, rows, BINS:].astype(F32)
                real += are * bre + aim * bim
                imag += are * bim - aim * bre
            rhi, rlo = halves(real)
            ihi, ilo = halves(imag)
            pq[0, rows, :BINS] = rhi
            pq[0, rows, BINS:] = ihi
            pq[1, rows, :BINS] = rlo
            pq[1, rows, BINS:] = ilo
        both = dot_nt(lag[...], pq[0])
        stack = both[:80] + both[80:] + dot_nt(lag[:80], pq[1])
        owner = jnp.where(p < HALF, 2 + p // 2, (p - HALF) // 2)
        put(owner, p * REACH + d - 1, stack)
        far = p - 6
        near = q - 12

        @pl.when((far >= 0) & (far < 2) & (near >= 0) & (near < 2))
        def _():
            put(0, 96 + far * 2 + near, stack)

    def visit(n, carry):
        p = n // REACH
        d = n % REACH + 1
        live = tab[row_of(b, p, total) * REACH + d - 1] != 0
        here = jnp.where(p < HALF, p + d >= HALF, (p + d < 12) | (p < 8))

        @pl.when(live & here)
        def _():
            pair(p, d)

        return carry

    lax.fori_loop(0, 12 * REACH, visit, 0)
    keep[...] = stk[0]
    out1[...] = stk[1].astype(BF)
    out2[...] = stk[2].astype(BF)
    out3[...] = stk[3].astype(BF)


def correlate(meta, tab, own_ext, own_int, got_ext, got_int, lag):
    segs = own_ext.shape[1]
    smem = pl.BlockSpec(memory_space=pltpu.SMEM)
    vmem = pl.BlockSpec(memory_space=pltpu.VMEM)
    hbm = pl.BlockSpec(memory_space=pl.ANY)
    chunk = jax.ShapeDtypeStruct((CHUNK, CHANS), BF)
    return pl.pallas_call(
        correlate_body,
        in_specs=[smem, smem, hbm, hbm, hbm, hbm, vmem],
        out_specs=[vmem, vmem, vmem, vmem, smem],
        out_shape=[
            jax.ShapeDtypeStruct((CHUNK, CHANS), F32),
            chunk,
            chunk,
            chunk,
            jax.ShapeDtypeStruct((128,), jnp.int32),
        ],
        scratch_shapes=[
            pltpu.VMEM((4 * HALF, segs, CHANS, LENGTH), BF),
            pltpu.VMEM((4, CHUNK, CHANS), F32),
            pltpu.VMEM((2, CHANS, LENGTH), BF),
            pltpu.SMEM((4,), jnp.int32),
            pltpu.SemaphoreType.DMA((4,)),
        ],
        compiler_params=pltpu.CompilerParams(vmem_limit_bytes=VMEM_LIMIT),
        name="correlate",
    )(meta, tab, own_ext, own_int, got_ext, got_int, lag)


def combine_body(meta, tab, slots, keep, got1, got2, got3, full, send2, out1, out2, out3, stage2, stage3):
    b = meta[0]
    s = meta[1]
    total = tab.shape[0] // REACH
    full[...] = (keep[...] + got1[...].astype(F32)) + (got2[...].astype(F32) + got3[...].astype(F32))

    def move(entry, p, d, dest, size, k):
        @pl.when(tab[row_of(b, p, total) * REACH + d - 1] != 0)
        def _():
            n = slots[entry]
            dest[pl.ds(k * BODY, BODY), :] = full[pl.ds(pl.multiple_of(n * BODY, BODY), BODY), :]
            dest[pl.ds(size * BODY + k, 1), :] = full[pl.ds(SLOTS * BODY + n, 1), :]

    @pl.when(s >= 2)
    def _():
        stage2[: 8 * BODY, :] = full[: 8 * BODY, :]
        stage2[8 * BODY :, :] = full[SLOTS * BODY :, :]

    for owner in (0, 1):

        @pl.when(s == owner)
        def _(owner=owner):
            for k, (i, j) in enumerate(UPWARD[owner]):
                p, d = HALF + i, GROUP + j - i
                entry = p * REACH + d - 1 if i // 2 == owner else 96 + (i - 2) * 2 + j
                move(entry, p, d, stage2, 8, k)

    send2[...] = stage2[...].astype(send2.dtype)
    for r, out in ((1, out1), (2, out2), (3, out3)):
        to = jnp.bitwise_and(s + r, 3)

        @pl.when((s < to) | (s >= 2))
        def _(r=r, to=to):
            for i in range(2):
                for j in range(2):
                    ahead = s < to
                    row = 2 * s + i
                    p = jnp.where(ahead, HALF + row, row - HALF)
                    d = 2 * to + j - row + jnp.where(ahead, 0, GROUP)
                    move(p * REACH + d - 1, p, d, stage3.at[r - 1], 4, 2 * i + j)

        out[...] = stage3[r - 1].astype(out.dtype)


UPWARD = (
    ((0, 0), (1, 0), (1, 1), (2, 0), (2, 1), (3, 0), (3, 1)),
    ((2, 2), (3, 2), (3, 3)),
)


def combine(meta, tab, slots, keep, got1, got2, got3):
    smem = pl.BlockSpec(memory_space=pltpu.SMEM)
    vmem = pl.BlockSpec(memory_space=pltpu.VMEM)
    third = jax.ShapeDtypeStruct((SEND3, CHANS), BF)
    return pl.pallas_call(
        combine_body,
        in_specs=[smem, smem, smem, vmem, vmem, vmem, vmem],
        out_specs=[vmem] * 5,
        out_shape=[
            jax.ShapeDtypeStruct((CHUNK, CHANS), F32),
            jax.ShapeDtypeStruct((SEND2, CHANS), BF),
            third,
            third,
            third,
        ],
        scratch_shapes=[
            pltpu.VMEM((SEND2, CHANS), F32),
            pltpu.VMEM((3, SEND3, CHANS), F32),
        ],
        compiler_params=pltpu.CompilerParams(vmem_limit_bytes=VMEM_LIMIT),
        name="combine",
    )(meta, tab, slots, keep, got1, got2, got3)


def finish_body(meta, tab, slots, full, got2, got31, got32, got33, fwd, bwd, two, three):
    b = meta[0]
    s = meta[1]
    total = tab.shape[0] // REACH
    two[...] = got2[...].astype(F32)
    three[0] = got31[...].astype(F32)
    three[1] = got32[...].astype(F32)
    three[2] = got33[...].astype(F32)
    fwd[...] = jnp.zeros(fwd.shape, F32)
    bwd[...] = jnp.zeros(bwd.shape, F32)

    def live(p, d):
        return tab[row_of(b, p, total) * REACH + d - 1] != 0

    def ahead(source, size, n, i, d):
        fwd[i, d - 1, pl.ds(0, BODY), :] = source[pl.ds(pl.multiple_of(n * BODY, BODY), BODY), :]
        fwd[i, d - 1, pl.ds(BODY, 1), :] = source[pl.ds(size * BODY + n, 1), :]

    def behind(source, size, n, j, d):
        bwd[j, d - 1, pl.ds(0, 1), :] = source[pl.ds(size * BODY + n, 1), :]
        for m in range(1, LAGS):
            bwd[j, d - 1, pl.ds(m, 1), :] = source[pl.ds(n * BODY + BODY - m, 1), :]

    from_above = jnp.int32(0)
    for i in range(2):
        for d in range(1, REACH + 1):
            row = 2 * s + i
            p = HALF + row
            on = live(p, d)
            crossed = (s >= 2) & (row + d >= GROUP)

            @pl.when(on & jnp.logical_not(crossed))
            def _(i=i, d=d, p=p):
                ahead(full, SLOTS, slots[p * REACH + d - 1], i, d)

            @pl.when(on & crossed)
            def _(i=i, d=d, n=from_above):
                ahead(two, 8, n, i, d)

            from_above = from_above + jnp.where(on & crossed, 1, 0)

    for j in range(2):
        for d in range(1, REACH + 1):
            col = 2 * s + j
            low = col - d
            p = HALF + low
            on = live(p, d)
            before = low < 0
            row = jnp.where(before, low + GROUP, low)
            owner = row // 2
            up = before & (owner < 2)
            mine = (owner == s) & jnp.logical_not(up)

            @pl.when(on & mine)
            def _(j=j, d=d, p=p):
                behind(full, SLOTS, slots[p * REACH + d - 1], j, d)

            @pl.when(on & up)
            def _(j=j, d=d, row=row):
                k0 = jnp.where(row == 0, 0, 2 * row - 1) + j
                k1 = jnp.where(row == 2, 0, 1) + j
                behind(two, 8, jnp.where(s == 0, k0, k1), j, d)

            @pl.when(on & jnp.logical_not(mine) & jnp.logical_not(up))
            def _(j=j, d=d, row=row, owner=owner):
                r = jnp.bitwise_and(s - owner, 3)
                behind(three.at[r - 1], 4, (row - 2 * owner) * 2 + j, j, d)


def finish(meta, tab, slots, full, got2, got31, got32, got33, blocks):
    smem = pl.BlockSpec(memory_space=pltpu.SMEM)
    vmem = pl.BlockSpec(memory_space=pltpu.VMEM)
    out = jax.ShapeDtypeStruct((blocks, REACH, LAGS, CHANS), F32)
    return pl.pallas_call(
        finish_body,
        in_specs=[smem, smem, smem] + [vmem] * 5,
        out_specs=[vmem, vmem],
        out_shape=[out, out],
        scratch_shapes=[
            pltpu.VMEM((SEND2, CHANS), F32),
            pltpu.VMEM((3, SEND3, CHANS), F32),
        ],
        compiler_params=pltpu.CompilerParams(vmem_limit_bytes=VMEM_LIMIT),
        name="finish",
    )(meta, tab, slots, full, got2, got31, got32, got33)


def shards(groups, planes, consts, lag, records, pairs):
    b = lax.axis_index("blk").astype(jnp.int32)
    s = lax.axis_index("seg").astype(jnp.int32)
    core = jnp.bitwise_and(b, 1)
    meta = jnp.stack([b, s, core])
    tab = lax.all_gather(pairs.reshape(-1), ("blk", "seg"), tiled=True)

    outer = [(g, (g + 1) % groups if g % 2 else (g - 1) % groups) for g in range(groups)]
    inner = [(g, g ^ 1) for g in range(groups)]
    own_ext = whiten(core[None], records, consts)
    got_ext = lax.ppermute(own_ext, "blk", outer)
    own_int = whiten((1 - core)[None], records, consts)
    got_int = lax.ppermute(own_int, "blk", inner)
    keep, out1, out2, out3, slots = correlate(meta, tab, own_ext, own_int, got_ext, got_int, lag)

    def ring(x, r):
        return lax.ppermute(x, "seg", [(z, (z + r) % planes) for z in range(planes)])

    full, send2, s31, s32, s33 = combine(
        meta, tab, slots, keep, ring(out1, 1), ring(out2, 2), ring(out3, 3)
    )
    shift = [
        (z * groups + g, z * groups + (g + (1 if z < 2 else -1)) % groups)
        for z in range(planes)
        for g in range(groups)
    ]
    got2 = lax.ppermute(send2, ("seg", "blk"), shift)
    return tuple(
        finish(
            meta, tab, slots, full, got2, ring(s31, 1), ring(s32, 2), ring(s33, 3), pairs.shape[0]
        )
    )


def solution(mesh):
    groups = mesh.shape["blk"]
    planes = mesh.shape["seg"]
    consts = tables()

    def run(records, pairs):
        body = functools.partial(
            shards,
            groups,
            planes,
            tuple(jnp.asarray(c) for c in consts),
            jnp.asarray(lag_rows(records.shape[0])),
        )
        return jax.shard_map(
            body,
            mesh=mesh,
            in_specs=(P("seg", "blk", None), P(("blk", "seg"), None)),
            out_specs=(P(("blk", "seg"), None, None, None), P(("blk", "seg"), None, None, None)),
            check_vma=False,
        )(records, pairs)

    return run
```

```python
import functools

import jax
import jax.numpy as jnp
import ml_dtypes
import numpy as np
from jax import lax
from jax.experimental import pallas as pl
from jax.experimental.pallas import tpu as pltpu
from jax.sharding import PartitionSpec as P

BINS = 256
LENGTH = 512
CHANS = 128
MAXLAG = 32
LAGS = 2 * MAXLAG + 1
REACH = 8
SMOOTH = 32
BAND = 64
GROUP = 8
HALF = GROUP // 2
ROWS = 512
SUB = 256
SLOTS = 8
BODY = 64
CHUNK = SLOTS * BODY + 16
SEND = 4 * BODY + 16
MIB = 1024 * 1024
BF = jnp.bfloat16
F32 = jnp.float32


def split(array):
    high = array.astype(ml_dtypes.bfloat16)
    low = (array - high.astype(np.float32)).astype(ml_dtypes.bfloat16)
    return high, low


def tables():
    times = np.arange(LENGTH)
    inside = (np.abs(times[:, None] - times[None, :]) <= SMOOTH).astype(np.float32)
    share = (1.0 / inside.sum(0, keepdims=True)).astype(np.float32)
    band = inside.astype(ml_dtypes.bfloat16)
    phase = (times[:, None] * np.arange(BINS)[None, :] % LENGTH) * (2.0 * np.pi / LENGTH)
    fourier = np.concatenate([np.cos(phase), -np.sin(phase)], axis=1).astype(np.float32)
    fhi, flo = split(fourier)
    which = np.arange(BINS) // BAND
    same = ((which[:, None] == which[None, :]) / (2.0 * BAND)).astype(ml_dtypes.bfloat16)
    return band, share, fhi, flo, same


def lag_rows(segments):
    shifts = np.arange(-MAXLAG, MAXLAG + 1)
    phase = (shifts[:, None] * np.arange(BINS)[None, :] % LENGTH) * (2.0 * np.pi / LENGTH)
    table = np.concatenate([np.cos(phase), -np.sin(phase)], axis=1) / np.sqrt(segments * BINS)
    table = np.concatenate([table, np.zeros((80 - LAGS, LENGTH))], axis=0).astype(np.float32)
    return np.concatenate(split(table), axis=0)


def dot(a, b):
    return jnp.dot(a, b, preferred_element_type=F32)


def dot_nt(a, b):
    return lax.dot_general(a, b, (((1,), (1,)), ((), ())), preferred_element_type=F32)


def halves(x):
    high = x.astype(BF)
    return high, (x - high.astype(F32)).astype(BF)


def inverse(y):
    r = pl.reciprocal(y, approx=True)
    return r * (2.0 - y * r)


def whiten_body(half, records, band, share, fhi, flo, same, white):
    del half
    parts = range(ROWS // SUB)
    xs = [records[0, pl.ds(k * SUB, SUB), :] for k in parts]
    levels = []
    for x in xs:
        ahi, alo = halves(jnp.abs(x))
        levels.append((dot(ahi, band[...]) + dot(alo, band[...])) * share[...])
    spectra = []
    for x, level in zip(xs, levels):
        nhi, nlo = halves(x * inverse(level + 1e-06))
        spectra.append(dot(nhi, fhi[...]) + dot(nlo, fhi[...]) + dot(nhi, flo[...]))
    for k in parts:
        re = spectra[k][:, :BINS]
        im = spectra[k][:, BINS:]
        power = dot((re * re + im * im).astype(BF), same[...])
        factor = lax.rsqrt(power + 1e-05)
        per = SUB // CHANS
        white[pl.ds(k * per, per), 0, :, :BINS] = (re * factor).astype(BF).reshape(per, CHANS, BINS)
        white[pl.ds(k * per, per), 0, :, BINS:] = (im * factor).astype(BF).reshape(per, CHANS, BINS)


def whiten(half, records, consts):
    segs = records.shape[0]
    steps = HALF * CHANS // ROWS
    per = ROWS // CHANS

    def whole(array):
        return pl.BlockSpec(array.shape, lambda s, i, h: (0, 0))

    return pl.pallas_call(
        whiten_body,
        grid_spec=pltpu.PrefetchScalarGridSpec(
            num_scalar_prefetch=1,
            grid=(segs, steps),
            in_specs=[pl.BlockSpec((1, ROWS, LENGTH), lambda s, i, h: (s, h[0] * steps + i, 0))]
            + [whole(c) for c in consts],
            out_specs=pl.BlockSpec((per, 1, CHANS, LENGTH), lambda s, i, h: (i, s, 0, 0)),
        ),
        out_shape=jax.ShapeDtypeStruct((HALF, segs, CHANS, LENGTH), BF),
        compiler_params=pltpu.CompilerParams(vmem_limit_bytes=57 * MIB),
        cost_estimate=pl.CostEstimate(
            flops=segs * HALF * CHANS * LENGTH * LENGTH * 11,
            bytes_accessed=segs * HALF * CHANS * LENGTH * 6,
            transcendentals=0,
        ),
        name="whiten",
    )(half, records, *consts)


def is_live(tab, s, p, d):
    row = jnp.where(p < HALF, p + HALF, p - HALF)
    base = jnp.where(p < HALF, 0, 4 * CHANS)
    return tab[base + jnp.bitwise_and(s - row // 2, 3) * CHANS + (row % 2) * REACH + d - 1] != 0


INTRA = [(p, d) for p in range(HALF, 12) for d in range(1, REACH + 1) if p + d < 12]
CROSSING = [(p, d) for p in range(HALF) for d in range(1, REACH + 1) if p + d >= HALF] + [
    (p, d) for p in range(HALF, GROUP) for d in range(1, REACH + 1) if p + d >= 12
]


def correlate_body(crossing, meta, codes, tab, *refs):
    s = meta[0]
    core = meta[1]
    if crossing:
        own_ext, own_int, got_ext, got_int = refs[:4]
        refs = refs[4:]
        sources = [(own_ext, 1 + core), (own_int, 2 - core), (got_ext, 3 * core), (got_int, 3 - 3 * core)]
    else:
        own_ext, own_int = refs[:2]
        refs = refs[2:]
        sources = [(own_ext, 1 + core), (own_int, 2 - core)]
    lag, keep, out1, out2, out3, slots, low, high, stk, pq, cnt = refs
    segs = low.shape[0]
    for k in range(4):
        cnt[k] = 0
    cnt[4] = -1

    def grab(dest, block):
        for ref, quad in sources:

            @pl.when(block // HALF == quad)
            def _(ref=ref):
                dest[...] = ref[block % HALF]

    def put(owner, entry, stack):
        n = cnt[owner]
        cnt[owner] = n + 1
        slots[entry] = n
        r = jnp.bitwise_and(owner - s, 3)
        stk[r, pl.ds(pl.multiple_of(n * BODY, BODY), BODY), :] = stack[:BODY]
        stk[r, pl.ds(SLOTS * BODY + n, 1), :] = stack[BODY:LAGS]

    def pair(p, d):
        q = p + d

        @pl.when(cnt[4] != p)
        def _():
            grab(low, p)
            cnt[4] = p

        grab(high, q)
        for chunk in range(CHANS // 16):
            rows = pl.ds(chunk * 16, 16)
            real = jnp.zeros((16, BINS), F32)
            imag = jnp.zeros((16, BINS), F32)
            for k in range(segs):
                are = low[k, rows, :BINS].astype(F32)
                aim = low[k, rows, BINS:].astype(F32)
                bre = high[k, rows, :BINS].astype(F32)
                bim = high[k, rows, BINS:].astype(F32)
                real += are * bre + aim * bim
                imag += are * bim - aim * bre
            rhi, rlo = halves(real)
            ihi, ilo = halves(imag)
            pq[0, rows, :BINS] = rhi
            pq[0, rows, BINS:] = ihi
            pq[1, rows, :BINS] = rlo
            pq[1, rows, BINS:] = ilo
        both = dot_nt(lag[...], pq[0])
        stack = both[:80] + both[80:] + dot_nt(lag[:80], pq[1])
        put(jnp.where(p < HALF, 2 + p // 2, (p - HALF) // 2), p * REACH + d - 1, stack)
        if crossing:
            @pl.when((p >= 6) & (p < 8) & (q >= 12) & (q < 14))
            def _():
                put(0, 96 + (p - 6) * 2 + q - 12, stack)

    def visit(n, carry):
        p = codes[n] // 16
        d = codes[n] % 16

        @pl.when(is_live(tab, s, p, d))
        def _():
            pair(p, d)

        return carry

    lax.fori_loop(0, len(CROSSING if crossing else INTRA), visit, 0)
    keep[...] = stk[0]
    out1[...] = stk[1].astype(BF)
    out2[...] = stk[2].astype(BF)
    out3[...] = stk[3].astype(BF)


SMEM = pl.BlockSpec(memory_space=pltpu.SMEM)
VMEM = pl.BlockSpec(memory_space=pltpu.VMEM)


def correlate(crossing, meta, tab, whites, lag):
    segs = whites[0].shape[1]
    chunk = jax.ShapeDtypeStruct((CHUNK, CHANS), BF)
    entries = CROSSING if crossing else INTRA
    codes = jnp.asarray(np.array([p * 16 + d for p, d in entries] + [0] * (64 - len(entries)), np.int32))
    block = segs * CHANS * LENGTH
    return pl.pallas_call(
        functools.partial(correlate_body, crossing),
        in_specs=[SMEM, SMEM, SMEM] + [VMEM] * (len(whites) + 1),
        out_specs=[VMEM, VMEM, VMEM, VMEM, SMEM],
        out_shape=[
            jax.ShapeDtypeStruct((CHUNK, CHANS), F32),
            chunk,
            chunk,
            chunk,
            jax.ShapeDtypeStruct((128,), jnp.int32),
        ],
        scratch_shapes=[
            pltpu.VMEM((segs, CHANS, LENGTH), BF),
            pltpu.VMEM((segs, CHANS, LENGTH), BF),
            pltpu.VMEM((4, CHUNK, CHANS), F32),
            pltpu.VMEM((2, CHANS, LENGTH), BF),
            pltpu.SMEM((8,), jnp.int32),
        ],
        compiler_params=pltpu.CompilerParams(vmem_limit_bytes=20 * MIB),
        cost_estimate=pl.CostEstimate(flops=8 * 10 * block, bytes_accessed=8 * block, transcendentals=0),
        name="correlate",
    )(meta, codes, tab, *whites, lag)


UPWARD = (
    ((0, 0), (1, 0), (1, 1), (2, 0), (2, 1), (3, 0), (3, 1)),
    ((2, 2), (3, 2), (3, 3)),
)


def combine_body(meta, tab, slots_in, slots_x, keep_in, in1, in2, in3, keep_x, x1, x2, x3, *refs):
    full_in, full_x, send2, out1, out2, out3, stage2, stage3 = refs
    s = meta[0]
    full_in[...] = (keep_in[...] + in1[...].astype(F32)) + (in2[...].astype(F32) + in3[...].astype(F32))
    full_x[...] = (keep_x[...] + x1[...].astype(F32)) + (x2[...].astype(F32) + x3[...].astype(F32))

    def move(full, n, dest, size, k):
        dest[pl.ds(k * BODY, BODY), :] = full[pl.ds(pl.multiple_of(n * BODY, BODY), BODY), :]
        dest[pl.ds(size * BODY + k, 1), :] = full[pl.ds(SLOTS * BODY + n, 1), :]

    @pl.when(s >= 2)
    def _():
        send2[...] = full_x[...].astype(BF)

    for owner in (0, 1):

        @pl.when(s == owner)
        def _(owner=owner):
            for k, (i, j) in enumerate(UPWARD[owner]):
                p, d = HALF + i, GROUP + j - i
                entry = p * REACH + d - 1 if i // 2 == owner else 96 + (i - 2) * 2 + j

                @pl.when(is_live(tab, s, jnp.int32(p), d))
                def _(entry=entry, k=k):
                    move(full_x, slots_x[entry], stage2, SLOTS, k)

            send2[...] = stage2[...].astype(BF)

    for r, out in ((1, out1), (2, out2), (3, out3)):
        to = jnp.bitwise_and(s + r, 3)
        for i in range(2):
            for j in range(2):
                row = 2 * s + i
                d = 2 * to + j - row

                @pl.when((s < to) & is_live(tab, s, HALF + row, d))
                def _(r=r, k=2 * i + j, row=row, d=d):
                    move(full_in, slots_in[(HALF + row) * REACH + d - 1], stage3.at[r - 1], 4, k)

                @pl.when((s > to) & (s >= 2) & is_live(tab, s, row - HALF, d + GROUP))
                def _(r=r, k=2 * i + j, row=row, d=d):
                    move(full_x, slots_x[(row - HALF) * REACH + d + GROUP - 1], stage3.at[r - 1], 4, k)

        out[...] = stage3[r - 1].astype(BF)


def combine(*args):
    third = jax.ShapeDtypeStruct((SEND, CHANS), BF)
    full = jax.ShapeDtypeStruct((CHUNK, CHANS), F32)
    return pl.pallas_call(
        combine_body,
        in_specs=[SMEM] * 4 + [VMEM] * 8,
        out_specs=[VMEM] * 6,
        out_shape=[full, full, jax.ShapeDtypeStruct((CHUNK, CHANS), BF), third, third, third],
        scratch_shapes=[
            pltpu.VMEM((CHUNK, CHANS), F32),
            pltpu.VMEM((3, SEND, CHANS), F32),
        ],
        compiler_params=pltpu.CompilerParams(vmem_limit_bytes=8 * MIB),
        name="combine",
    )(*args)


def finish_body(meta, tab, slots_in, slots_x, full_in, full_x, got2, got31, got32, got33, fwd, bwd, two, three):
    s = meta[0]
    two[...] = got2[...].astype(F32)
    three[0] = got31[...].astype(F32)
    three[1] = got32[...].astype(F32)
    three[2] = got33[...].astype(F32)
    fwd[...] = jnp.zeros(fwd.shape, F32)
    bwd[...] = jnp.zeros(bwd.shape, F32)

    def ahead(source, size, n, i, d):
        fwd[i, BODY, pl.ds(d - 1, 1), :] = source[pl.ds(size * BODY + n, 1), :]
        for m in range(BODY):
            fwd[i, m, pl.ds(d - 1, 1), :] = source[pl.ds(n * BODY + m, 1), :]

    def behind(source, size, n, j, d):
        bwd[j, 0, pl.ds(d - 1, 1), :] = source[pl.ds(size * BODY + n, 1), :]
        for m in range(BODY):
            bwd[j, BODY - m, pl.ds(d - 1, 1), :] = source[pl.ds(n * BODY + m, 1), :]

    from_above = jnp.int32(0)
    for i in range(2):
        for d in range(1, REACH + 1):
            row = 2 * s + i
            p = HALF + row
            entry = p * REACH + d - 1
            on = is_live(tab, s, p, d)
            crossed = row + d >= GROUP

            @pl.when(on & jnp.logical_not(crossed))
            def _(i=i, d=d, entry=entry):
                ahead(full_in, SLOTS, slots_in[entry], i, d)

            @pl.when(on & crossed & (s < 2))
            def _(i=i, d=d, entry=entry):
                ahead(full_x, SLOTS, slots_x[entry], i, d)

            @pl.when(on & crossed & (s >= 2))
            def _(i=i, d=d, n=from_above):
                ahead(two, SLOTS, n, i, d)

            from_above = from_above + jnp.where(on & crossed, 1, 0)

    for j in range(2):
        for d in range(1, REACH + 1):
            low = 2 * s + j - d
            p = HALF + low
            entry = p * REACH + d - 1
            on = is_live(tab, s, p, d)
            before = low < 0
            row = jnp.where(before, low + GROUP, low)
            owner = row // 2
            up = before & (owner < 2)
            mine = (owner == s) & jnp.logical_not(up)

            @pl.when(on & mine & jnp.logical_not(before))
            def _(j=j, d=d, entry=entry):
                behind(full_in, SLOTS, slots_in[entry], j, d)

            @pl.when(on & mine & before)
            def _(j=j, d=d, entry=entry):
                behind(full_x, SLOTS, slots_x[entry], j, d)

            @pl.when(on & up)
            def _(j=j, d=d, row=row):
                k0 = jnp.where(row == 0, 0, 2 * row - 1) + j
                k1 = jnp.where(row == 2, 0, 1) + j
                behind(two, SLOTS, jnp.where(s == 0, k0, k1), j, d)

            @pl.when(on & jnp.logical_not(mine) & jnp.logical_not(up))
            def _(j=j, d=d, row=row, owner=owner):
                r = jnp.bitwise_and(s - owner, 3)
                behind(three.at[r - 1], 4, (row - 2 * owner) * 2 + j, j, d)


def finish(blocks, *args):
    out = jax.ShapeDtypeStruct((blocks, LAGS, REACH, CHANS), F32)
    return pl.pallas_call(
        finish_body,
        in_specs=[SMEM] * 4 + [VMEM] * 6,
        out_specs=[VMEM, VMEM],
        out_shape=[out, out],
        scratch_shapes=[
            pltpu.VMEM((CHUNK, CHANS), F32),
            pltpu.VMEM((3, SEND, CHANS), F32),
        ],
        compiler_params=pltpu.CompilerParams(vmem_limit_bytes=8 * MIB),
        name="finish",
    )(*args)


def shards(groups, planes, consts, lag, records, pairs):
    b = lax.axis_index("blk").astype(jnp.int32)
    s = lax.axis_index("seg").astype(jnp.int32)
    core = jnp.bitwise_and(b, 1)
    meta = jnp.stack([s, core])

    def ring(x, r):
        return lax.ppermute(x, "seg", [(z, (z + r) % planes) for z in range(planes)])

    outer = [(g, (g + 1) % groups if g % 2 else (g - 1) % groups) for g in range(groups)]
    inner = [(g, g ^ 1) for g in range(groups)]
    upward = [(g, (g + 1) % groups) for g in range(groups)]
    own_ext = whiten(core[None], records, consts)
    got_ext = lax.ppermute(own_ext, "blk", outer)
    row, _ = lax.optimization_barrier((jnp.pad(pairs.reshape(-1), (0, CHANS - pairs.size)), own_ext))
    own_tab = jnp.concatenate([row, ring(row, 1), ring(row, 2), ring(row, 3)])
    tab = jnp.concatenate([lax.ppermute(own_tab, "blk", upward), own_tab])
    own_int = whiten((1 - core)[None], records, consts)
    got_int = lax.ppermute(own_int, "blk", inner)

    keep_in, in1, in2, in3, slots_in = correlate(
        False, meta, jnp.concatenate([own_tab, own_tab]), (own_ext, own_int), lag
    )
    in1, in2, in3 = ring(in1, 1), ring(in2, 2), ring(in3, 3)
    keep_x, x1, x2, x3, slots_x = correlate(True, meta, tab, (own_ext, own_int, got_ext, got_int), lag)
    x1, x2, x3 = ring(x1, 1), ring(x2, 2), ring(x3, 3)
    full_in, full_x, send2, s31, s32, s33 = combine(
        meta, tab, slots_in, slots_x, keep_in, in1, in2, in3, keep_x, x1, x2, x3
    )
    shift = [
        (z * groups + g, z * groups + (g + (1 if z < 2 else -1)) % groups)
        for z in range(planes)
        for g in range(groups)
    ]
    got2 = lax.ppermute(send2, ("seg", "blk"), shift)
    outs = finish(
        pairs.shape[0], meta, tab, slots_in, slots_x, full_in, full_x, got2, ring(s31, 1), ring(s32, 2), ring(s33, 3)
    )
    return tuple(jnp.transpose(out, (0, 2, 1, 3)) for out in outs)


def solution(mesh):
    groups = mesh.shape["blk"]
    planes = mesh.shape["seg"]
    consts = tables()

    def run(records, pairs):
        body = functools.partial(
            shards,
            groups,
            planes,
            tuple(jnp.asarray(c) for c in consts),
            jnp.asarray(lag_rows(records.shape[0])),
        )
        return jax.shard_map(
            body,
            mesh=mesh,
            in_specs=(P("seg", "blk", None), P(("blk", "seg"), None)),
            out_specs=(P(("blk", "seg"), None, None, None), P(("blk", "seg"), None, None, None)),
            check_vma=False,
        )(records, pairs)

    return run
```

```python
import functools

import jax
import jax.numpy as jnp
import ml_dtypes
import numpy as np
from jax import lax
from jax.experimental import pallas as pl
from jax.experimental.pallas import tpu as pltpu
from jax.sharding import PartitionSpec as P

BINS = 256
LENGTH = 512
CHANS = 128
MAXLAG = 32
LAGS = 2 * MAXLAG + 1
REACH = 8
SMOOTH = 32
BAND = 64
GROUP = 8
HALF = GROUP // 2
BATCH = 2
SUB = BATCH * CHANS
REACHED = 384
SLOTS = 13
BODY = 64
CHUNK = SLOTS * BODY + 16
SHIFTED = 8
SEND2 = SHIFTED * BODY + 16
SEND3 = 4 * BODY + 16
MIB = 1024 * 1024
TINY = pl.CostEstimate(flops=1, bytes_accessed=1, transcendentals=0)
BF = jnp.bfloat16
F32 = jnp.float32


def split(array):
    high = array.astype(ml_dtypes.bfloat16)
    low = (array - high.astype(np.float32)).astype(ml_dtypes.bfloat16)
    return high, low


def tables():
    times = np.arange(LENGTH)
    inside = (np.abs(times[:, None] - times[None, :]) <= SMOOTH).astype(np.float32)
    share = (1.0 / inside.sum(0, keepdims=True)).astype(np.float32)
    first, second = inside[:REACHED, :BINS], inside[LENGTH - REACHED :, BINS:]
    first = np.concatenate([first, first], axis=0).astype(ml_dtypes.bfloat16)
    second = np.concatenate([second, second], axis=0).astype(ml_dtypes.bfloat16)
    phase = (times[:, None] * np.arange(BINS)[None, :] % LENGTH) * (2.0 * np.pi / LENGTH)
    fourier = np.concatenate([np.cos(phase), -np.sin(phase)], axis=1).astype(np.float32)
    fhi, flo = split(fourier)
    fourier = np.concatenate([fhi, fhi, flo], axis=0)
    which = np.arange(BINS) // BAND
    same = ((which[:, None] == which[None, :]) / (2.0 * BAND)).astype(ml_dtypes.bfloat16)
    return first, second, share, fourier, same


def lag_rows(segments):
    shifts = np.arange(-MAXLAG, MAXLAG + 1)
    phase = (shifts[:, None] * np.arange(BINS)[None, :] % LENGTH) * (2.0 * np.pi / LENGTH)
    table = np.concatenate([np.cos(phase), -np.sin(phase)], axis=1) / np.sqrt(segments * BINS)
    table = np.concatenate([table, np.zeros((CHANS - LAGS, LENGTH))], axis=0).T.astype(np.float32)
    return np.concatenate(split(table), axis=1)


def dot(a, b):
    return jnp.dot(a, b, preferred_element_type=F32)


def halves(x):
    high = x.astype(BF)
    return high, (x - high.astype(F32)).astype(BF)


def inverse(y):
    r = pl.reciprocal(y, approx=True)
    return r * (2.0 - y * r)


def whiten_body(start, records, first, second, share, fourier, same, *whites):
    del start
    parts = range(records.shape[1] // SUB)
    xs = [records[0, pl.ds(k * SUB, SUB), :] for k in parts]
    levels = []
    for x in xs:
        ahi, alo = halves(jnp.abs(x))
        left = dot(jnp.concatenate([ahi[:, :REACHED], alo[:, :REACHED]], axis=1), first[...])
        right = dot(jnp.concatenate([ahi[:, LENGTH - REACHED :], alo[:, LENGTH - REACHED :]], axis=1), second[...])
        levels.append(jnp.concatenate([left, right], axis=1) * share[...])
    spectra = []
    for x, level in zip(xs, levels):
        nhi, nlo = halves(x * inverse(level + 1e-06))
        spectra.append(dot(jnp.concatenate([nhi, nlo, nhi], axis=1), fourier[...]))
    for k in parts:
        re = spectra[k][:, :BINS]
        im = spectra[k][:, BINS:]
        power = dot((re * re + im * im).astype(BF), same[...])
        factor = lax.rsqrt(power + 1e-05)
        whites[k][:, 0, :, :BINS] = (re * factor).astype(BF).reshape(BATCH, CHANS, BINS)
        whites[k][:, 0, :, BINS:] = (im * factor).astype(BF).reshape(BATCH, CHANS, BINS)


def whiten(first_block, blocks, records, consts):
    segs = records.shape[0]
    rows = blocks * CHANS
    return pl.pallas_call(
        whiten_body,
        grid_spec=pltpu.PrefetchScalarGridSpec(
            num_scalar_prefetch=1,
            grid=(segs,),
            in_specs=[pl.BlockSpec((1, rows, LENGTH), lambda s, at: (s, at[0] // blocks, 0))]
            + [pl.BlockSpec(memory_space=pltpu.VMEM)] * len(consts),
            out_specs=[pl.BlockSpec((BATCH, 1, CHANS, LENGTH), lambda s, at: (0, s, 0, 0))] * (blocks // BATCH),
        ),
        out_shape=[jax.ShapeDtypeStruct((BATCH, segs, CHANS, LENGTH), BF)] * (blocks // BATCH),
        compiler_params=pltpu.CompilerParams(vmem_limit_bytes=56 * MIB),
        cost_estimate=TINY,
        name="whiten",
    )(first_block[None], records, *consts)


CODES, OWN, BEFORE = 64, CHANS, 5 * CHANS


def is_live(info, s, p, d):
    row = jnp.where(p < HALF, p + HALF, p - HALF)
    base = jnp.where(p < HALF, BEFORE, OWN)
    return info[base + jnp.bitwise_and(s - row // 2, 3) * CHANS + (row % 2) * REACH + d - 1] != 0


VISITS = [(p, d) for p in range(HALF) for d in range(1, REACH + 1) if p + d >= HALF] + [
    (p, d) for p in range(HALF, 12) for d in range(1, REACH + 1) if p < GROUP or p + d < 12
]


def correlate_body(info, *refs):
    s = info[0]
    core = info[1]
    ext = HALF * (1 + core)
    inner = HALF * (2 - core)
    got_ext = 3 * HALF * core
    got_inner = 3 * HALF * (1 - core)
    sources = [at + k for at in (ext, inner, got_ext, got_inner) for k in (0, BATCH)]
    whites = refs[: len(sources)]
    lag, keep, out1, out2, out3, slots, low, high, stk, pq, cnt = refs[len(sources) :]
    segs = low.shape[0]
    for k in range(4):
        cnt[k] = 0
    cnt[4] = -1

    def grab(dest, block):
        for ref, begin in zip(whites, sources):

            @pl.when((block >= begin) & (block < begin + BATCH))
            def _(ref=ref, begin=begin):
                dest[...] = ref[block - begin]

    def put(owner, entry, stack):
        n = cnt[owner]
        cnt[owner] = n + 1
        slots[entry] = n
        r = jnp.bitwise_and(owner - s, 3)
        stk[r, pl.ds(pl.multiple_of(n * BODY, BODY), BODY), :] = stack[:BODY]
        stk[r, pl.ds(SLOTS * BODY + n, 1), :] = stack[BODY:LAGS]

    def pair(p, d):
        q = p + d

        @pl.when(cnt[4] != p)
        def _():
            grab(low, p)
            cnt[4] = p

        grab(high, q)
        for chunk in range(CHANS // 16):
            rows = pl.ds(chunk * 16, 16)
            real = jnp.zeros((16, BINS), F32)
            imag = jnp.zeros((16, BINS), F32)
            for k in range(segs):
                are = low[k, rows, :BINS].astype(F32)
                aim = low[k, rows, BINS:].astype(F32)
                bre = high[k, rows, :BINS].astype(F32)
                bim = high[k, rows, BINS:].astype(F32)
                real += are * bre + aim * bim
                imag += are * bim - aim * bre
            rhi, rlo = halves(real)
            ihi, ilo = halves(imag)
            pq[0, rows, :BINS] = rhi
            pq[0, rows, BINS:] = ihi
            pq[1, rows, :BINS] = rlo
            pq[1, rows, BINS:] = ilo
        both = dot(pq[0], lag[...])
        stack = (both[:, :CHANS] + both[:, CHANS:] + dot(pq[1], lag[:, :CHANS])).T
        put(jnp.where(p < HALF, 2 + p // 2, (p - HALF) // 2), p * REACH + d - 1, stack)

        @pl.when((p >= 6) & (p < 8) & (q >= 12) & (q < 14))
        def _():
            put(0, 96 + (p - 6) * 2 + q - 12, stack)

    def visit(n, carry):
        code = info[CODES + n]
        p = jnp.right_shift(code, 4)
        d = jnp.bitwise_and(code, 15)

        @pl.when(is_live(info, s, p, d))
        def _():
            pair(p, d)

        return carry

    lax.fori_loop(0, len(VISITS), visit, 0)
    keep[...] = stk[0]
    out1[...] = stk[1].astype(BF)
    out2[...] = stk[2].astype(BF)
    out3[...] = stk[3].astype(BF)


SMEM = pl.BlockSpec(memory_space=pltpu.SMEM)
VMEM = pl.BlockSpec(memory_space=pltpu.VMEM)


def correlate(info, whites, lag):
    segs = whites[0].shape[1]
    chunk = jax.ShapeDtypeStruct((CHUNK, CHANS), BF)
    return pl.pallas_call(
        correlate_body,
        in_specs=[SMEM] + [VMEM] * (len(whites) + 1),
        out_specs=[VMEM, VMEM, VMEM, VMEM, SMEM],
        out_shape=[
            jax.ShapeDtypeStruct((CHUNK, CHANS), F32),
            chunk,
            chunk,
            chunk,
            jax.ShapeDtypeStruct((128,), jnp.int32),
        ],
        scratch_shapes=[
            pltpu.VMEM((segs, CHANS, LENGTH), BF),
            pltpu.VMEM((segs, CHANS, LENGTH), BF),
            pltpu.VMEM((4, CHUNK, CHANS), F32),
            pltpu.VMEM((2, CHANS, LENGTH), BF),
            pltpu.SMEM((8,), jnp.int32),
        ],
        compiler_params=pltpu.CompilerParams(vmem_limit_bytes=20 * MIB),
        cost_estimate=TINY,
        name="correlate",
    )(info, *whites, lag)


UPWARD = (
    ((0, 0), (1, 0), (1, 1), (2, 0), (2, 1), (3, 0), (3, 1)),
    ((2, 2), (3, 2), (3, 3)),
)


def combine_body(info, slots, keep, got1, got2, got3, full, send2, out1, out2, out3, stage2, stage3):
    s = info[0]
    full[...] = (keep[...] + got1[...].astype(F32)) + (got2[...].astype(F32) + got3[...].astype(F32))

    def move(n, dest, size, k):
        dest[pl.ds(k * BODY, BODY), :] = full[pl.ds(pl.multiple_of(n * BODY, BODY), BODY), :]
        dest[pl.ds(size * BODY + k, 1), :] = full[pl.ds(SLOTS * BODY + n, 1), :]

    @pl.when(s >= 2)
    def _():
        send2[: SHIFTED * BODY, :] = full[: SHIFTED * BODY, :].astype(BF)
        send2[SHIFTED * BODY :, :] = full[SLOTS * BODY :, :].astype(BF)

    for owner in (0, 1):

        @pl.when(s == owner)
        def _(owner=owner):
            for k, (i, j) in enumerate(UPWARD[owner]):
                p, d = HALF + i, GROUP + j - i
                entry = p * REACH + d - 1 if i // 2 == owner else 96 + (i - 2) * 2 + j

                @pl.when(is_live(info, s, jnp.int32(p), d))
                def _(entry=entry, k=k):
                    move(slots[entry], stage2, SHIFTED, k)

            send2[...] = stage2[...].astype(BF)

    for r, out in ((1, out1), (2, out2), (3, out3)):
        to = jnp.bitwise_and(s + r, 3)
        for i in range(2):
            for j in range(2):
                row = 2 * s + i
                d = 2 * to + j - row

                @pl.when((s < to) & is_live(info, s, HALF + row, d))
                def _(r=r, k=2 * i + j, row=row, d=d):
                    move(slots[(HALF + row) * REACH + d - 1], stage3.at[r - 1], 4, k)

                @pl.when((s > to) & (s >= 2) & is_live(info, s, row - HALF, d + GROUP))
                def _(r=r, k=2 * i + j, row=row, d=d):
                    move(slots[(row - HALF) * REACH + d + GROUP - 1], stage3.at[r - 1], 4, k)

        out[...] = stage3[r - 1].astype(BF)


def combine(*args):
    third = jax.ShapeDtypeStruct((SEND3, CHANS), BF)
    full = jax.ShapeDtypeStruct((CHUNK, CHANS), F32)
    return pl.pallas_call(
        combine_body,
        in_specs=[SMEM] * 2 + [VMEM] * 4,
        out_specs=[VMEM] * 5,
        out_shape=[full, jax.ShapeDtypeStruct((SEND2, CHANS), BF), third, third, third],
        scratch_shapes=[
            pltpu.VMEM((SEND2, CHANS), F32),
            pltpu.VMEM((3, SEND3, CHANS), F32),
        ],
        compiler_params=pltpu.CompilerParams(vmem_limit_bytes=8 * MIB),
        cost_estimate=TINY,
        name="combine",
    )(*args)


def finish_body(info, slots, full, got2, got31, got32, got33, fwd, bwd, two, three):
    s = info[0]
    two[...] = got2[...].astype(F32)
    three[0] = got31[...].astype(F32)
    three[1] = got32[...].astype(F32)
    three[2] = got33[...].astype(F32)
    fwd[...] = jnp.zeros(fwd.shape, F32)
    bwd[...] = jnp.zeros(bwd.shape, F32)

    def ahead(source, size, n, i, d):
        fwd[i, BODY, pl.ds(d - 1, 1), :] = source[pl.ds(size * BODY + n, 1), :]
        for m in range(BODY):
            fwd[i, m, pl.ds(d - 1, 1), :] = source[pl.ds(n * BODY + m, 1), :]

    def behind(source, size, n, j, d):
        bwd[j, 0, pl.ds(d - 1, 1), :] = source[pl.ds(size * BODY + n, 1), :]
        for m in range(BODY):
            bwd[j, BODY - m, pl.ds(d - 1, 1), :] = source[pl.ds(n * BODY + m, 1), :]

    from_above = jnp.int32(0)
    for i in range(2):
        for d in range(1, REACH + 1):
            row = 2 * s + i
            p = HALF + row
            entry = p * REACH + d - 1
            on = is_live(info, s, p, d)
            crossed = row + d >= GROUP

            @pl.when(on)
            def _(i=i, d=d, entry=entry, crossed=crossed, n=from_above):
                @pl.when(jnp.logical_not(crossed) | (s < 2))
                def _():
                    ahead(full, SLOTS, slots[entry], i, d)

                @pl.when(crossed & (s >= 2))
                def _():
                    ahead(two, SHIFTED, n, i, d)

            from_above = from_above + jnp.where(on & crossed, 1, 0)

    for j in range(2):
        for d in range(1, REACH + 1):
            low = 2 * s + j - d
            p = HALF + low

            @pl.when(is_live(info, s, p, d))
            def _(j=j, d=d, low=low, p=p):
                entry = p * REACH + d - 1
                before = low < 0
                row = jnp.where(before, low + GROUP, low)
                owner = row // 2
                up = before & (owner < 2)
                mine = (owner == s) & jnp.logical_not(up)

                @pl.when(mine)
                def _():
                    behind(full, SLOTS, slots[entry], j, d)

                @pl.when(up)
                def _():
                    k0 = jnp.where(row == 0, 0, 2 * row - 1) + j
                    k1 = jnp.where(row == 2, 0, 1) + j
                    behind(two, SHIFTED, jnp.where(s == 0, k0, k1), j, d)

                @pl.when(jnp.logical_not(mine) & jnp.logical_not(up))
                def _():
                    r = jnp.bitwise_and(s - owner, 3)
                    behind(three.at[r - 1], 4, (row - 2 * owner) * 2 + j, j, d)


def finish(blocks, *args):
    out = jax.ShapeDtypeStruct((blocks, LAGS, REACH, CHANS), F32)
    return pl.pallas_call(
        finish_body,
        in_specs=[SMEM] * 2 + [VMEM] * 5,
        out_specs=[VMEM, VMEM],
        out_shape=[out, out],
        scratch_shapes=[
            pltpu.VMEM((SEND2, CHANS), F32),
            pltpu.VMEM((3, SEND3, CHANS), F32),
        ],
        compiler_params=pltpu.CompilerParams(vmem_limit_bytes=8 * MIB),
        cost_estimate=TINY,
        name="finish",
    )(*args)


def shards(groups, planes, consts, lag, records, pairs):
    b = lax.axis_index("blk").astype(jnp.int32)
    s = lax.axis_index("seg").astype(jnp.int32)
    core = jnp.bitwise_and(b, 1)
    codes = np.array([p * 16 + d for p, d in VISITS], np.int32)
    place = jnp.concatenate([jnp.stack([s, core]), jnp.zeros((CODES - 2,), jnp.int32), jnp.asarray(codes)])

    def ring(x, r):
        return lax.ppermute(x, "seg", [(z, (z + r) % planes) for z in range(planes)])

    outer = [(g, g + 1 if g % 2 else g - 1) for g in range(1, groups - 1)]
    inner = [(g, g ^ 1) for g in range(groups)]
    upward = [(g, g + 1) for g in range(groups - 1)]
    shift = [
        (z * groups + g, z * groups + g + step)
        for z in range(planes)
        for g in range(groups)
        for step in (1 if z < 2 else -1,)
        if 0 <= g + step < groups
    ]

    (ext1,) = whiten(core * HALF, BATCH, records, consts)
    got1 = lax.ppermute(ext1, "blk", outer)
    (ext2,) = whiten(core * HALF + BATCH, BATCH, records, consts)
    got2 = lax.ppermute(ext2, "blk", outer)
    row, _ = lax.optimization_barrier((jnp.pad(pairs.reshape(-1), (0, CHANS - pairs.size)), ext2))
    own = jnp.concatenate([place, row, ring(row, 1), ring(row, 2), ring(row, 3)])
    start, own, _ = lax.optimization_barrier(((1 - core) * HALF, own, ext2))
    in1, in2 = whiten(start, HALF, records, consts)
    info = jnp.concatenate([own, lax.ppermute(own[OWN:], "blk", upward)])
    got3, got4 = lax.ppermute(in1, "blk", inner), lax.ppermute(in2, "blk", inner)

    whites = (ext1, ext2, in1, in2, got1, got2, got3, got4)
    keep, out1, out2, out3, slots = correlate(info, whites, lag)
    full, send2, s31, s32, s33 = combine(info, slots, keep, ring(out1, 1), ring(out2, 2), ring(out3, 3))
    shifted = lax.ppermute(send2, ("seg", "blk"), shift)
    outs = finish(pairs.shape[0], info, slots, full, shifted, ring(s31, 1), ring(s32, 2), ring(s33, 3))
    return tuple(jnp.transpose(out, (0, 2, 1, 3)) for out in outs)


def solution(mesh):
    groups = mesh.shape["blk"]
    planes = mesh.shape["seg"]
    consts = tables()

    def run(records, pairs):
        body = functools.partial(
            shards,
            groups,
            planes,
            tuple(jnp.asarray(c) for c in consts),
            jnp.asarray(lag_rows(records.shape[0])),
        )
        return jax.shard_map(
            body,
            mesh=mesh,
            in_specs=(P("seg", "blk", None), P(("blk", "seg"), None)),
            out_specs=(P(("blk", "seg"), None, None, None), P(("blk", "seg"), None, None, None)),
            check_vma=False,
        )(records, pairs)

    return run
```

```python
import functools

import jax
import jax.numpy as jnp
import ml_dtypes
import numpy as np
from jax import lax
from jax.experimental import pallas as pl
from jax.experimental.pallas import tpu as pltpu
from jax.sharding import PartitionSpec as P

BINS = 256
LENGTH = 512
CHANS = 128
MAXLAG = 32
LAGS = 2 * MAXLAG + 1
REACH = 8
SMOOTH = 32
BAND = 64
GROUP = 8
HALF = GROUP // 2
PLANES = 4
ROWS = HALF * CHANS
SUB = 256
REACHED = 384
SLOTS = 13
SHIFTED = 8
BODY = 64
CHUNK = SLOTS * BODY + 16
SEND2 = SHIFTED * BODY + 16
SEND3 = 4 * BODY + 16
SEG, PAIRS, MOVES, WRITES, PLAN = 4, 16, 80, 112, 256
TWO = CHUNK
THREE = CHUNK + SEND2
POOL = THREE + 3 * SEND3
MIB = 1024 * 1024
TINY = pl.CostEstimate(flops=1, bytes_accessed=1, transcendentals=0)
BF = jnp.bfloat16
F32 = jnp.float32
SMEM = pl.BlockSpec(memory_space=pltpu.SMEM)
VMEM = pl.BlockSpec(memory_space=pltpu.VMEM)


def split(array):
    high = array.astype(ml_dtypes.bfloat16)
    low = (array - high.astype(np.float32)).astype(ml_dtypes.bfloat16)
    return high, low


def lag_rows(segments):
    shifts = np.arange(-MAXLAG, MAXLAG + 1)
    phase = (shifts[:, None] * np.arange(BINS)[None, :] % LENGTH) * (2.0 * np.pi / LENGTH)
    table = np.concatenate([np.cos(phase), -np.sin(phase)], axis=1) / np.sqrt(segments * BINS)
    table = np.concatenate([table, np.zeros((CHANS - LAGS, LENGTH))], axis=0).T.astype(np.float32)
    return np.concatenate(split(table), axis=1)


def dot(a, b):
    return jnp.dot(a, b, preferred_element_type=F32)


def halves(x):
    high = x.astype(BF)
    return high, (x - high.astype(F32)).astype(BF)


def inverse(y):
    r = pl.reciprocal(y, approx=True)
    return r * (2.0 - y * r)


def make_tables(tab):
    at = lax.broadcasted_iota(jnp.int32, (REACHED, LENGTH), 0)
    col = lax.broadcasted_iota(jnp.int32, (REACHED, LENGTH), 1)
    apart = at - col + jnp.where(col < BINS, 0, LENGTH - REACHED)
    tab[:REACHED] = jnp.where(jnp.abs(apart) <= SMOOTH, 1.0, 0.0).astype(BF)
    row = lax.broadcasted_iota(jnp.int32, (CHANS, LENGTH), 0)
    col = lax.broadcasted_iota(jnp.int32, (CHANS, LENGTH), 1)
    row = row + jnp.where(col < BINS, 0, CHANS)
    col = jnp.bitwise_and(col, BINS - 1)
    tab[REACHED:LENGTH] = jnp.where(row // BAND == col // BAND, 0.5 / BAND, 0.0).astype(BF)

    def cosine(step, shift, rows):
        k = lax.broadcasted_iota(jnp.int32, (rows, BINS), 0) * lax.broadcasted_iota(jnp.int32, (rows, BINS), 1)
        k = jnp.bitwise_and(k * step - shift + BINS, LENGTH - 1) - BINS
        square = jnp.square(k.astype(F32) * (2.0 * np.pi / LENGTH))
        value = jnp.ones_like(square)
        for n in range(20, 0, -2):
            value = 1.0 - value * square * (1.0 / (n * (n - 1)))
        return value

    quarter = LENGTH // 4
    fine_cos, fine_sin = cosine(1, 0, 16), cosine(1, quarter, 16)
    coarse_cos, coarse_sin = cosine(16, 0, 32), cosine(16, quarter, 32)
    for a in range(LENGTH // 16):
        c, s = coarse_cos[a : a + 1], coarse_sin[a : a + 1]
        for k, part in enumerate((c * fine_cos - s * fine_sin, -(s * fine_cos) - c * fine_sin)):
            high, low = halves(part)
            tab[LENGTH + 16 * a : LENGTH + 16 * a + 16, k * BINS : (k + 1) * BINS] = high
            tab[2 * LENGTH + 16 * a : 2 * LENGTH + 16 * a + 16, k * BINS : (k + 1) * BINS] = low


def whiten_body(outer, records, white, buf, tab, sems):
    segs = records.shape[0]
    core = jnp.bitwise_and(lax.axis_index("blk"), 1)
    begin = pl.multiple_of((core if outer else 1 - core) * ROWS, ROWS)

    def load(k):
        return pltpu.make_async_copy(records.at[k, pl.ds(begin, ROWS)], buf.at[k], sems.at[k])

    for k in range(segs):
        load(k).start()
    at = lax.broadcasted_iota(jnp.int32, (1, LENGTH), 1)
    count = jnp.minimum(at, SMOOTH) + jnp.minimum(LENGTH - 1 - at, SMOOTH) + 1
    share = 1.0 / count.astype(F32)
    make_tables(tab)

    def step(k, carry):
        load(k).wait()
        parts = range(ROWS // SUB)
        xs = [buf[k, pl.ds(n * SUB, SUB), :] for n in parts]
        levels = []
        first = tab[:REACHED, :BINS]
        second = tab[:REACHED, BINS:]
        for x in xs:
            ahi, alo = halves(jnp.abs(x))
            left = jnp.concatenate([ahi[:, :REACHED], alo[:, :REACHED]], axis=1)
            right = jnp.concatenate([ahi[:, LENGTH - REACHED :], alo[:, LENGTH - REACHED :]], axis=1)
            left = dot(left, jnp.concatenate([first, first], axis=0))
            right = dot(right, jnp.concatenate([second, second], axis=0))
            levels.append(jnp.concatenate([left, right], axis=1) * share)
        spectra = []
        fhi = tab[LENGTH : 2 * LENGTH]
        fourier = jnp.concatenate([fhi, fhi, tab[2 * LENGTH :]], axis=0)
        for x, level in zip(xs, levels):
            nhi, nlo = halves(x * inverse(level + 1e-06))
            spectra.append(dot(jnp.concatenate([nhi, nlo, nhi], axis=1), fourier))
        same = jnp.concatenate([tab[REACHED:LENGTH, :BINS], tab[REACHED:LENGTH, BINS:]], axis=0)
        for n in parts:
            re = spectra[n][:, :BINS]
            im = spectra[n][:, BINS:]
            power = dot((re * re + im * im).astype(BF), same)
            factor = lax.rsqrt(power + 1e-05)
            per = SUB // CHANS
            white[pl.ds(n * per, per), k, :, :BINS] = (re * factor).astype(BF).reshape(per, CHANS, BINS)
            white[pl.ds(n * per, per), k, :, BINS:] = (im * factor).astype(BF).reshape(per, CHANS, BINS)
        return carry

    lax.fori_loop(0, segs, step, 0)


def whiten(outer, records):
    segs = records.shape[0]
    return pl.pallas_call(
        functools.partial(whiten_body, outer),
        in_specs=[pl.BlockSpec(memory_space=pltpu.HBM)],
        out_specs=VMEM,
        out_shape=jax.ShapeDtypeStruct((HALF, segs, CHANS, LENGTH), BF),
        scratch_shapes=[
            pltpu.VMEM((segs, ROWS, LENGTH), F32),
            pltpu.VMEM((3 * LENGTH, LENGTH), BF),
            pltpu.SemaphoreType.DMA((segs,)),
        ],
        compiler_params=pltpu.CompilerParams(vmem_limit_bytes=50 * MIB),
        cost_estimate=TINY,
        name="whiten",
    )(records)


VISITS = [(p, d) for p in range(HALF) for d in range(1, REACH + 1) if p + d >= HALF] + [
    (p, d) for p in range(HALF, 12) for d in range(1, REACH + 1) if p < GROUP or p + d < 12
]
UPWARD = (
    ((0, 0), (1, 0), (1, 1), (2, 0), (2, 1), (3, 0), (3, 1)),
    ((2, 2), (3, 2), (3, 3)),
)


def plan_body(own, before, plan, slots):
    s = lax.axis_index("seg").astype(jnp.int32)
    plan[SEG] = s
    zero = jnp.int32(0)

    def behind(owner):
        return 2 * jnp.bitwise_and(s - owner, 3)

    used = [zero] * PLANES
    n = zero
    for p, d in VISITS:
        row = p + HALF if p < HALF else p - HALF
        owner = row // 2
        live = (before if p < HALF else own)[behind(owner) + row % 2, d - 1]
        code = p + d * 16 + jnp.bitwise_and(owner - s, 3) * 256 + used[owner] * 4096
        slots[p * REACH + d - 1] = used[owner]
        used[owner] = used[owner] + live
        if p in (6, 7) and p + d in (12, 13):
            slots[96 + (p - 6) * 2 + p + d - 12] = used[0]
            code = code + (used[0] + 1) * 65536
            used[0] = used[0] + live
        plan[PAIRS + n] = code
        n = n + live
    plan[0] = n

    n = zero
    for owner in (0, 1):
        for k, (i, j) in enumerate(UPWARD[owner]):
            p, d = HALF + i, GROUP + j - i
            entry = p * REACH + d - 1 if i // 2 == owner else 96 + (i - 2) * 2 + j
            plan[MOVES + n] = slots[entry] + k * 4096
            n = n + jnp.where(s == owner, own[behind(i // 2) + i % 2, d - 1], 0)
    for r in range(1, PLANES):
        to = jnp.bitwise_and(s + r, 3)
        ahead = s < to
        for i in range(2):
            for j in range(2):
                row = 2 * s + i
                p = jnp.where(ahead, row + HALF, jnp.maximum(row - HALF, 0))
                d = 2 * to + j - row + jnp.where(ahead, 0, GROUP)
                live = jnp.where(ahead, own[i, d - 1], jnp.where(s >= 2, before[i, d - 1], 0))
                plan[MOVES + n] = slots[p * REACH + d - 1] + r * 256 + (2 * i + j) * 4096
                n = n + live
    plan[1] = n

    def write(n, i, d, base, size, slot):
        plan[WRITES + n] = base + slot * BODY + (base + size * BODY + slot) * 4096 + (i * 8 + d - 1) * 16777216

    n = zero
    above = zero
    for i in range(2):
        for d in range(1, REACH + 1):
            row = 2 * s + i
            live = own[i, d - 1]
            shift = (row + d >= GROUP) & (s >= 2)
            slot = jnp.where(shift, above, slots[(HALF + row) * REACH + d - 1])
            write(n, i, d, jnp.where(shift, TWO, 0), jnp.where(shift, SHIFTED, SLOTS), slot)
            n = n + live
            above = above + jnp.where(shift, live, 0)
    plan[2] = n
    for j in range(2):
        for d in range(1, REACH + 1):
            low = 2 * s + j - d
            crossing = low < 0
            row = jnp.where(crossing, low + GROUP, low)
            owner = jnp.right_shift(row, 1)
            at = behind(owner) + jnp.bitwise_and(row, 1)
            live = jnp.where(crossing, before[at, d - 1], own[at, d - 1])
            up = crossing & (owner < 2)
            mine = (owner == s) & jnp.logical_not(up)
            k0 = jnp.where(row == 0, 0, 2 * row - 1) + j
            k1 = jnp.where(row == 2, 0, 1) + j
            entry = jnp.maximum((HALF + low) * REACH + d - 1, 0)
            slot = jnp.where(mine, slots[entry], 2 * (row - 2 * owner) + j)
            slot = jnp.where(up, jnp.where(s == 0, k0, k1), slot)
            base = jnp.where(mine, 0, THREE + (jnp.bitwise_and(s - owner, 3) - 1) * SEND3)
            base = jnp.where(up, TWO, base)
            size = jnp.where(mine, SLOTS, jnp.where(up, SHIFTED, 4))
            write(n, j, d, base, size, slot)
            n = n + live
    plan[3] = n


def make_plan(own, before):
    return pl.pallas_call(
        plan_body,
        in_specs=[SMEM, SMEM],
        out_specs=SMEM,
        out_shape=jax.ShapeDtypeStruct((PLAN,), jnp.int32),
        scratch_shapes=[pltpu.SMEM((128,), jnp.int32)],
        cost_estimate=TINY,
        name="plan",
    )(own, before)


def correlate_body(plan, own_ext, own_int, got_ext, got_int, lag, keep, out1, out2, out3, low, high, stk, pq, last):
    core = jnp.bitwise_and(lax.axis_index("blk"), 1)
    sources = (
        (own_ext, HALF * (1 + core)),
        (own_int, HALF * (2 - core)),
        (got_ext, 3 * HALF * core),
        (got_int, 3 * HALF * (1 - core)),
    )
    segs = low.shape[0]
    last[0] = -1

    def grab(dest, block):
        for ref, begin in sources:

            @pl.when((block >= begin) & (block < begin + HALF))
            def _(ref=ref, begin=begin):
                dest[...] = ref[block - begin]

    def put(r, n, stack):
        stk[r, pl.ds(pl.multiple_of(n * BODY, BODY), BODY), :] = stack[:BODY]
        stk[r, pl.ds(SLOTS * BODY + n, 1), :] = stack[BODY:LAGS]

    def pair(n, carry):
        code = plan[PAIRS + n]
        p = jnp.bitwise_and(code, 15)
        d = jnp.bitwise_and(jnp.right_shift(code, 4), 15)

        @pl.when(last[0] != p)
        def _():
            grab(low, p)
            last[0] = p

        grab(high, p + d)
        for chunk in range(CHANS // 16):
            rows = pl.ds(chunk * 16, 16)
            real = jnp.zeros((16, BINS), F32)
            imag = jnp.zeros((16, BINS), F32)
            for k in range(segs):
                are = low[k, rows, :BINS].astype(F32)
                aim = low[k, rows, BINS:].astype(F32)
                bre = high[k, rows, :BINS].astype(F32)
                bim = high[k, rows, BINS:].astype(F32)
                real += are * bre + aim * bim
                imag += are * bim - aim * bre
            rhi, rlo = halves(real)
            ihi, ilo = halves(imag)
            pq[0, rows, :BINS] = rhi
            pq[0, rows, BINS:] = ihi
            pq[1, rows, :BINS] = rlo
            pq[1, rows, BINS:] = ilo
        both = dot(pq[0], lag[...])
        stack = (both[:, :CHANS] + both[:, CHANS:] + dot(pq[1], lag[:, :CHANS])).T
        put(jnp.bitwise_and(jnp.right_shift(code, 8), 3), jnp.bitwise_and(jnp.right_shift(code, 12), 15), stack)
        second = jnp.right_shift(code, 16)

        @pl.when(second > 0)
        def _():
            put(jnp.bitwise_and(-plan[SEG], 3), second - 1, stack)

        return carry

    lax.fori_loop(0, plan[0], pair, 0)
    keep[...] = stk[0]
    out1[...] = stk[1].astype(BF)
    out2[...] = stk[2].astype(BF)
    out3[...] = stk[3].astype(BF)


def correlate(plan, whites, lag):
    segs = whites[0].shape[1]
    chunk = jax.ShapeDtypeStruct((CHUNK, CHANS), BF)
    return pl.pallas_call(
        correlate_body,
        in_specs=[SMEM] + [VMEM] * 5,
        out_specs=[VMEM] * 4,
        out_shape=[jax.ShapeDtypeStruct((CHUNK, CHANS), F32), chunk, chunk, chunk],
        scratch_shapes=[
            pltpu.VMEM((segs, CHANS, LENGTH), BF),
            pltpu.VMEM((segs, CHANS, LENGTH), BF),
            pltpu.VMEM((PLANES, CHUNK, CHANS), F32),
            pltpu.VMEM((2, CHANS, LENGTH), BF),
            pltpu.SMEM((1,), jnp.int32),
        ],
        compiler_params=pltpu.CompilerParams(vmem_limit_bytes=16 * MIB),
        cost_estimate=TINY,
        name="correlate",
    )(plan, *whites, lag)


def combine_body(plan, keep, got2, got1, got3, full, send, out1, out2, out3, stage):
    full[...] = (keep[...] + got1[...].astype(F32)) + (got2[...].astype(F32) + got3[...].astype(F32))

    def move(n, carry):
        code = plan[MOVES + n]
        slot = jnp.bitwise_and(code, 255)
        message = jnp.bitwise_and(jnp.right_shift(code, 8), 15)
        k = jnp.right_shift(code, 12)
        size = jnp.where(message == 0, SHIFTED, 4)
        body = pl.ds(pl.multiple_of(slot * BODY, BODY), BODY)
        stage[message, pl.ds(pl.multiple_of(k * BODY, BODY), BODY), :] = full[body, :]
        stage[message, pl.ds(size * BODY + k, 1), :] = full[pl.ds(SLOTS * BODY + slot, 1), :]
        return carry

    lax.fori_loop(0, plan[1], move, 0)

    @pl.when(plan[SEG] >= 2)
    def _():
        send[: SHIFTED * BODY, :] = full[: SHIFTED * BODY, :].astype(BF)
        send[SHIFTED * BODY :, :] = full[SLOTS * BODY :, :].astype(BF)

    @pl.when(plan[SEG] < 2)
    def _():
        send[...] = stage[0].astype(BF)

    for r, out in ((1, out1), (2, out2), (3, out3)):
        out[...] = stage[r, :SEND3].astype(BF)


def combine(*args):
    third = jax.ShapeDtypeStruct((SEND3, CHANS), BF)
    return pl.pallas_call(
        combine_body,
        in_specs=[SMEM] + [VMEM] * 4,
        out_specs=[VMEM] * 5,
        out_shape=[
            jax.ShapeDtypeStruct((CHUNK, CHANS), F32),
            jax.ShapeDtypeStruct((SEND2, CHANS), BF),
            third,
            third,
            third,
        ],
        scratch_shapes=[pltpu.VMEM((PLANES, SEND2, CHANS), F32)],
        compiler_params=pltpu.CompilerParams(vmem_limit_bytes=8 * MIB),
        cost_estimate=TINY,
        name="combine",
    )(*args)


def finish_body(plan, full, shifted, got2, got1, got3, fwd, bwd, pool):
    pool[:TWO, :] = full[...]
    pool[TWO:THREE, :] = shifted[...].astype(F32)
    for r, got in ((1, got1), (2, got2), (3, got3)):
        pool[THREE + (r - 1) * SEND3 : THREE + r * SEND3, :] = got[...].astype(F32)
    fwd[...] = jnp.zeros(fwd.shape, F32)
    bwd[...] = jnp.zeros(bwd.shape, F32)

    def write(out, place, n):
        code = plan[WRITES + n]
        body = jnp.bitwise_and(code, 4095)
        i = jnp.right_shift(code, 27)
        at = pl.ds(jnp.bitwise_and(jnp.right_shift(code, 24), 7), 1)
        out[i, place(BODY), at, :] = pool[pl.ds(jnp.bitwise_and(jnp.right_shift(code, 12), 4095), 1), :]
        for m in range(BODY):
            out[i, place(m), at, :] = pool[pl.ds(body + m, 1), :]

    def ahead(n, carry):
        write(fwd, lambda m: m, n)
        return carry

    def behind(n, carry):
        write(bwd, lambda m: BODY - m, n)
        return carry

    lax.fori_loop(0, plan[2], ahead, 0)
    lax.fori_loop(plan[2], plan[3], behind, 0)


def finish(blocks, *args):
    out = jax.ShapeDtypeStruct((blocks, LAGS, REACH, CHANS), F32)
    return pl.pallas_call(
        finish_body,
        in_specs=[SMEM] + [VMEM] * 5,
        out_specs=[VMEM, VMEM],
        out_shape=[out, out],
        scratch_shapes=[pltpu.VMEM((POOL, CHANS), F32)],
        compiler_params=pltpu.CompilerParams(vmem_limit_bytes=8 * MIB),
        cost_estimate=TINY,
        name="finish",
    )(*args)


def shards(groups, planes, lag, records, pairs):
    def ring(x, r):
        return lax.ppermute(x, "seg", [(z, (z + r) % planes) for z in range(planes)])

    outer = [(g, g + 1 if g % 2 else g - 1) for g in range(1, groups - 1)]
    inner = [(g, g ^ 1) for g in range(groups)]
    upward = [(g, g + 1) for g in range(groups - 1)]
    shift = [
        (z * groups + g, z * groups + g + step)
        for z in range(planes)
        for g in range(groups)
        for step in (1 if z < 2 else -1,)
        if 0 <= g + step < groups
    ]
    own_ext = whiten(True, records)
    got_ext = lax.ppermute(own_ext, "blk", outer)
    own_int = whiten(False, records)
    got_int = lax.ppermute(own_int, "blk", inner)
    rows, _ = lax.optimization_barrier((pairs, own_int))
    own = jnp.concatenate([rows, ring(rows, 1), ring(rows, 2), ring(rows, 3)])
    plan = make_plan(own, lax.ppermute(own, "blk", upward))

    keep, out1, out2, out3 = correlate(plan, (own_ext, own_int, got_ext, got_int), lag)
    full, send, out1, out2, out3 = combine(plan, keep, ring(out2, 2), ring(out1, 1), ring(out3, 3))
    shifted = lax.ppermute(send, ("seg", "blk"), shift)
    outs = finish(pairs.shape[0], plan, full, shifted, ring(out2, 2), ring(out1, 1), ring(out3, 3))
    return tuple(jnp.transpose(out, (0, 2, 1, 3)) for out in outs)


def solution(mesh):
    groups = mesh.shape["blk"]
    planes = mesh.shape["seg"]

    def run(records, pairs):
        body = functools.partial(
            shards,
            groups,
            planes,
            jnp.asarray(lag_rows(records.shape[0])),
        )
        return jax.shard_map(
            body,
            mesh=mesh,
            in_specs=(P("seg", "blk", None), P(("blk", "seg"), None)),
            out_specs=(P(("blk", "seg"), None, None, None), P(("blk", "seg"), None, None, None)),
            check_vma=False,
        )(records, pairs)

    return run
```

```python
import functools

import jax
import jax.numpy as jnp
import ml_dtypes
import numpy as np
from jax import lax
from jax.experimental import pallas as pl
from jax.experimental.pallas import tpu as pltpu
from jax.sharding import PartitionSpec as P

BINS = 256
LENGTH = 512
CHANS = 128
MAXLAG = 32
LAGS = 2 * MAXLAG + 1
REACH = 8
SMOOTH = 32
BAND = 64
GROUP = 8
HALF = GROUP // 2
PLANES = 4
ROWS = HALF * CHANS
SUB = 256
REACHED = 384
SLOTS = 13
SHIFTED = 8
BODY = 64
CHUNK = SLOTS * BODY + 16
SEND2 = SHIFTED * BODY + 16
SEND3 = 4 * BODY + 16
SEG, PAIRS, MOVES, WRITES, PLAN = 4, 16, 80, 112, 256
TWO = CHUNK
THREE = CHUNK + SEND2
POOL = THREE + 3 * SEND3
MIB = 1024 * 1024
TINY = pl.CostEstimate(flops=1, bytes_accessed=1, transcendentals=0)
BF = jnp.bfloat16
F32 = jnp.float32
SMEM = pl.BlockSpec(memory_space=pltpu.SMEM)
VMEM = pl.BlockSpec(memory_space=pltpu.VMEM)


def split(array):
    high = array.astype(ml_dtypes.bfloat16)
    low = (array - high.astype(np.float32)).astype(ml_dtypes.bfloat16)
    return high, low


def lag_rows(segments):
    shifts = np.arange(-MAXLAG, MAXLAG + 1)
    phase = (shifts[:, None] * np.arange(BINS)[None, :] % LENGTH) * (2.0 * np.pi / LENGTH)
    table = np.concatenate([np.cos(phase), -np.sin(phase)], axis=1) / np.sqrt(segments * BINS)
    table = np.concatenate([table, np.zeros((CHANS - LAGS, LENGTH))], axis=0).T.astype(np.float32)
    return np.concatenate(split(table), axis=1)


def dot(a, b):
    return jnp.dot(a, b, preferred_element_type=F32)


def halves(x):
    high = x.astype(BF)
    return high, (x - high.astype(F32)).astype(BF)


def inverse(y):
    r = pl.reciprocal(y, approx=True)
    return r * (2.0 - y * r)


def make_tables(tab):
    at = lax.broadcasted_iota(jnp.int32, (REACHED, LENGTH), 0)
    col = lax.broadcasted_iota(jnp.int32, (REACHED, LENGTH), 1)
    apart = at - col + jnp.where(col < BINS, 0, LENGTH - REACHED)
    tab[:REACHED] = jnp.where(jnp.abs(apart) <= SMOOTH, 1.0, 0.0).astype(BF)
    row = lax.broadcasted_iota(jnp.int32, (CHANS, LENGTH), 0)
    col = lax.broadcasted_iota(jnp.int32, (CHANS, LENGTH), 1)
    row = row + jnp.where(col < BINS, 0, CHANS)
    col = jnp.bitwise_and(col, BINS - 1)
    tab[REACHED:LENGTH] = jnp.where(row // BAND == col // BAND, 0.5 / BAND, 0.0).astype(BF)

    def cosine(step, shift, rows):
        k = lax.broadcasted_iota(jnp.int32, (rows, BINS), 0) * lax.broadcasted_iota(jnp.int32, (rows, BINS), 1)
        k = jnp.bitwise_and(k * step - shift + BINS, LENGTH - 1) - BINS
        square = jnp.square(k.astype(F32) * (2.0 * np.pi / LENGTH))
        value = jnp.ones_like(square)
        for n in range(20, 0, -2):
            value = 1.0 - value * square * (1.0 / (n * (n - 1)))
        return value

    quarter = LENGTH // 4
    fine_cos, fine_sin = cosine(1, 0, 16), cosine(1, quarter, 16)
    coarse_cos, coarse_sin = cosine(16, 0, 32), cosine(16, quarter, 32)
    for a in range(LENGTH // 16):
        c, s = coarse_cos[a : a + 1], coarse_sin[a : a + 1]
        for k, part in enumerate((c * fine_cos - s * fine_sin, -(s * fine_cos) - c * fine_sin)):
            high, low = halves(part)
            tab[LENGTH + 16 * a : LENGTH + 16 * a + 16, k * BINS : (k + 1) * BINS] = high
            tab[2 * LENGTH + 16 * a : 2 * LENGTH + 16 * a + 16, k * BINS : (k + 1) * BINS] = low


def whiten_body(outer, after, records, white, buf, tab, sems):
    del after
    segs = records.shape[0]
    core = jnp.bitwise_and(lax.axis_index("blk"), 1)
    begin = pl.multiple_of((core if outer else 1 - core) * ROWS, ROWS)

    def load(k):
        return pltpu.make_async_copy(records.at[k, pl.ds(begin, ROWS)], buf.at[k], sems.at[k])

    for k in range(segs):
        load(k).start()
    at = lax.broadcasted_iota(jnp.int32, (1, LENGTH), 1)
    count = jnp.minimum(at, SMOOTH) + jnp.minimum(LENGTH - 1 - at, SMOOTH) + 1
    share = 1.0 / count.astype(F32)
    make_tables(tab)

    def step(k, carry):
        load(k).wait()
        parts = range(ROWS // SUB)
        xs = [buf[k, pl.ds(n * SUB, SUB), :] for n in parts]
        levels = []
        first = tab[:REACHED, :BINS]
        second = tab[:REACHED, BINS:]
        for x in xs:
            ahi, alo = halves(jnp.abs(x))
            left = jnp.concatenate([ahi[:, :REACHED], alo[:, :REACHED]], axis=1)
            right = jnp.concatenate([ahi[:, LENGTH - REACHED :], alo[:, LENGTH - REACHED :]], axis=1)
            left = dot(left, jnp.concatenate([first, first], axis=0))
            right = dot(right, jnp.concatenate([second, second], axis=0))
            levels.append(jnp.concatenate([left, right], axis=1) * share)
        spectra = []
        fhi = tab[LENGTH : 2 * LENGTH]
        fourier = jnp.concatenate([fhi, fhi, tab[2 * LENGTH :]], axis=0)
        for x, level in zip(xs, levels):
            nhi, nlo = halves(x * inverse(level + 1e-06))
            spectra.append(dot(jnp.concatenate([nhi, nlo, nhi], axis=1), fourier))
        same = jnp.concatenate([tab[REACHED:LENGTH, :BINS], tab[REACHED:LENGTH, BINS:]], axis=0)
        for n in parts:
            re = spectra[n][:, :BINS]
            im = spectra[n][:, BINS:]
            power = dot((re * re + im * im).astype(BF), same)
            factor = lax.rsqrt(power + 1e-05)
            per = SUB // CHANS
            white[pl.ds(n * per, per), k, :, :BINS] = (re * factor).astype(BF).reshape(per, CHANS, BINS)
            white[pl.ds(n * per, per), k, :, BINS:] = (im * factor).astype(BF).reshape(per, CHANS, BINS)
        return carry

    lax.fori_loop(0, segs, step, 0)


def whiten(outer, after, records):
    segs = records.shape[0]
    return pl.pallas_call(
        functools.partial(whiten_body, outer),
        in_specs=[SMEM, pl.BlockSpec(memory_space=pltpu.HBM)],
        out_specs=VMEM,
        out_shape=jax.ShapeDtypeStruct((HALF, segs, CHANS, LENGTH), BF),
        scratch_shapes=[
            pltpu.VMEM((segs, ROWS, LENGTH), F32),
            pltpu.VMEM((3 * LENGTH, LENGTH), BF),
            pltpu.SemaphoreType.DMA((segs,)),
        ],
        compiler_params=pltpu.CompilerParams(vmem_limit_bytes=50 * MIB),
        cost_estimate=TINY,
        name="whiten",
    )(after, records)


VISITS = [(p, d) for p in range(HALF) for d in range(1, REACH + 1) if p + d >= HALF] + [
    (p, d) for p in range(HALF, 12) for d in range(1, REACH + 1) if p < GROUP or p + d < 12
]
UPWARD = (
    ((0, 0), (1, 0), (1, 1), (2, 0), (2, 1), (3, 0), (3, 1)),
    ((2, 2), (3, 2), (3, 3)),
)


def plan_body(pairs, plan, slots):
    s = lax.axis_index("seg").astype(jnp.int32)
    plan[SEG] = s
    zero = jnp.int32(0)

    def look(row, before, d):
        return pairs[4 * (row // 2) + row % 2 + 2 * before, d - 1]

    used = [zero] * PLANES
    n = zero
    for p, d in VISITS:
        row = p + HALF if p < HALF else p - HALF
        owner = row // 2
        live = look(row, int(p < HALF), d)
        code = p + d * 16 + jnp.bitwise_and(owner - s, 3) * 256 + used[owner] * 4096
        slots[p * REACH + d - 1] = used[owner]
        used[owner] = used[owner] + live
        if p in (6, 7) and p + d in (12, 13):
            slots[96 + (p - 6) * 2 + p + d - 12] = used[0]
            code = code + (used[0] + 1) * 65536
            used[0] = used[0] + live
        plan[PAIRS + n] = code
        n = n + live
    plan[0] = n

    n = zero
    for owner in (0, 1):
        for k, (i, j) in enumerate(UPWARD[owner]):
            p, d = HALF + i, GROUP + j - i
            entry = p * REACH + d - 1 if i // 2 == owner else 96 + (i - 2) * 2 + j
            plan[MOVES + n] = slots[entry] + k * 4096
            n = n + jnp.where(s == owner, look(i, 0, d), 0)
    for r in range(1, PLANES):
        to = jnp.bitwise_and(s + r, 3)
        ahead = s < to
        for i in range(2):
            for j in range(2):
                row = 2 * s + i
                p = jnp.where(ahead, row + HALF, jnp.maximum(row - HALF, 0))
                d = 2 * to + j - row + jnp.where(ahead, 0, GROUP)
                live = jnp.where(ahead, pairs[4 * s + i, d - 1], jnp.where(s >= 2, pairs[4 * s + 2 + i, d - 1], 0))
                plan[MOVES + n] = slots[p * REACH + d - 1] + r * 256 + (2 * i + j) * 4096
                n = n + live
    plan[1] = n

    def write(n, i, d, base, size, slot):
        plan[WRITES + n] = base + slot * BODY + (base + size * BODY + slot) * 4096 + (i * 8 + d - 1) * 16777216

    n = zero
    above = zero
    for i in range(2):
        for d in range(1, REACH + 1):
            row = 2 * s + i
            live = pairs[4 * s + i, d - 1]
            shift = (row + d >= GROUP) & (s >= 2)
            slot = jnp.where(shift, above, slots[(HALF + row) * REACH + d - 1])
            write(n, i, d, jnp.where(shift, TWO, 0), jnp.where(shift, SHIFTED, SLOTS), slot)
            n = n + live
            above = above + jnp.where(shift, live, 0)
    plan[2] = n
    for j in range(2):
        for d in range(1, REACH + 1):
            low = 2 * s + j - d
            crossing = low < 0
            row = jnp.where(crossing, low + GROUP, low)
            owner = jnp.right_shift(row, 1)
            live = pairs[4 * owner + jnp.bitwise_and(row, 1) + jnp.where(crossing, 2, 0), d - 1]
            up = crossing & (owner < 2)
            mine = (owner == s) & jnp.logical_not(up)
            k0 = jnp.where(row == 0, 0, 2 * row - 1) + j
            k1 = jnp.where(row == 2, 0, 1) + j
            entry = jnp.maximum((HALF + low) * REACH + d - 1, 0)
            slot = jnp.where(mine, slots[entry], 2 * (row - 2 * owner) + j)
            slot = jnp.where(up, jnp.where(s == 0, k0, k1), slot)
            base = jnp.where(mine, 0, THREE + (jnp.bitwise_and(s - owner, 3) - 1) * SEND3)
            base = jnp.where(up, TWO, base)
            size = jnp.where(mine, SLOTS, jnp.where(up, SHIFTED, 4))
            write(n, j, d, base, size, slot)
            n = n + live
    plan[3] = n


def make_plan(pairs):
    return pl.pallas_call(
        plan_body,
        in_specs=[SMEM],
        out_specs=SMEM,
        out_shape=jax.ShapeDtypeStruct((PLAN,), jnp.int32),
        scratch_shapes=[pltpu.SMEM((128,), jnp.int32)],
        cost_estimate=TINY,
        name="plan",
    )(pairs)


def correlate_body(plan, own_ext, own_int, got_ext, got_int, lag, keep, out1, out2, out3, low, high, stk, pq, last):
    core = jnp.bitwise_and(lax.axis_index("blk"), 1)
    sources = (
        (own_ext, HALF * (1 + core)),
        (own_int, HALF * (2 - core)),
        (got_ext, 3 * HALF * core),
        (got_int, 3 * HALF * (1 - core)),
    )
    segs = low.shape[0]
    last[0] = -1

    def grab(dest, block):
        for ref, begin in sources:

            @pl.when((block >= begin) & (block < begin + HALF))
            def _(ref=ref, begin=begin):
                dest[...] = ref[block - begin]

    def put(r, n, stack):
        stk[r, pl.ds(pl.multiple_of(n * BODY, BODY), BODY), :] = stack[:BODY]
        stk[r, pl.ds(SLOTS * BODY + n, 1), :] = stack[BODY:LAGS]

    def pair(n, carry):
        code = plan[PAIRS + n]
        p = jnp.bitwise_and(code, 15)
        d = jnp.bitwise_and(jnp.right_shift(code, 4), 15)

        @pl.when(last[0] != p)
        def _():
            grab(low, p)
            last[0] = p

        grab(high, p + d)
        for chunk in range(CHANS // 16):
            rows = pl.ds(chunk * 16, 16)
            real = jnp.zeros((16, BINS), F32)
            imag = jnp.zeros((16, BINS), F32)
            for k in range(segs):
                are = low[k, rows, :BINS].astype(F32)
                aim = low[k, rows, BINS:].astype(F32)
                bre = high[k, rows, :BINS].astype(F32)
                bim = high[k, rows, BINS:].astype(F32)
                real += are * bre + aim * bim
                imag += are * bim - aim * bre
            rhi, rlo = halves(real)
            ihi, ilo = halves(imag)
            pq[0, rows, :BINS] = rhi
            pq[0, rows, BINS:] = ihi
            pq[1, rows, :BINS] = rlo
            pq[1, rows, BINS:] = ilo
        both = dot(pq[0], lag[...])
        stack = (both[:, :CHANS] + both[:, CHANS:] + dot(pq[1], lag[:, :CHANS])).T
        put(jnp.bitwise_and(jnp.right_shift(code, 8), 3), jnp.bitwise_and(jnp.right_shift(code, 12), 15), stack)
        second = jnp.right_shift(code, 16)

        @pl.when(second > 0)
        def _():
            put(jnp.bitwise_and(-plan[SEG], 3), second - 1, stack)

        return carry

    lax.fori_loop(0, plan[0], pair, 0)
    keep[...] = stk[0]
    out1[...] = stk[1].astype(BF)
    out2[...] = stk[2].astype(BF)
    out3[...] = stk[3].astype(BF)


def correlate(plan, whites, lag):
    segs = whites[0].shape[1]
    chunk = jax.ShapeDtypeStruct((CHUNK, CHANS), BF)
    return pl.pallas_call(
        correlate_body,
        in_specs=[SMEM] + [VMEM] * 5,
        out_specs=[VMEM] * 4,
        out_shape=[jax.ShapeDtypeStruct((CHUNK, CHANS), F32), chunk, chunk, chunk],
        scratch_shapes=[
            pltpu.VMEM((segs, CHANS, LENGTH), BF),
            pltpu.VMEM((segs, CHANS, LENGTH), BF),
            pltpu.VMEM((PLANES, CHUNK, CHANS), F32),
            pltpu.VMEM((2, CHANS, LENGTH), BF),
            pltpu.SMEM((1,), jnp.int32),
        ],
        compiler_params=pltpu.CompilerParams(vmem_limit_bytes=16 * MIB),
        cost_estimate=TINY,
        name="correlate",
    )(plan, *whites, lag)


def combine_body(plan, keep, got2, got1, got3, full, send, out1, out2, out3, stage):
    full[...] = (keep[...] + got1[...].astype(F32)) + (got2[...].astype(F32) + got3[...].astype(F32))

    def move(n, carry):
        code = plan[MOVES + n]
        slot = jnp.bitwise_and(code, 255)
        message = jnp.bitwise_and(jnp.right_shift(code, 8), 15)
        k = jnp.right_shift(code, 12)
        size = jnp.where(message == 0, SHIFTED, 4)
        body = pl.ds(pl.multiple_of(slot * BODY, BODY), BODY)
        stage[message, pl.ds(pl.multiple_of(k * BODY, BODY), BODY), :] = full[body, :]
        stage[message, pl.ds(size * BODY + k, 1), :] = full[pl.ds(SLOTS * BODY + slot, 1), :]
        return carry

    lax.fori_loop(0, plan[1], move, 0)

    @pl.when(plan[SEG] >= 2)
    def _():
        send[: SHIFTED * BODY, :] = full[: SHIFTED * BODY, :].astype(BF)
        send[SHIFTED * BODY :, :] = full[SLOTS * BODY :, :].astype(BF)

    @pl.when(plan[SEG] < 2)
    def _():
        send[...] = stage[0].astype(BF)

    for r, out in ((1, out1), (2, out2), (3, out3)):
        out[...] = stage[r, :SEND3].astype(BF)


def combine(*args):
    third = jax.ShapeDtypeStruct((SEND3, CHANS), BF)
    return pl.pallas_call(
        combine_body,
        in_specs=[SMEM] + [VMEM] * 4,
        out_specs=[VMEM] * 5,
        out_shape=[
            jax.ShapeDtypeStruct((CHUNK, CHANS), F32),
            jax.ShapeDtypeStruct((SEND2, CHANS), BF),
            third,
            third,
            third,
        ],
        scratch_shapes=[pltpu.VMEM((PLANES, SEND2, CHANS), F32)],
        compiler_params=pltpu.CompilerParams(vmem_limit_bytes=8 * MIB),
        cost_estimate=TINY,
        name="combine",
    )(*args)


def finish_body(plan, full, shifted, got2, got1, got3, fwd, bwd, pool):
    pool[:TWO, :] = full[...]
    pool[TWO:THREE, :] = shifted[...].astype(F32)
    for r, got in ((1, got1), (2, got2), (3, got3)):
        pool[THREE + (r - 1) * SEND3 : THREE + r * SEND3, :] = got[...].astype(F32)
    fwd[...] = jnp.zeros(fwd.shape, F32)
    bwd[...] = jnp.zeros(bwd.shape, F32)

    def write(out, place, n):
        code = plan[WRITES + n]
        body = jnp.bitwise_and(code, 4095)
        i = jnp.right_shift(code, 27)
        at = pl.ds(jnp.bitwise_and(jnp.right_shift(code, 24), 7), 1)
        out[i, place(BODY), at, :] = pool[pl.ds(jnp.bitwise_and(jnp.right_shift(code, 12), 4095), 1), :]
        for m in range(BODY):
            out[i, place(m), at, :] = pool[pl.ds(body + m, 1), :]

    def ahead(n, carry):
        write(fwd, lambda m: m, n)
        return carry

    def behind(n, carry):
        write(bwd, lambda m: BODY - m, n)
        return carry

    lax.fori_loop(0, plan[2], ahead, 0)
    lax.fori_loop(plan[2], plan[3], behind, 0)


def finish(blocks, *args):
    out = jax.ShapeDtypeStruct((blocks, LAGS, REACH, CHANS), F32)
    return pl.pallas_call(
        finish_body,
        in_specs=[SMEM] + [VMEM] * 5,
        out_specs=[VMEM, VMEM],
        out_shape=[out, out],
        scratch_shapes=[pltpu.VMEM((POOL, CHANS), F32)],
        compiler_params=pltpu.CompilerParams(vmem_limit_bytes=8 * MIB),
        cost_estimate=TINY,
        name="finish",
    )(*args)


def shards(groups, planes, lag, records, pairs):
    def ring(x, r):
        return lax.ppermute(x, "seg", [(z, (z + r) % planes) for z in range(planes)])

    outer = [(g, g + 1 if g % 2 else g - 1) for g in range(1, groups - 1)]
    inner = [(g, g ^ 1) for g in range(groups)]
    upward = [(g, g + 1) for g in range(groups - 1)]
    shift = [
        (z * groups + g, z * groups + g + step)
        for z in range(planes)
        for g in range(groups)
        for step in (1 if z < 2 else -1,)
        if 0 <= g + step < groups
    ]
    before = lax.ppermute(pairs, "blk", upward)
    both = jnp.concatenate([pairs, before]).astype(F32)
    both = lax.optimization_barrier(jnp.broadcast_to(both[:, :, None, None], (4, REACH, 8, CHANS)))
    both = lax.all_gather(both, "seg", axis=0, tiled=True)
    both = both[:, :, 0, 0].astype(jnp.int32)

    own_ext = whiten(True, before, records)
    got_ext = lax.ppermute(own_ext, "blk", outer)
    own_int = whiten(False, before, records)
    own_int, both = lax.optimization_barrier((own_int, both))
    got_int = lax.ppermute(own_int, "blk", inner)
    plan = make_plan(both)
    keep, out1, out2, out3 = correlate(plan, (own_ext, own_int, got_ext, got_int), lag)
    full, send, out1, out2, out3 = combine(plan, keep, ring(out2, 2), ring(out1, 1), ring(out3, 3))
    shifted = lax.ppermute(send, ("seg", "blk"), shift)
    outs = finish(pairs.shape[0], plan, full, shifted, ring(out2, 2), ring(out1, 1), ring(out3, 3))
    return tuple(jnp.transpose(out, (0, 2, 1, 3)) for out in outs)


def solution(mesh):
    groups = mesh.shape["blk"]
    planes = mesh.shape["seg"]

    def run(records, pairs):
        body = functools.partial(
            shards,
            groups,
            planes,
            jnp.asarray(lag_rows(records.shape[0])),
        )
        return jax.shard_map(
            body,
            mesh=mesh,
            in_specs=(P("seg", "blk", None), P(("blk", "seg"), None)),
            out_specs=(P(("blk", "seg"), None, None, None), P(("blk", "seg"), None, None, None)),
            check_vma=False,
        )(records, pairs)

    return run
```

```python
import functools

import jax
import jax.numpy as jnp
import ml_dtypes
import numpy as np
from jax import lax
from jax.experimental import pallas as pl
from jax.experimental.pallas import tpu as pltpu
from jax.sharding import PartitionSpec as P

BINS = 256
LENGTH = 512
CHANS = 128
MAXLAG = 32
LAGS = 2 * MAXLAG + 1
REACH = 8
SMOOTH = 32
BAND = 64
GROUP = 8
HALF = GROUP // 2
PLANES = 4
ROWS = HALF * CHANS
SUB = 256
REACHED = 384
SLOTS = 13
SHIFTED = 8
BODY = 64
CHUNK = SLOTS * BODY + 16
SEND2 = SHIFTED * BODY + 16
SEND3 = 4 * BODY + 16
PAIRS, MOVES, WRITES = 48, 32, 8
TWO = CHUNK
THREE = CHUNK + SEND2
POOL = THREE + 3 * SEND3
MIB = 1024 * 1024
TINY = pl.CostEstimate(flops=1, bytes_accessed=1, transcendentals=0)
BF = jnp.bfloat16
F32 = jnp.float32
SMEM = pl.BlockSpec(memory_space=pltpu.SMEM)
VMEM = pl.BlockSpec(memory_space=pltpu.VMEM)


def split(array):
    high = array.astype(ml_dtypes.bfloat16)
    low = (array - high.astype(np.float32)).astype(ml_dtypes.bfloat16)
    return high, low


def lag_rows(segments):
    freqs = np.concatenate([np.arange(0, BINS, 2), np.arange(1, BINS, 2)])
    shifts = np.arange(-MAXLAG, MAXLAG + 1)
    phase = (shifts[:, None] * freqs[None, :] % LENGTH) * (2.0 * np.pi / LENGTH)
    table = np.concatenate([np.cos(phase), -np.sin(phase)], axis=1) / np.sqrt(segments * BINS)
    table = np.concatenate([table, np.zeros((CHANS - LAGS, LENGTH))], axis=0).T.astype(np.float32)
    return np.concatenate(split(table), axis=1)


def dot(a, b):
    return jnp.dot(a, b, preferred_element_type=F32)


def halves(x):
    high = x.astype(BF)
    return high, (x - high.astype(F32)).astype(BF)


def inverse(y):
    r = pl.reciprocal(y, approx=True)
    return r * (2.0 - y * r)


def make_tables(tab):
    at = lax.broadcasted_iota(jnp.int32, (REACHED, LENGTH), 0)
    col = lax.broadcasted_iota(jnp.int32, (REACHED, LENGTH), 1)
    apart = at - col + jnp.where(col < BINS, 0, LENGTH - REACHED)
    tab[:REACHED] = jnp.where(jnp.abs(apart) <= SMOOTH, 1.0, 0.0).astype(BF)
    half = BINS // 2
    row = lax.broadcasted_iota(jnp.int32, (CHANS, LENGTH), 0)
    col = lax.broadcasted_iota(jnp.int32, (CHANS, LENGTH), 1)
    row = jnp.bitwise_and(row, half - 1) // (BAND // 2)
    col = jnp.bitwise_and(col, half - 1) // (BAND // 2)
    tab[REACHED:LENGTH] = jnp.where(row == col, 0.5 / BAND, 0.0).astype(BF)

    def cosine(step, shift):
        col = lax.broadcasted_iota(jnp.int32, (16, BINS), 1)
        freq = 2 * jnp.bitwise_and(col, half - 1) + jnp.right_shift(col, 7)
        k = lax.broadcasted_iota(jnp.int32, (16, BINS), 0) * freq
        k = jnp.bitwise_and(k * step - shift + BINS, LENGTH - 1) - BINS
        square = jnp.square(k.astype(F32) * (2.0 * np.pi / LENGTH))
        value = jnp.ones_like(square)
        for n in range(20, 0, -2):
            value = 1.0 - value * square * (1.0 / (n * (n - 1)))
        return value

    quarter = LENGTH // 4
    fine_cos, fine_sin = cosine(1, 0), cosine(1, quarter)
    coarse_cos, coarse_sin = cosine(16, 0), cosine(16, quarter)
    for a in range(16):
        c, s = coarse_cos[a : a + 1], coarse_sin[a : a + 1]
        for k, part in enumerate((c * fine_cos - s * fine_sin, -(s * fine_cos) - c * fine_sin)):
            for n, rounded in enumerate(halves(part)):
                rows = pl.ds(LENGTH + n * BINS + 16 * a, 16)
                tab[rows, k * half : (k + 1) * half] = rounded[:, :half]
                tab[rows, BINS + k * half : BINS + (k + 1) * half] = rounded[:, half:]


def whiten_body(outer, records, white, buf, tab, sems):
    segs = records.shape[0]
    core = jnp.bitwise_and(lax.axis_index("blk"), 1)
    begin = pl.multiple_of((core if outer else 1 - core) * ROWS, ROWS)

    def load(k):
        return pltpu.make_async_copy(records.at[k, pl.ds(begin, ROWS)], buf.at[k], sems.at[k])

    for k in range(segs):
        load(k).start()
    at = lax.broadcasted_iota(jnp.int32, (1, LENGTH), 1)
    count = jnp.minimum(at, SMOOTH) + jnp.minimum(LENGTH - 1 - at, SMOOTH) + 1
    share = 1.0 / count.astype(F32)
    make_tables(tab)

    def step(k, carry):
        load(k).wait()
        parts = range(ROWS // SUB)
        xs = [buf[k, pl.ds(n * SUB, SUB), :] for n in parts]
        levels = []
        first = tab[:REACHED, :BINS]
        second = tab[:REACHED, BINS:]
        for x in xs:
            ahi, alo = halves(jnp.abs(x))
            left = jnp.concatenate([ahi[:, :REACHED], alo[:, :REACHED]], axis=1)
            right = jnp.concatenate([ahi[:, LENGTH - REACHED :], alo[:, LENGTH - REACHED :]], axis=1)
            left = dot(left, jnp.concatenate([first, first], axis=0))
            right = dot(right, jnp.concatenate([second, second], axis=0))
            levels.append(jnp.concatenate([left, right], axis=1) * share)
        spectra = []
        products = []
        for at in (0, BINS):
            high = tab[LENGTH : LENGTH + BINS, at : at + BINS]
            products.append(jnp.concatenate([high, high, tab[LENGTH + BINS :, at : at + BINS]], axis=0))
        for x, level in zip(xs, levels):
            normed = x * inverse(level + 1e-06)
            left, right = normed[:, :BINS], normed[:, BINS:]
            pair = []
            for part, product in zip((left + right, left - right), products):
                high, low = halves(part)
                pair.append(dot(jnp.concatenate([high, low, high], axis=1), product))
            spectra.append(pair)
        same = jnp.concatenate([tab[REACHED:LENGTH, :BINS], tab[REACHED:LENGTH, BINS:]], axis=0)
        for n in parts:
            even, odd = spectra[n]
            re = jnp.concatenate([even[:, : BINS // 2], odd[:, : BINS // 2]], axis=1)
            im = jnp.concatenate([even[:, BINS // 2 :], odd[:, BINS // 2 :]], axis=1)
            power = dot((re * re + im * im).astype(BF), same)
            factor = lax.rsqrt(power + 1e-05)
            per = SUB // CHANS
            white[pl.ds(n * per, per), k, :, :BINS] = (re * factor).astype(BF).reshape(per, CHANS, BINS)
            white[pl.ds(n * per, per), k, :, BINS:] = (im * factor).astype(BF).reshape(per, CHANS, BINS)
        return carry

    lax.fori_loop(0, segs, step, 0)


def whiten(outer, records):
    segs = records.shape[0]
    return pl.pallas_call(
        functools.partial(whiten_body, outer),
        in_specs=[pl.BlockSpec(memory_space=pltpu.HBM)],
        out_specs=VMEM,
        out_shape=jax.ShapeDtypeStruct((HALF, segs, CHANS, LENGTH), BF),
        scratch_shapes=[
            pltpu.VMEM((segs, ROWS, LENGTH), F32),
            pltpu.VMEM((2 * LENGTH, LENGTH), BF),
            pltpu.SemaphoreType.DMA((segs,)),
        ],
        compiler_params=pltpu.CompilerParams(vmem_limit_bytes=50 * MIB),
        cost_estimate=TINY,
        name="whiten",
    )(records)


VISITS = [(p, d) for p in range(HALF) for d in range(1, REACH + 1) if p + d >= HALF] + [
    (p, d) for p in range(HALF, 12) for d in range(1, REACH + 1) if p < GROUP or p + d < 12
]
UPWARD = (
    ((0, 0), (1, 0), (1, 1), (2, 0), (2, 1), (3, 0), (3, 1)),
    ((2, 2), (3, 2), (3, 3)),
)


def seg_index():
    return lax.axis_index("seg").astype(jnp.int32)


def behind(owner):
    return 2 * jnp.bitwise_and(seg_index() - owner, 3)


def list_pairs(own, before, codes, slots):
    s = seg_index()
    used = [jnp.int32(0)] * PLANES
    n = jnp.int32(0)
    for p, d in VISITS:
        row = p + HALF if p < HALF else p - HALF
        owner = row // 2
        live = (before if p < HALF else own)[behind(owner) + row % 2, d - 1]
        code = p + d * 16 + jnp.bitwise_and(owner - s, 3) * 256 + used[owner] * 4096
        slots[p * REACH + d - 1] = used[owner]
        used[owner] = used[owner] + live
        if p in (6, 7) and p + d in (12, 13):
            slots[96 + (p - 6) * 2 + p + d - 12] = used[0]
            code = code + (used[0] + 1) * 65536
            used[0] = used[0] + live
        codes[n] = code
        n = n + live
    return n


def list_moves(own, before, slots, moves):
    s = seg_index()
    n = jnp.int32(0)
    for owner in (0, 1):
        for k, (i, j) in enumerate(UPWARD[owner]):
            p, d = HALF + i, GROUP + j - i
            entry = p * REACH + d - 1 if i // 2 == owner else 96 + (i - 2) * 2 + j
            moves[n] = slots[entry] + k * 4096
            n = n + jnp.where(s == owner, own[behind(i // 2) + i % 2, d - 1], 0)
    for r in range(1, PLANES):
        to = jnp.bitwise_and(s + r, 3)
        ahead = s < to
        for i in range(2):
            for j in range(2):
                row = 2 * s + i
                p = jnp.where(ahead, row + HALF, jnp.maximum(row - HALF, 0))
                d = 2 * to + j - row + jnp.where(ahead, 0, GROUP)
                live = jnp.where(ahead, own[i, d - 1], jnp.where(s >= 2, before[i, d - 1], 0))
                moves[n] = slots[p * REACH + d - 1] + r * 256 + (2 * i + j) * 4096
                n = n + live
    return n


def list_writes(own, before, slots, writes):
    s = seg_index()

    def write(n, i, d, base, size, slot):
        writes[WRITES + n] = base + slot * BODY + (base + size * BODY + slot) * 4096 + (i * 8 + d - 1) * 16777216

    n = jnp.int32(0)
    above = jnp.int32(0)
    for i in range(2):
        for d in range(1, REACH + 1):
            row = 2 * s + i
            live = own[i, d - 1]
            shift = (row + d >= GROUP) & (s >= 2)
            slot = jnp.where(shift, above, slots[(HALF + row) * REACH + d - 1])
            write(n, i, d, jnp.where(shift, TWO, 0), jnp.where(shift, SHIFTED, SLOTS), slot)
            n = n + live
            above = above + jnp.where(shift, live, 0)
    writes[0] = n
    for j in range(2):
        for d in range(1, REACH + 1):
            low = 2 * s + j - d
            crossing = low < 0
            row = jnp.where(crossing, low + GROUP, low)
            owner = jnp.right_shift(row, 1)
            at = behind(owner) + jnp.bitwise_and(row, 1)
            live = jnp.where(crossing, before[at, d - 1], own[at, d - 1])
            up = crossing & (owner < 2)
            mine = (owner == s) & jnp.logical_not(up)
            k0 = jnp.where(row == 0, 0, 2 * row - 1) + j
            k1 = jnp.where(row == 2, 0, 1) + j
            entry = jnp.maximum((HALF + low) * REACH + d - 1, 0)
            slot = jnp.where(mine, slots[entry], 2 * (row - 2 * owner) + j)
            slot = jnp.where(up, jnp.where(s == 0, k0, k1), slot)
            base = jnp.where(mine, 0, THREE + (jnp.bitwise_and(s - owner, 3) - 1) * SEND3)
            base = jnp.where(up, TWO, base)
            size = jnp.where(mine, SLOTS, jnp.where(up, SHIFTED, 4))
            write(n, j, d, base, size, slot)
            n = n + live
    writes[1] = n


def correlate_body(
    own, before, own_ext, own_int, got_ext, got_int, lag, keep, out1, out2, out3, slots, low, high, stk, pq, codes, last
):
    count = list_pairs(own, before, codes, slots)
    core = jnp.bitwise_and(lax.axis_index("blk"), 1)
    sources = (
        (own_ext, HALF * (1 + core)),
        (own_int, HALF * (2 - core)),
        (got_ext, 3 * HALF * core),
        (got_int, 3 * HALF * (1 - core)),
    )
    segs = low.shape[0]
    last[0] = -1

    def grab(dest, block):
        for ref, begin in sources:

            @pl.when((block >= begin) & (block < begin + HALF))
            def _(ref=ref, begin=begin):
                dest[...] = ref[block - begin]

    def put(r, n, stack):
        stk[r, pl.ds(pl.multiple_of(n * BODY, BODY), BODY), :] = stack[:BODY]
        stk[r, pl.ds(SLOTS * BODY + n, 1), :] = stack[BODY:LAGS]

    def pair(n, carry):
        code = codes[n]
        p = jnp.bitwise_and(code, 15)
        d = jnp.bitwise_and(jnp.right_shift(code, 4), 15)

        @pl.when(last[0] != p)
        def _():
            grab(low, p)
            last[0] = p

        grab(high, p + d)
        for chunk in range(CHANS // 16):
            rows = pl.ds(chunk * 16, 16)
            real = jnp.zeros((16, BINS), F32)
            imag = jnp.zeros((16, BINS), F32)
            for k in range(segs):
                are = low[k, rows, :BINS].astype(F32)
                aim = low[k, rows, BINS:].astype(F32)
                bre = high[k, rows, :BINS].astype(F32)
                bim = high[k, rows, BINS:].astype(F32)
                real += are * bre + aim * bim
                imag += are * bim - aim * bre
            rhi, rlo = halves(real)
            ihi, ilo = halves(imag)
            pq[0, rows, :BINS] = rhi
            pq[0, rows, BINS:] = ihi
            pq[1, rows, :BINS] = rlo
            pq[1, rows, BINS:] = ilo
        both = dot(pq[0], lag[...])
        stack = (both[:, :CHANS] + both[:, CHANS:] + dot(pq[1], lag[:, :CHANS])).T
        put(jnp.bitwise_and(jnp.right_shift(code, 8), 3), jnp.bitwise_and(jnp.right_shift(code, 12), 15), stack)
        second = jnp.right_shift(code, 16)

        @pl.when(second > 0)
        def _():
            put(jnp.bitwise_and(-seg_index(), 3), second - 1, stack)

        return carry

    lax.fori_loop(0, count, pair, 0)
    keep[...] = stk[0]
    out1[...] = stk[1].astype(BF)
    out2[...] = stk[2].astype(BF)
    out3[...] = stk[3].astype(BF)


def correlate(own, before, whites, lag):
    segs = whites[0].shape[1]
    chunk = jax.ShapeDtypeStruct((CHUNK, CHANS), BF)
    return pl.pallas_call(
        correlate_body,
        in_specs=[SMEM] * 2 + [VMEM] * 5,
        out_specs=[VMEM] * 4 + [SMEM],
        out_shape=[
            jax.ShapeDtypeStruct((CHUNK, CHANS), F32),
            chunk,
            chunk,
            chunk,
            jax.ShapeDtypeStruct((128,), jnp.int32),
        ],
        scratch_shapes=[
            pltpu.VMEM((segs, CHANS, LENGTH), BF),
            pltpu.VMEM((segs, CHANS, LENGTH), BF),
            pltpu.VMEM((PLANES, CHUNK, CHANS), F32),
            pltpu.VMEM((2, CHANS, LENGTH), BF),
            pltpu.SMEM((PAIRS,), jnp.int32),
            pltpu.SMEM((1,), jnp.int32),
        ],
        compiler_params=pltpu.CompilerParams(vmem_limit_bytes=16 * MIB),
        cost_estimate=TINY,
        name="correlate",
    )(own, before, *whites, lag)


def combine_body(
    own, before, slots, keep, got2, got1, got3, full, send, out1, out2, out3, writes, stage, moves
):
    count = list_moves(own, before, slots, moves)
    full[...] = (keep[...] + got1[...].astype(F32)) + (got2[...].astype(F32) + got3[...].astype(F32))

    def move(n, carry):
        code = moves[n]
        slot = jnp.bitwise_and(code, 255)
        message = jnp.bitwise_and(jnp.right_shift(code, 8), 15)
        k = jnp.right_shift(code, 12)
        size = jnp.where(message == 0, SHIFTED, 4)
        body = pl.ds(pl.multiple_of(slot * BODY, BODY), BODY)
        stage[message, pl.ds(pl.multiple_of(k * BODY, BODY), BODY), :] = full[body, :]
        stage[message, pl.ds(size * BODY + k, 1), :] = full[pl.ds(SLOTS * BODY + slot, 1), :]
        return carry

    lax.fori_loop(0, count, move, 0)

    @pl.when(seg_index() >= 2)
    def _():
        send[: SHIFTED * BODY, :] = full[: SHIFTED * BODY, :].astype(BF)
        send[SHIFTED * BODY :, :] = full[SLOTS * BODY :, :].astype(BF)

    @pl.when(seg_index() < 2)
    def _():
        send[...] = stage[0].astype(BF)

    for r, out in ((1, out1), (2, out2), (3, out3)):
        out[...] = stage[r, :SEND3].astype(BF)
    list_writes(own, before, slots, writes)


def combine(*args):
    third = jax.ShapeDtypeStruct((SEND3, CHANS), BF)
    return pl.pallas_call(
        combine_body,
        in_specs=[SMEM] * 3 + [VMEM] * 4,
        out_specs=[VMEM] * 5 + [SMEM],
        out_shape=[
            jax.ShapeDtypeStruct((CHUNK, CHANS), F32),
            jax.ShapeDtypeStruct((SEND2, CHANS), BF),
            third,
            third,
            third,
            jax.ShapeDtypeStruct((WRITES + 40,), jnp.int32),
        ],
        scratch_shapes=[pltpu.VMEM((PLANES, SEND2, CHANS), F32), pltpu.SMEM((MOVES,), jnp.int32)],
        compiler_params=pltpu.CompilerParams(vmem_limit_bytes=8 * MIB),
        cost_estimate=TINY,
        name="combine",
    )(*args)


def finish_body(writes, full, got2, got1, got3, shifted, fwd, bwd, pool):
    pool[:TWO, :] = full[...]
    pool[TWO:THREE, :] = shifted[...].astype(F32)
    for r, got in ((1, got1), (2, got2), (3, got3)):
        pool[THREE + (r - 1) * SEND3 : THREE + r * SEND3, :] = got[...].astype(F32)
    fwd[...] = jnp.zeros(fwd.shape, F32)
    bwd[...] = jnp.zeros(bwd.shape, F32)

    def write(out, place, n):
        code = writes[WRITES + n]
        body = jnp.bitwise_and(code, 4095)
        i = jnp.right_shift(code, 27)
        at = pl.ds(jnp.bitwise_and(jnp.right_shift(code, 24), 7), 1)
        out[i, place(BODY), at, :] = pool[pl.ds(jnp.bitwise_and(jnp.right_shift(code, 12), 4095), 1), :]
        for m in range(BODY):
            out[i, place(m), at, :] = pool[pl.ds(body + m, 1), :]

    def ahead(n, carry):
        write(fwd, lambda m: m, n)
        return carry

    def behind(n, carry):
        write(bwd, lambda m: BODY - m, n)
        return carry

    lax.fori_loop(0, writes[0], ahead, 0)
    lax.fori_loop(writes[0], writes[1], behind, 0)


def finish(blocks, *args):
    out = jax.ShapeDtypeStruct((blocks, LAGS, REACH, CHANS), F32)
    return pl.pallas_call(
        finish_body,
        in_specs=[SMEM] + [VMEM] * 5,
        out_specs=[VMEM, VMEM],
        out_shape=[out, out],
        scratch_shapes=[pltpu.VMEM((POOL, CHANS), F32)],
        compiler_params=pltpu.CompilerParams(vmem_limit_bytes=8 * MIB),
        cost_estimate=TINY,
        name="finish",
    )(*args)


def shards(groups, planes, lag, records, pairs):
    def ring(x, r):
        return lax.ppermute(x, "seg", [(z, (z + r) % planes) for z in range(planes)])

    outer = [(g, g + 1 if g % 2 else g - 1) for g in range(1, groups - 1)]
    inner = [(g, g ^ 1) for g in range(groups)]
    upward = [(g, g + 1) for g in range(groups - 1)]
    shift = [
        (z * groups + g, z * groups + g + step)
        for z in range(planes)
        for g in range(groups)
        for step in (1 if z < 2 else -1,)
        if 0 <= g + step < groups
    ]
    own_ext = whiten(True, records)
    got_ext = lax.ppermute(own_ext, "blk", outer)
    own_int = whiten(False, records)
    got_int = lax.ppermute(own_int, "blk", inner)
    rows, _ = lax.optimization_barrier((pairs, own_int))
    own = jnp.concatenate([rows, ring(rows, 1), ring(rows, 2), ring(rows, 3)])
    before = lax.ppermute(own, "blk", upward)

    keep, out1, out2, out3, slots = correlate(own, before, (own_ext, own_int, got_ext, got_int), lag)
    full, send, out1, out2, out3, writes = combine(
        own, before, slots, keep, ring(out2, 2), ring(out1, 1), ring(out3, 3)
    )
    shifted = lax.ppermute(send, ("seg", "blk"), shift)
    outs = finish(pairs.shape[0], writes, full, ring(out2, 2), ring(out1, 1), ring(out3, 3), shifted)
    return tuple(jnp.transpose(out, (0, 2, 1, 3)) for out in outs)


def solution(mesh):
    groups = mesh.shape["blk"]
    planes = mesh.shape["seg"]

    def run(records, pairs):
        body = functools.partial(
            shards,
            groups,
            planes,
            jnp.asarray(lag_rows(records.shape[0])),
        )
        return jax.shard_map(
            body,
            mesh=mesh,
            in_specs=(P("seg", "blk", None), P(("blk", "seg"), None)),
            out_specs=(P(("blk", "seg"), None, None, None), P(("blk", "seg"), None, None, None)),
            check_vma=False,
        )(records, pairs)

    return run
```

```python
import functools

import jax
import jax.numpy as jnp
import ml_dtypes
import numpy as np
from jax import lax
from jax.experimental import pallas as pl
from jax.experimental.pallas import tpu as pltpu
from jax.sharding import PartitionSpec as P

BINS = 256
LENGTH = 512
CHANS = 128
MAXLAG = 32
LAGS = 2 * MAXLAG + 1
REACH = 8
SMOOTH = 32
BAND = 64
GROUP = 8
HALF = GROUP // 2
PLANES = 4
ROWS = HALF * CHANS
SUB = 256
REACHED = 384
SLOTS = 13
SHIFTED = 8
BODY = 64
CHUNK = SLOTS * BODY + 16
SEND2 = SHIFTED * BODY + 16
SEND3 = 4 * BODY + 16
CODES, PLACED, LISTED = 16, 64, 192
PAIRS, MOVES, WRITES, PLAN = 48, 8, 40, 128
TWO = CHUNK
THREE = CHUNK + SEND2
POOL = THREE + 3 * SEND3
MIB = 1024 * 1024
TINY = pl.CostEstimate(flops=1, bytes_accessed=1, transcendentals=0)
BF = jnp.bfloat16
F32 = jnp.float32
SMEM = pl.BlockSpec(memory_space=pltpu.SMEM)
VMEM = pl.BlockSpec(memory_space=pltpu.VMEM)


def split(array):
    high = array.astype(ml_dtypes.bfloat16)
    low = (array - high.astype(np.float32)).astype(ml_dtypes.bfloat16)
    return high, low


def lag_rows(segments):
    freqs = np.concatenate([np.arange(0, BINS, 2), np.arange(1, BINS, 2)])
    shifts = np.arange(-MAXLAG, MAXLAG + 1)
    phase = (shifts[:, None] * freqs[None, :] % LENGTH) * (2.0 * np.pi / LENGTH)
    table = np.concatenate([np.cos(phase), -np.sin(phase)], axis=1) / np.sqrt(segments * BINS)
    table = np.concatenate([table, np.zeros((CHANS - LAGS, LENGTH))], axis=0).T.astype(np.float32)
    return np.concatenate(split(table), axis=1)


def dot(a, b):
    return jnp.dot(a, b, preferred_element_type=F32)


def halves(x):
    high = x.astype(BF)
    return high, (x - high.astype(F32)).astype(BF)


def inverse(y):
    r = pl.reciprocal(y, approx=True)
    return r * (2.0 - y * r)


def make_tables(tab):
    at = lax.broadcasted_iota(jnp.int32, (REACHED, LENGTH), 0)
    col = lax.broadcasted_iota(jnp.int32, (REACHED, LENGTH), 1)
    apart = at - col + jnp.where(col < BINS, 0, LENGTH - REACHED)
    tab[:REACHED] = jnp.where(jnp.abs(apart) <= SMOOTH, 1.0, 0.0).astype(BF)
    half = BINS // 2
    row = lax.broadcasted_iota(jnp.int32, (CHANS, LENGTH), 0)
    col = lax.broadcasted_iota(jnp.int32, (CHANS, LENGTH), 1)
    row = jnp.bitwise_and(row, half - 1) // (BAND // 2)
    col = jnp.bitwise_and(col, half - 1) // (BAND // 2)
    tab[REACHED:LENGTH] = jnp.where(row == col, 0.5 / BAND, 0.0).astype(BF)

    def cosine(step, shift):
        col = lax.broadcasted_iota(jnp.int32, (16, BINS), 1)
        freq = 2 * jnp.bitwise_and(col, half - 1) + jnp.right_shift(col, 7)
        k = lax.broadcasted_iota(jnp.int32, (16, BINS), 0) * freq
        k = jnp.bitwise_and(k * step - shift + BINS, LENGTH - 1) - BINS
        square = jnp.square(k.astype(F32) * (2.0 * np.pi / LENGTH))
        value = jnp.ones_like(square)
        for n in range(20, 0, -2):
            value = 1.0 - value * square * (1.0 / (n * (n - 1)))
        return value

    quarter = LENGTH // 4
    fine_cos, fine_sin = cosine(1, 0), cosine(1, quarter)
    coarse_cos, coarse_sin = cosine(16, 0), cosine(16, quarter)
    for a in range(16):
        c, s = coarse_cos[a : a + 1], coarse_sin[a : a + 1]
        for k, part in enumerate((c * fine_cos - s * fine_sin, -(s * fine_cos) - c * fine_sin)):
            for n, rounded in enumerate(halves(part)):
                rows = pl.ds(LENGTH + n * BINS + 16 * a, 16)
                tab[rows, k * half : (k + 1) * half] = rounded[:, :half]
                tab[rows, BINS + k * half : BINS + (k + 1) * half] = rounded[:, half:]


def whiten_body(outer, records, white, buf, tab, sems):
    segs = records.shape[0]
    core = jnp.bitwise_and(lax.axis_index("blk"), 1)
    begin = pl.multiple_of((core if outer else 1 - core) * ROWS, ROWS)

    def load(k):
        return pltpu.make_async_copy(records.at[k, pl.ds(begin, ROWS)], buf.at[k], sems.at[k])

    for k in range(segs):
        load(k).start()
    at = lax.broadcasted_iota(jnp.int32, (1, LENGTH), 1)
    count = jnp.minimum(at, SMOOTH) + jnp.minimum(LENGTH - 1 - at, SMOOTH) + 1
    share = 1.0 / count.astype(F32)
    make_tables(tab)

    def step(k, carry):
        load(k).wait()
        parts = range(ROWS // SUB)
        xs = [buf[k, pl.ds(n * SUB, SUB), :] for n in parts]
        levels = []
        first = tab[:REACHED, :BINS]
        second = tab[:REACHED, BINS:]
        for x in xs:
            ahi, alo = halves(jnp.abs(x))
            left = jnp.concatenate([ahi[:, :REACHED], alo[:, :REACHED]], axis=1)
            right = jnp.concatenate([ahi[:, LENGTH - REACHED :], alo[:, LENGTH - REACHED :]], axis=1)
            left = dot(left, jnp.concatenate([first, first], axis=0))
            right = dot(right, jnp.concatenate([second, second], axis=0))
            levels.append(jnp.concatenate([left, right], axis=1) * share)
        spectra = []
        products = []
        for at in (0, BINS):
            high = tab[LENGTH : LENGTH + BINS, at : at + BINS]
            products.append(jnp.concatenate([high, high, tab[LENGTH + BINS :, at : at + BINS]], axis=0))
        for x, level in zip(xs, levels):
            normed = x * inverse(level + 1e-06)
            left, right = normed[:, :BINS], normed[:, BINS:]
            pair = []
            for part, product in zip((left + right, left - right), products):
                high, low = halves(part)
                pair.append(dot(jnp.concatenate([high, low, high], axis=1), product))
            spectra.append(pair)
        same = jnp.concatenate([tab[REACHED:LENGTH, :BINS], tab[REACHED:LENGTH, BINS:]], axis=0)
        for n in parts:
            even, odd = spectra[n]
            re = jnp.concatenate([even[:, : BINS // 2], odd[:, : BINS // 2]], axis=1)
            im = jnp.concatenate([even[:, BINS // 2 :], odd[:, BINS // 2 :]], axis=1)
            power = dot((re * re + im * im).astype(BF), same)
            factor = lax.rsqrt(power + 1e-05)
            per = SUB // CHANS
            white[pl.ds(n * per, per), k, :, :BINS] = (re * factor).astype(BF).reshape(per, CHANS, BINS)
            white[pl.ds(n * per, per), k, :, BINS:] = (im * factor).astype(BF).reshape(per, CHANS, BINS)
        return carry

    lax.fori_loop(0, segs, step, 0)


def whiten(outer, records):
    segs = records.shape[0]
    return pl.pallas_call(
        functools.partial(whiten_body, outer),
        in_specs=[pl.BlockSpec(memory_space=pltpu.HBM)],
        out_specs=VMEM,
        out_shape=jax.ShapeDtypeStruct((HALF, segs, CHANS, LENGTH), BF),
        scratch_shapes=[
            pltpu.VMEM((segs, ROWS, LENGTH), F32),
            pltpu.VMEM((2 * LENGTH, LENGTH), BF),
            pltpu.SemaphoreType.DMA((segs,)),
        ],
        compiler_params=pltpu.CompilerParams(vmem_limit_bytes=50 * MIB),
        cost_estimate=TINY,
        name="whiten",
    )(records)


OWN = [(p, d) for p in range(HALF, 12) for d in range(1, REACH + 1) if p < GROUP or p + d < 12]
BEFORE = [(p, d) for p in range(HALF) for d in range(1, REACH + 1) if p + d >= HALF]
UPWARD = (
    ((0, 0), (1, 0), (1, 1), (2, 0), (2, 1), (3, 0), (3, 1)),
    ((2, 2), (3, 2), (3, 3)),
)


def seg_index():
    return lax.axis_index("seg").astype(jnp.int32)


def behind(owner):
    apart = jnp.bitwise_xor(seg_index(), owner)
    return 2 * jnp.bitwise_xor(apart, jnp.right_shift(apart, 1))


def list_pairs(visits, used, table, codes, at, slots, placed):
    s = seg_index()
    n = jnp.int32(0)
    for p, d in visits:
        row = p + HALF if p < HALF else p - HALF
        owner = row // 2
        live = table[behind(owner) + row % 2, d - 1]
        code = p + d * 16 + jnp.bitwise_xor(owner, s) * 256 + used[owner] * 4096
        slots[placed + p * REACH + d - 1] = used[owner]
        used[owner] = used[owner] + live
        if p in (6, 7) and p + d in (12, 13):
            slots[placed + 96 + (p - 6) * 2 + p + d - 12] = used[0]
            code = code + (used[0] + 1) * 65536
            used[0] = used[0] + live
        codes[at + n] = code
        n = n + live
    return n


def list_body(own, listed):
    used = [jnp.int32(0)] * 2 + [jnp.int32(SHIFTED)] * 2
    listed[0] = list_pairs(OWN, used, own, listed, CODES, listed, PLACED)


def list_own(own):
    return pl.pallas_call(
        list_body,
        in_specs=[SMEM],
        out_specs=SMEM,
        out_shape=jax.ShapeDtypeStruct((LISTED,), jnp.int32),
        compiler_params=pltpu.CompilerParams(vmem_limit_bytes=4 * MIB),
        cost_estimate=TINY,
        name="plan",
    )(own)


def plan_body(own, before, listed, slots, plan):
    s = seg_index()
    n = jnp.int32(0)
    for owner in (0, 1):
        for k, (i, j) in enumerate(UPWARD[owner]):
            p, d = HALF + i, GROUP + j - i
            entry = p * REACH + d - 1 if i // 2 == owner else 96 + (i - 2) * 2 + j
            plan[MOVES + n] = listed[PLACED + entry] + k * 4096
            n = n + jnp.where(s == owner, own[behind(i // 2) + i % 2, d - 1], 0)
    for r in range(1, PLANES):
        to = jnp.bitwise_xor(s, r)
        ahead = s < to
        for i in range(2):
            for j in range(2):
                row = 2 * s + i
                p = jnp.where(ahead, row + HALF, jnp.maximum(row - HALF, 0))
                d = 2 * to + j - row + jnp.where(ahead, 0, GROUP)
                live = jnp.where(ahead, own[i, d - 1], jnp.where(s >= 2, before[i, d - 1], 0))
                entry = p * REACH + d - 1
                slot = jnp.where(ahead, listed[PLACED + entry], slots[entry])
                plan[MOVES + n] = slot + r * 256 + (2 * i + j) * 4096
                n = n + live
    plan[0] = n

    def write(n, i, d, base, size, slot):
        plan[WRITES + n] = base + slot * BODY + (base + size * BODY + slot) * 4096 + (i * 8 + d - 1) * 16777216

    n = jnp.int32(0)
    above = jnp.int32(0)
    for i in range(2):
        for d in range(1, REACH + 1):
            row = 2 * s + i
            live = own[i, d - 1]
            shift = (row + d >= GROUP) & (s >= 2)
            slot = jnp.where(shift, above, listed[PLACED + (HALF + row) * REACH + d - 1])
            write(n, i, d, jnp.where(shift, TWO, 0), jnp.where(shift, SHIFTED, SLOTS), slot)
            n = n + live
            above = above + jnp.where(shift, live, 0)
    plan[1] = n
    for j in range(2):
        for d in range(1, REACH + 1):
            low = 2 * s + j - d
            crossing = low < 0
            row = jnp.where(crossing, low + GROUP, low)
            owner = jnp.right_shift(row, 1)
            at = behind(owner) + jnp.bitwise_and(row, 1)
            live = jnp.where(crossing, before[at, d - 1], own[at, d - 1])
            up = crossing & (owner < 2)
            mine = (owner == s) & jnp.logical_not(up)
            k0 = jnp.where(row == 0, 0, 2 * row - 1) + j
            k1 = jnp.where(row == 2, 0, 1) + j
            entry = jnp.maximum((HALF + low) * REACH + d - 1, 0)
            slot = jnp.where(crossing, slots[entry], listed[PLACED + entry])
            slot = jnp.where(mine, slot, 2 * (row - 2 * owner) + j)
            slot = jnp.where(up, jnp.where(s == 0, k0, k1), slot)
            base = jnp.where(mine, 0, THREE + (jnp.bitwise_xor(s, owner) - 1) * SEND3)
            base = jnp.where(up, TWO, base)
            size = jnp.where(mine, SLOTS, jnp.where(up, SHIFTED, 4))
            write(n, j, d, base, size, slot)
            n = n + live
    plan[2] = n


def make_plan(*args):
    return pl.pallas_call(
        plan_body,
        in_specs=[SMEM] * 4,
        out_specs=SMEM,
        out_shape=jax.ShapeDtypeStruct((PLAN,), jnp.int32),
        compiler_params=pltpu.CompilerParams(vmem_limit_bytes=4 * MIB),
        cost_estimate=TINY,
        name="plan",
    )(*args)


def correlate_body(
    listed, before, own_ext, own_int, got_ext, got_int, lag, keep, out1, out2, out3, slots, low, high, stk, pq, codes, last
):
    others = list_pairs(BEFORE, [jnp.int32(0)] * PLANES, before, codes, 0, slots, 0)
    first = listed[0]
    count = first + others
    core = jnp.bitwise_and(lax.axis_index("blk"), 1)
    sources = (
        (own_ext, HALF * (1 + core)),
        (own_int, HALF * (2 - core)),
        (got_ext, 3 * HALF * core),
        (got_int, 3 * HALF * (1 - core)),
    )
    segs = low.shape[0]
    last[0] = -1

    def grab(dest, block):
        for ref, begin in sources:

            @pl.when((block >= begin) & (block < begin + HALF))
            def _(ref=ref, begin=begin):
                dest[...] = ref[block - begin]

    def put(r, n, stack):
        stk[r, pl.ds(pl.multiple_of(n * BODY, BODY), BODY), :] = stack[:BODY]
        stk[r, pl.ds(SLOTS * BODY + n, 1), :] = stack[BODY:LAGS]

    def code_of(n):
        mine = n < first
        return jnp.where(mine, listed[CODES + jnp.where(mine, n, 0)], codes[jnp.where(mine, 0, n - first)])

    def products(n, half):
        code = code_of(n)
        p = jnp.bitwise_and(code, 15)
        d = jnp.bitwise_and(jnp.right_shift(code, 4), 15)

        @pl.when(last[0] != p)
        def _():
            grab(low, p)
            last[0] = p

        grab(high, p + d)
        for chunk in range(CHANS // 16):
            rows = pl.ds(chunk * 16, 16)
            to = pl.ds(half * CHANS + chunk * 16, 16)
            real = jnp.zeros((16, BINS), F32)
            imag = jnp.zeros((16, BINS), F32)
            for k in range(segs):
                are = low[k, rows, :BINS].astype(F32)
                aim = low[k, rows, BINS:].astype(F32)
                bre = high[k, rows, :BINS].astype(F32)
                bim = high[k, rows, BINS:].astype(F32)
                real += are * bre + aim * bim
                imag += are * bim - aim * bre
            rhi, rlo = halves(real)
            ihi, ilo = halves(imag)
            pq[0, to, :BINS] = rhi
            pq[0, to, BINS:] = ihi
            pq[1, to, :BINS] = rlo
            pq[1, to, BINS:] = ilo

    def place(n, stack):
        code = code_of(n)
        put(jnp.bitwise_and(jnp.right_shift(code, 8), 3), jnp.bitwise_and(jnp.right_shift(code, 12), 15), stack)
        second = jnp.right_shift(code, 16)

        @pl.when(second > 0)
        def _():
            put(seg_index(), second - 1, stack)

    def couple(m, carry):
        n = 2 * m
        products(n, 0)

        @pl.when(n + 1 < count)
        def _():
            products(n + 1, 1)

        both = dot(pq[0], lag[...])
        stacks = both[:, :CHANS] + both[:, CHANS:] + dot(pq[1], lag[:, :CHANS])
        place(n, stacks[:CHANS].T)

        @pl.when(n + 1 < count)
        def _():
            place(n + 1, stacks[CHANS:].T)

        return carry

    lax.fori_loop(0, (count + 1) // 2, couple, 0)
    keep[...] = stk[0]
    out1[...] = stk[1].astype(BF)
    out2[...] = stk[2].astype(BF)
    out3[...] = stk[3].astype(BF)


def correlate(listed, before, whites, lag):
    segs = whites[0].shape[1]
    chunk = jax.ShapeDtypeStruct((CHUNK, CHANS), BF)
    return pl.pallas_call(
        correlate_body,
        in_specs=[SMEM] * 2 + [VMEM] * 5,
        out_specs=[VMEM] * 4 + [SMEM],
        out_shape=[
            jax.ShapeDtypeStruct((CHUNK, CHANS), F32),
            chunk,
            chunk,
            chunk,
            jax.ShapeDtypeStruct((128,), jnp.int32),
        ],
        scratch_shapes=[
            pltpu.VMEM((segs, CHANS, LENGTH), BF),
            pltpu.VMEM((segs, CHANS, LENGTH), BF),
            pltpu.VMEM((PLANES, CHUNK, CHANS), F32),
            pltpu.VMEM((2, 2 * CHANS, LENGTH), BF),
            pltpu.SMEM((PAIRS,), jnp.int32),
            pltpu.SMEM((1,), jnp.int32),
        ],
        compiler_params=pltpu.CompilerParams(vmem_limit_bytes=16 * MIB),
        cost_estimate=TINY,
        name="correlate",
    )(listed, before, *whites, lag)


def combine_body(plan, keep, got2, got1, got3, full, send, out1, out2, out3, stage):
    full[...] = (keep[...] + got1[...].astype(F32)) + (got2[...].astype(F32) + got3[...].astype(F32))

    def move(n, carry):
        code = plan[MOVES + n]
        slot = jnp.bitwise_and(code, 255)
        message = jnp.bitwise_and(jnp.right_shift(code, 8), 15)
        k = jnp.right_shift(code, 12)
        size = jnp.where(message == 0, SHIFTED, 4)
        body = pl.ds(pl.multiple_of(slot * BODY, BODY), BODY)
        stage[message, pl.ds(pl.multiple_of(k * BODY, BODY), BODY), :] = full[body, :]
        stage[message, pl.ds(size * BODY + k, 1), :] = full[pl.ds(SLOTS * BODY + slot, 1), :]
        return carry

    lax.fori_loop(0, plan[0], move, 0)

    @pl.when(seg_index() >= 2)
    def _():
        send[: SHIFTED * BODY, :] = full[: SHIFTED * BODY, :].astype(BF)
        send[SHIFTED * BODY :, :] = full[SLOTS * BODY :, :].astype(BF)

    @pl.when(seg_index() < 2)
    def _():
        send[...] = stage[0].astype(BF)

    for r, out in ((1, out1), (2, out2), (3, out3)):
        out[...] = stage[r, :SEND3].astype(BF)


def combine(*args):
    third = jax.ShapeDtypeStruct((SEND3, CHANS), BF)
    return pl.pallas_call(
        combine_body,
        in_specs=[SMEM] + [VMEM] * 4,
        out_specs=[VMEM] * 5,
        out_shape=[
            jax.ShapeDtypeStruct((CHUNK, CHANS), F32),
            jax.ShapeDtypeStruct((SEND2, CHANS), BF),
            third,
            third,
            third,
        ],
        scratch_shapes=[pltpu.VMEM((PLANES, SEND2, CHANS), F32)],
        compiler_params=pltpu.CompilerParams(vmem_limit_bytes=8 * MIB),
        cost_estimate=TINY,
        name="combine",
    )(*args)


def finish_body(plan, full, got2, got1, got3, shifted, fwd, bwd, pool):
    pool[:TWO, :] = full[...]
    pool[TWO:THREE, :] = shifted[...].astype(F32)
    for r, got in ((1, got1), (2, got2), (3, got3)):
        pool[THREE + (r - 1) * SEND3 : THREE + r * SEND3, :] = got[...].astype(F32)
    fwd[...] = jnp.zeros(fwd.shape, F32)
    bwd[...] = jnp.zeros(bwd.shape, F32)

    def write(out, place, n):
        code = plan[WRITES + n]
        body = jnp.bitwise_and(code, 4095)
        i = jnp.right_shift(code, 27)
        at = pl.ds(jnp.bitwise_and(jnp.right_shift(code, 24), 7), 1)
        out[i, place(BODY), at, :] = pool[pl.ds(jnp.bitwise_and(jnp.right_shift(code, 12), 4095), 1), :]
        for m in range(BODY):
            out[i, place(m), at, :] = pool[pl.ds(body + m, 1), :]

    def ahead(n, carry):
        write(fwd, lambda m: m, n)
        return carry

    def behind(n, carry):
        write(bwd, lambda m: BODY - m, n)
        return carry

    lax.fori_loop(0, plan[1], ahead, 0)
    lax.fori_loop(plan[1], plan[2], behind, 0)


def finish(blocks, *args):
    out = jax.ShapeDtypeStruct((blocks, LAGS, REACH, CHANS), F32)
    return pl.pallas_call(
        finish_body,
        in_specs=[SMEM] + [VMEM] * 5,
        out_specs=[VMEM, VMEM],
        out_shape=[out, out],
        scratch_shapes=[pltpu.VMEM((POOL, CHANS), F32)],
        compiler_params=pltpu.CompilerParams(vmem_limit_bytes=8 * MIB),
        cost_estimate=TINY,
        name="finish",
    )(*args)


def shards(groups, planes, lag, records, pairs):
    def across(x, r):
        return lax.ppermute(x, "seg", [(z, z ^ r) for z in range(planes)])

    outer = [(g, g + 1 if g % 2 else g - 1) for g in range(1, groups - 1)]
    inner = [(g, g ^ 1) for g in range(groups)]
    upward = [(g, g + 1) for g in range(groups - 1)]
    shift = [
        (z * groups + g, z * groups + g + step)
        for z in range(planes)
        for g in range(groups)
        for step in (1 if z < 2 else -1,)
        if 0 <= g + step < groups
    ]
    own_ext = whiten(True, records)
    got_ext = lax.ppermute(own_ext, "blk", outer)
    own_int = whiten(False, records)
    got_int = lax.ppermute(own_int, "blk", inner)
    rows, _ = lax.optimization_barrier((pairs, own_int))
    own = jnp.concatenate([rows, across(rows, 1)])
    own = jnp.concatenate([own, across(own, 3)])
    before = lax.ppermute(own, "blk", upward)

    listed = list_own(own)
    keep, out1, out2, out3, slots = correlate(listed, before, (own_ext, own_int, got_ext, got_int), lag)
    plan = make_plan(own, before, listed, slots)
    full, send, out1, out2, out3 = combine(plan, keep, across(out2, 2), across(out1, 1), across(out3, 3))
    shifted = lax.ppermute(send, ("seg", "blk"), shift)
    outs = finish(pairs.shape[0], plan, full, across(out2, 2), across(out1, 1), across(out3, 3), shifted)
    return tuple(jnp.transpose(out, (0, 2, 1, 3)) for out in outs)


def solution(mesh):
    groups = mesh.shape["blk"]
    planes = mesh.shape["seg"]

    def run(records, pairs):
        body = functools.partial(
            shards,
            groups,
            planes,
            jnp.asarray(lag_rows(records.shape[0])),
        )
        return jax.shard_map(
            body,
            mesh=mesh,
            in_specs=(P("seg", "blk", None), P(("blk", "seg"), None)),
            out_specs=(P(("blk", "seg"), None, None, None), P(("blk", "seg"), None, None, None)),
            check_vma=False,
        )(records, pairs)

    return run
```

```python
import functools

import jax
import jax.numpy as jnp
import ml_dtypes
import numpy as np
from jax import lax
from jax.experimental import pallas as pl
from jax.experimental.pallas import tpu as pltpu
from jax.sharding import PartitionSpec as P

BINS = 256
LENGTH = 512
CHANS = 128
MAXLAG = 32
LAGS = 2 * MAXLAG + 1
REACH = 8
SMOOTH = 32
BAND = 64
GROUP = 8
HALF = GROUP // 2
PLANES = 4
ROWS = HALF * CHANS
SUB = 256
REACHED = 384
SLOTS = 13
SHIFTED = 8
BODY = 64
CHUNK = SLOTS * BODY + 16
SEND2 = SHIFTED * BODY + 16
SEND3 = 4 * BODY + 16
PAIRS, MOVES, WRITES, PLAN = 48, 8, 40, 128
TWO = CHUNK
THREE = CHUNK + SEND2
POOL = THREE + 3 * SEND3
MIB = 1024 * 1024
TINY = pl.CostEstimate(flops=1, bytes_accessed=1, transcendentals=0)
BF = jnp.bfloat16
F32 = jnp.float32
SMEM = pl.BlockSpec(memory_space=pltpu.SMEM)
VMEM = pl.BlockSpec(memory_space=pltpu.VMEM)


def split(array):
    high = array.astype(ml_dtypes.bfloat16)
    low = (array - high.astype(np.float32)).astype(ml_dtypes.bfloat16)
    return high, low


def lag_rows(segments):
    freqs = np.concatenate([np.arange(0, BINS, 2), np.arange(1, BINS, 2)])
    shifts = np.arange(-MAXLAG, MAXLAG + 1)
    phase = (shifts[:, None] * freqs[None, :] % LENGTH) * (2.0 * np.pi / LENGTH)
    table = np.concatenate([np.cos(phase), -np.sin(phase)], axis=1) / np.sqrt(segments * BINS)
    table = np.concatenate([table, np.zeros((CHANS - LAGS, LENGTH))], axis=0).T.astype(np.float32)
    return np.concatenate(split(table), axis=1)


def dot(a, b):
    return jnp.dot(a, b, preferred_element_type=F32)


def halves(x):
    high = x.astype(BF)
    return high, (x - high.astype(F32)).astype(BF)


def inverse(y):
    r = pl.reciprocal(y, approx=True)
    return r * (2.0 - y * r)


def make_tables(tab):
    at = lax.broadcasted_iota(jnp.int32, (REACHED, LENGTH), 0)
    col = lax.broadcasted_iota(jnp.int32, (REACHED, LENGTH), 1)
    apart = at - col + jnp.where(col < BINS, 0, LENGTH - REACHED)
    tab[:REACHED] = jnp.where(jnp.abs(apart) <= SMOOTH, 1.0, 0.0).astype(BF)
    half = BINS // 2
    row = lax.broadcasted_iota(jnp.int32, (CHANS, LENGTH), 0)
    col = lax.broadcasted_iota(jnp.int32, (CHANS, LENGTH), 1)
    row = jnp.bitwise_and(row, half - 1) // (BAND // 2)
    col = jnp.bitwise_and(col, half - 1) // (BAND // 2)
    tab[REACHED:LENGTH] = jnp.where(row == col, 0.5 / BAND, 0.0).astype(BF)

    def cosine(step, shift):
        col = lax.broadcasted_iota(jnp.int32, (16, BINS), 1)
        freq = 2 * jnp.bitwise_and(col, half - 1) + jnp.right_shift(col, 7)
        k = lax.broadcasted_iota(jnp.int32, (16, BINS), 0) * freq
        k = jnp.bitwise_and(k * step - shift + BINS, LENGTH - 1) - BINS
        square = jnp.square(k.astype(F32) * (2.0 * np.pi / LENGTH))
        value = jnp.ones_like(square)
        for n in range(20, 0, -2):
            value = 1.0 - value * square * (1.0 / (n * (n - 1)))
        return value

    quarter = LENGTH // 4
    fine_cos, fine_sin = cosine(1, 0), cosine(1, quarter)
    coarse_cos, coarse_sin = cosine(16, 0), cosine(16, quarter)
    for a in range(16):
        c, s = coarse_cos[a : a + 1], coarse_sin[a : a + 1]
        for k, part in enumerate((c * fine_cos - s * fine_sin, -(s * fine_cos) - c * fine_sin)):
            for n, rounded in enumerate(halves(part)):
                rows = pl.ds(LENGTH + n * BINS + 16 * a, 16)
                tab[rows, k * half : (k + 1) * half] = rounded[:, :half]
                tab[rows, BINS + k * half : BINS + (k + 1) * half] = rounded[:, half:]


def whiten_body(outer, records, white, buf, tab, sems):
    segs = records.shape[0]
    core = jnp.bitwise_and(lax.axis_index("blk"), 1)
    begin = pl.multiple_of((core if outer else 1 - core) * ROWS, ROWS)

    def load(k):
        return pltpu.make_async_copy(records.at[k, pl.ds(begin, ROWS)], buf.at[k], sems.at[k])

    for k in range(segs):
        load(k).start()
    at = lax.broadcasted_iota(jnp.int32, (1, LENGTH), 1)
    count = jnp.minimum(at, SMOOTH) + jnp.minimum(LENGTH - 1 - at, SMOOTH) + 1
    share = 1.0 / count.astype(F32)
    make_tables(tab)

    def step(k, carry):
        load(k).wait()
        parts = range(ROWS // SUB)
        xs = [buf[k, pl.ds(n * SUB, SUB), :] for n in parts]
        levels = []
        first = tab[:REACHED, :BINS]
        second = tab[:REACHED, BINS:]
        for x in xs:
            ahi, alo = halves(jnp.abs(x))
            left = jnp.concatenate([ahi[:, :REACHED], alo[:, :REACHED]], axis=1)
            right = jnp.concatenate([ahi[:, LENGTH - REACHED :], alo[:, LENGTH - REACHED :]], axis=1)
            left = dot(left, jnp.concatenate([first, first], axis=0))
            right = dot(right, jnp.concatenate([second, second], axis=0))
            levels.append(jnp.concatenate([left, right], axis=1) * share)
        spectra = []
        products = []
        for at in (0, BINS):
            high = tab[LENGTH : LENGTH + BINS, at : at + BINS]
            products.append(jnp.concatenate([high, high, tab[LENGTH + BINS :, at : at + BINS]], axis=0))
        for x, level in zip(xs, levels):
            normed = x * inverse(level + 1e-06)
            left, right = normed[:, :BINS], normed[:, BINS:]
            pair = []
            for part, product in zip((left + right, left - right), products):
                high, low = halves(part)
                pair.append(dot(jnp.concatenate([high, low, high], axis=1), product))
            spectra.append(pair)
        same = jnp.concatenate([tab[REACHED:LENGTH, :BINS], tab[REACHED:LENGTH, BINS:]], axis=0)
        for n in parts:
            even, odd = spectra[n]
            re = jnp.concatenate([even[:, : BINS // 2], odd[:, : BINS // 2]], axis=1)
            im = jnp.concatenate([even[:, BINS // 2 :], odd[:, BINS // 2 :]], axis=1)
            power = dot((re * re + im * im).astype(BF), same)
            factor = lax.rsqrt(power + 1e-05)
            per = SUB // CHANS
            white[pl.ds(n * per, per), k, :, :BINS] = (re * factor).astype(BF).reshape(per, CHANS, BINS)
            white[pl.ds(n * per, per), k, :, BINS:] = (im * factor).astype(BF).reshape(per, CHANS, BINS)
        return carry

    lax.fori_loop(0, segs, step, 0)


def whiten(outer, records):
    segs = records.shape[0]
    return pl.pallas_call(
        functools.partial(whiten_body, outer),
        in_specs=[pl.BlockSpec(memory_space=pltpu.HBM)],
        out_specs=VMEM,
        out_shape=jax.ShapeDtypeStruct((HALF, segs, CHANS, LENGTH), BF),
        scratch_shapes=[
            pltpu.VMEM((segs, ROWS, LENGTH), F32),
            pltpu.VMEM((2 * LENGTH, LENGTH), BF),
            pltpu.SemaphoreType.DMA((segs,)),
        ],
        compiler_params=pltpu.CompilerParams(vmem_limit_bytes=50 * MIB),
        cost_estimate=TINY,
        name="whiten",
    )(records)


VISITS = [(p, d) for p in range(HALF) for d in range(1, REACH + 1) if p + d >= HALF] + [
    (p, d) for p in range(HALF, 12) for d in range(1, REACH + 1) if p < GROUP or p + d < 12
]
UPWARD = (
    ((0, 0), (1, 0), (1, 1), (2, 0), (2, 1), (3, 0), (3, 1)),
    ((2, 2), (3, 2), (3, 3)),
)


def seg_index():
    return lax.axis_index("seg").astype(jnp.int32)


def behind(owner):
    apart = jnp.bitwise_xor(seg_index(), owner)
    return 2 * jnp.bitwise_xor(apart, jnp.right_shift(apart, 1))


def list_pairs(own, before, codes, slots):
    s = seg_index()
    used = [jnp.int32(0)] * PLANES
    n = jnp.int32(0)
    for p, d in VISITS:
        row = p + HALF if p < HALF else p - HALF
        owner = row // 2
        live = (before if p < HALF else own)[behind(owner) + row % 2, d - 1]
        code = p + d * 16 + jnp.bitwise_xor(owner, s) * 256 + used[owner] * 4096
        slots[p * REACH + d - 1] = used[owner]
        used[owner] = used[owner] + live
        if p in (6, 7) and p + d in (12, 13):
            slots[96 + (p - 6) * 2 + p + d - 12] = used[0]
            code = code + (used[0] + 1) * 65536
            used[0] = used[0] + live
        codes[n] = code
        n = n + live
    return n


def plan_body(own, before, slots, plan):
    s = seg_index()
    n = jnp.int32(0)
    for owner in (0, 1):
        for k, (i, j) in enumerate(UPWARD[owner]):
            p, d = HALF + i, GROUP + j - i
            entry = p * REACH + d - 1 if i // 2 == owner else 96 + (i - 2) * 2 + j
            plan[MOVES + n] = slots[entry] + k * 4096
            n = n + jnp.where(s == owner, own[behind(i // 2) + i % 2, d - 1], 0)
    for r in range(1, PLANES):
        to = jnp.bitwise_xor(s, r)
        ahead = s < to
        for i in range(2):
            for j in range(2):
                row = 2 * s + i
                p = jnp.where(ahead, row + HALF, jnp.maximum(row - HALF, 0))
                d = 2 * to + j - row + jnp.where(ahead, 0, GROUP)
                live = jnp.where(ahead, own[i, d - 1], jnp.where(s >= 2, before[i, d - 1], 0))
                plan[MOVES + n] = slots[p * REACH + d - 1] + r * 256 + (2 * i + j) * 4096
                n = n + live
    plan[0] = n

    def write(n, i, d, base, size, slot):
        plan[WRITES + n] = base + slot * BODY + (base + size * BODY + slot) * 4096 + (i * 8 + d - 1) * 16777216

    n = jnp.int32(0)
    above = jnp.int32(0)
    for i in range(2):
        for d in range(1, REACH + 1):
            row = 2 * s + i
            live = own[i, d - 1]
            shift = (row + d >= GROUP) & (s >= 2)
            slot = jnp.where(shift, above, slots[(HALF + row) * REACH + d - 1])
            write(n, i, d, jnp.where(shift, TWO, 0), jnp.where(shift, SHIFTED, SLOTS), slot)
            n = n + live
            above = above + jnp.where(shift, live, 0)
    plan[1] = n
    for j in range(2):
        for d in range(1, REACH + 1):
            low = 2 * s + j - d
            crossing = low < 0
            row = jnp.where(crossing, low + GROUP, low)
            owner = jnp.right_shift(row, 1)
            at = behind(owner) + jnp.bitwise_and(row, 1)
            live = jnp.where(crossing, before[at, d - 1], own[at, d - 1])
            up = crossing & (owner < 2)
            mine = (owner == s) & jnp.logical_not(up)
            k0 = jnp.where(row == 0, 0, 2 * row - 1) + j
            k1 = jnp.where(row == 2, 0, 1) + j
            entry = jnp.maximum((HALF + low) * REACH + d - 1, 0)
            slot = jnp.where(mine, slots[entry], 2 * (row - 2 * owner) + j)
            slot = jnp.where(up, jnp.where(s == 0, k0, k1), slot)
            base = jnp.where(mine, 0, THREE + (jnp.bitwise_xor(s, owner) - 1) * SEND3)
            base = jnp.where(up, TWO, base)
            size = jnp.where(mine, SLOTS, jnp.where(up, SHIFTED, 4))
            write(n, j, d, base, size, slot)
            n = n + live
    plan[2] = n


def make_plan(*args):
    return pl.pallas_call(
        plan_body,
        in_specs=[SMEM] * 3,
        out_specs=SMEM,
        out_shape=jax.ShapeDtypeStruct((PLAN,), jnp.int32),
        compiler_params=pltpu.CompilerParams(vmem_limit_bytes=4 * MIB),
        cost_estimate=TINY,
        name="plan",
    )(*args)


def correlate_body(
    own, before, own_ext, own_int, got_ext, got_int, lag, keep, out1, out2, out3, slots, low, tails, pq, codes, last
):
    count = list_pairs(own, before, codes, slots)
    core = jnp.bitwise_and(lax.axis_index("blk"), 1)
    sources = (
        (own_ext, HALF * (1 + core)),
        (own_int, HALF * (2 - core)),
        (got_ext, 3 * HALF * core),
        (got_int, 3 * HALF * (1 - core)),
    )
    segs = low.shape[0]
    last[0] = -1

    def grab(dest, block):
        for ref, begin in sources:

            @pl.when((block >= begin) & (block < begin + HALF))
            def _(ref=ref, begin=begin):
                dest[...] = ref[block - begin]

    def put(r, n, stack):
        tails[r, pl.ds(n, 1), :] = stack[BODY:LAGS]
        body = pl.ds(pl.multiple_of(n * BODY, BODY), BODY)

        @pl.when(r == 0)
        def _():
            keep[body, :] = stack[:BODY]

        for k, out in ((1, out1), (2, out2), (3, out3)):

            @pl.when(r == k)
            def _(out=out):
                out[body, :] = stack[:BODY].astype(BF)

    def products(high, block):
        for chunk in range(CHANS // 16):
            rows = pl.ds(chunk * 16, 16)
            real = jnp.zeros((16, BINS), F32)
            imag = jnp.zeros((16, BINS), F32)
            for k in range(segs):
                are = low[k, rows, :BINS].astype(F32)
                aim = low[k, rows, BINS:].astype(F32)
                bre = high[block, k, rows, :BINS].astype(F32)
                bim = high[block, k, rows, BINS:].astype(F32)
                real += are * bre + aim * bim
                imag += are * bim - aim * bre
            rhi, rlo = halves(real)
            ihi, ilo = halves(imag)
            pq[0, rows, :BINS] = rhi
            pq[0, rows, BINS:] = ihi
            pq[1, rows, :BINS] = rlo
            pq[1, rows, BINS:] = ilo

    def pair(n, carry):
        code = codes[n]
        p = jnp.bitwise_and(code, 15)
        d = jnp.bitwise_and(jnp.right_shift(code, 4), 15)

        @pl.when(last[0] != p)
        def _():
            grab(low, p)
            last[0] = p

        for ref, begin in sources:

            @pl.when((p + d >= begin) & (p + d < begin + HALF))
            def _(ref=ref, begin=begin):
                products(ref, p + d - begin)

        both = dot(pq[0], lag[...])
        stack = (both[:, :CHANS] + both[:, CHANS:] + dot(pq[1], lag[:, :CHANS])).T
        put(jnp.bitwise_and(jnp.right_shift(code, 8), 3), jnp.bitwise_and(jnp.right_shift(code, 12), 15), stack)
        second = jnp.right_shift(code, 16)

        @pl.when(second > 0)
        def _():
            put(seg_index(), second - 1, stack)

        return carry

    lax.fori_loop(0, count, pair, 0)
    keep[SLOTS * BODY :, :] = tails[0]
    for k, out in ((1, out1), (2, out2), (3, out3)):
        out[SLOTS * BODY :, :] = tails[k].astype(BF)


def correlate(own, before, whites, lag):
    segs = whites[0].shape[1]
    chunk = jax.ShapeDtypeStruct((CHUNK, CHANS), BF)
    return pl.pallas_call(
        correlate_body,
        in_specs=[SMEM] * 2 + [VMEM] * 5,
        out_specs=[VMEM] * 4 + [SMEM],
        out_shape=[
            jax.ShapeDtypeStruct((CHUNK, CHANS), F32),
            chunk,
            chunk,
            chunk,
            jax.ShapeDtypeStruct((128,), jnp.int32),
        ],
        scratch_shapes=[
            pltpu.VMEM((segs, CHANS, LENGTH), BF),
            pltpu.VMEM((PLANES, 16, CHANS), F32),
            pltpu.VMEM((2, CHANS, LENGTH), BF),
            pltpu.SMEM((PAIRS,), jnp.int32),
            pltpu.SMEM((1,), jnp.int32),
        ],
        compiler_params=pltpu.CompilerParams(vmem_limit_bytes=16 * MIB),
        cost_estimate=TINY,
        name="correlate",
    )(own, before, *whites, lag)


def combine_body(plan, keep, got2, got1, got3, full, send, out1, out2, out3, stage):
    full[...] = (keep[...] + got1[...].astype(F32)) + (got2[...].astype(F32) + got3[...].astype(F32))

    def move(n, carry):
        code = plan[MOVES + n]
        slot = jnp.bitwise_and(code, 255)
        message = jnp.bitwise_and(jnp.right_shift(code, 8), 15)
        k = jnp.right_shift(code, 12)
        size = jnp.where(message == 0, SHIFTED, 4)
        body = pl.ds(pl.multiple_of(slot * BODY, BODY), BODY)
        stage[message, pl.ds(pl.multiple_of(k * BODY, BODY), BODY), :] = full[body, :]
        stage[message, pl.ds(size * BODY + k, 1), :] = full[pl.ds(SLOTS * BODY + slot, 1), :]
        return carry

    lax.fori_loop(0, plan[0], move, 0)

    @pl.when(seg_index() >= 2)
    def _():
        send[: SHIFTED * BODY, :] = full[: SHIFTED * BODY, :].astype(BF)
        send[SHIFTED * BODY :, :] = full[SLOTS * BODY :, :].astype(BF)

    @pl.when(seg_index() < 2)
    def _():
        send[...] = stage[0].astype(BF)

    for r, out in ((1, out1), (2, out2), (3, out3)):
        out[...] = stage[r, :SEND3].astype(BF)


def combine(*args):
    third = jax.ShapeDtypeStruct((SEND3, CHANS), BF)
    return pl.pallas_call(
        combine_body,
        in_specs=[SMEM] + [VMEM] * 4,
        out_specs=[VMEM] * 5,
        out_shape=[
            jax.ShapeDtypeStruct((CHUNK, CHANS), F32),
            jax.ShapeDtypeStruct((SEND2, CHANS), BF),
            third,
            third,
            third,
        ],
        scratch_shapes=[pltpu.VMEM((PLANES, SEND2, CHANS), F32)],
        compiler_params=pltpu.CompilerParams(vmem_limit_bytes=8 * MIB),
        cost_estimate=TINY,
        name="combine",
    )(*args)


def finish_body(plan, full, got2, got1, got3, shifted, fwd, bwd, pool):
    pool[:TWO, :] = full[...]
    pool[TWO:THREE, :] = shifted[...].astype(F32)
    for r, got in ((1, got1), (2, got2), (3, got3)):
        pool[THREE + (r - 1) * SEND3 : THREE + r * SEND3, :] = got[...].astype(F32)
    fwd[...] = jnp.zeros(fwd.shape, F32)
    bwd[...] = jnp.zeros(bwd.shape, F32)

    def write(out, place, n):
        code = plan[WRITES + n]
        body = jnp.bitwise_and(code, 4095)
        i = jnp.right_shift(code, 27)
        at = pl.ds(jnp.bitwise_and(jnp.right_shift(code, 24), 7), 1)
        out[i, place(BODY), at, :] = pool[pl.ds(jnp.bitwise_and(jnp.right_shift(code, 12), 4095), 1), :]
        for m in range(BODY):
            out[i, place(m), at, :] = pool[pl.ds(body + m, 1), :]

    def ahead(n, carry):
        write(fwd, lambda m: m, n)
        return carry

    def behind(n, carry):
        write(bwd, lambda m: BODY - m, n)
        return carry

    lax.fori_loop(0, plan[1], ahead, 0)
    lax.fori_loop(plan[1], plan[2], behind, 0)


def finish(blocks, *args):
    out = jax.ShapeDtypeStruct((blocks, LAGS, REACH, CHANS), F32)
    return pl.pallas_call(
        finish_body,
        in_specs=[SMEM] + [VMEM] * 5,
        out_specs=[VMEM, VMEM],
        out_shape=[out, out],
        scratch_shapes=[pltpu.VMEM((POOL, CHANS), F32)],
        compiler_params=pltpu.CompilerParams(vmem_limit_bytes=8 * MIB),
        cost_estimate=TINY,
        name="finish",
    )(*args)


def shards(groups, planes, lag, records, pairs):
    def across(x, r):
        return lax.ppermute(x, "seg", [(z, z ^ r) for z in range(planes)])

    outer = [(g, g + 1 if g % 2 else g - 1) for g in range(1, groups - 1)]
    inner = [(g, g ^ 1) for g in range(groups)]
    upward = [(g, g + 1) for g in range(groups - 1)]
    shift = [
        (z * groups + g, z * groups + g + step)
        for z in range(planes)
        for g in range(groups)
        for step in (1 if z < 2 else -1,)
        if 0 <= g + step < groups
    ]
    own_ext = whiten(True, records)
    got_ext = lax.ppermute(own_ext, "blk", outer)
    own_int = whiten(False, records)
    got_int = lax.ppermute(own_int, "blk", inner)
    rows, _ = lax.optimization_barrier((pairs, own_int))
    own = jnp.concatenate([rows, across(rows, 1)])
    own = jnp.concatenate([own, across(own, 3)])
    before = lax.ppermute(own, "blk", upward)

    keep, out1, out2, out3, slots = correlate(own, before, (own_ext, own_int, got_ext, got_int), lag)
    plan = make_plan(own, before, slots)
    full, send, out1, out2, out3 = combine(plan, keep, across(out2, 2), across(out1, 1), across(out3, 3))
    shifted = lax.ppermute(send, ("seg", "blk"), shift)
    outs = finish(pairs.shape[0], plan, full, across(out2, 2), across(out1, 1), across(out3, 3), shifted)
    return tuple(jnp.transpose(out, (0, 2, 1, 3)) for out in outs)


def solution(mesh):
    groups = mesh.shape["blk"]
    planes = mesh.shape["seg"]

    def run(records, pairs):
        body = functools.partial(
            shards,
            groups,
            planes,
            jnp.asarray(lag_rows(records.shape[0])),
        )
        return jax.shard_map(
            body,
            mesh=mesh,
            in_specs=(P("seg", "blk", None), P(("blk", "seg"), None)),
            out_specs=(P(("blk", "seg"), None, None, None), P(("blk", "seg"), None, None, None)),
            check_vma=False,
        )(records, pairs)

    return run
```

```python
import functools

import jax
import jax.numpy as jnp
import ml_dtypes
import numpy as np
from jax import lax
from jax.experimental import pallas as pl
from jax.experimental.pallas import tpu as pltpu
from jax.sharding import PartitionSpec as P

BINS = 256
LENGTH = 512
CHANS = 128
MAXLAG = 32
LAGS = 2 * MAXLAG + 1
REACH = 8
SMOOTH = 32
BAND = 64
GROUP = 8
HALF = GROUP // 2
PLANES = 4
ROWS = HALF * CHANS
SUB = ROWS
REACHED = 384
SLOTS = 13
SHIFTED = 8
BODY = 64
CHUNK = SLOTS * BODY + 16
SEND2 = SHIFTED * BODY + 16
SEND3 = 4 * BODY + 16
PAIRS, MOVES, WRITES, PLAN = 48, 8, 40, 128
TWO = CHUNK
THREE = CHUNK + SEND2
POOL = THREE + 3 * SEND3
MIB = 1024 * 1024
TINY = pl.CostEstimate(flops=1, bytes_accessed=1, transcendentals=0)
BF = jnp.bfloat16
F32 = jnp.float32
SMEM = pl.BlockSpec(memory_space=pltpu.SMEM)
VMEM = pl.BlockSpec(memory_space=pltpu.VMEM)


def split(array):
    high = array.astype(ml_dtypes.bfloat16)
    low = (array - high.astype(np.float32)).astype(ml_dtypes.bfloat16)
    return high, low


def lag_rows(segments):
    freqs = np.concatenate([np.arange(0, BINS, 2), np.arange(1, BINS, 2)])
    shifts = np.arange(-MAXLAG, MAXLAG + 1)
    phase = (shifts[:, None] * freqs[None, :] % LENGTH) * (2.0 * np.pi / LENGTH)
    table = np.concatenate([np.cos(phase), -np.sin(phase)], axis=1) / np.sqrt(segments * BINS)
    table = np.concatenate([table, np.zeros((CHANS - LAGS, LENGTH))], axis=0).T.astype(np.float32)
    return np.concatenate(split(table), axis=1)


def dot(a, b):
    return jnp.dot(a, b, preferred_element_type=F32)


def halves(x):
    high = x.astype(BF)
    return high, (x - high.astype(F32)).astype(BF)


def make_tables(tab):
    at = lax.broadcasted_iota(jnp.int32, (REACHED, LENGTH), 0)
    col = lax.broadcasted_iota(jnp.int32, (REACHED, LENGTH), 1)
    apart = at - col + jnp.where(col < BINS, 0, LENGTH - REACHED)
    tab[:REACHED] = jnp.where(jnp.abs(apart) <= SMOOTH, 1.0, 0.0).astype(BF)
    half = BINS // 2
    row = lax.broadcasted_iota(jnp.int32, (CHANS, LENGTH), 0)
    col = lax.broadcasted_iota(jnp.int32, (CHANS, LENGTH), 1)
    row = jnp.bitwise_and(row, half - 1) // (BAND // 2)
    col = jnp.bitwise_and(col, half - 1) // (BAND // 2)
    tab[REACHED:LENGTH] = jnp.where(row == col, 0.5 / BAND, 0.0).astype(BF)

    def cosine(step, shift):
        col = lax.broadcasted_iota(jnp.int32, (16, BINS), 1)
        freq = 2 * jnp.bitwise_and(col, half - 1) + jnp.right_shift(col, 7)
        k = lax.broadcasted_iota(jnp.int32, (16, BINS), 0) * freq
        k = jnp.bitwise_and(k * step - shift + BINS, LENGTH - 1) - BINS
        square = jnp.square(k.astype(F32) * (2.0 * np.pi / LENGTH))
        value = jnp.ones_like(square)
        for n in range(20, 0, -2):
            value = 1.0 - value * square * (1.0 / (n * (n - 1)))
        return value

    quarter = LENGTH // 4
    fine_cos, fine_sin = cosine(1, 0), cosine(1, quarter)
    coarse_cos, coarse_sin = cosine(16, 0), cosine(16, quarter)
    for a in range(16):
        c, s = coarse_cos[a : a + 1], coarse_sin[a : a + 1]
        for k, part in enumerate((c * fine_cos - s * fine_sin, -(s * fine_cos) - c * fine_sin)):
            for n, rounded in enumerate(halves(part)):
                rows = pl.ds(LENGTH + n * BINS + 16 * a, 16)
                tab[rows, k * half : (k + 1) * half] = rounded[:, :half]
                tab[rows, BINS + k * half : BINS + (k + 1) * half] = rounded[:, half:]


def whiten_body(outer, records, white, buf, tab, sems):
    segs = records.shape[0]
    core = jnp.bitwise_and(lax.axis_index("blk"), 1)
    begin = pl.multiple_of((core if outer else 1 - core) * ROWS, ROWS)

    def load(k):
        return pltpu.make_async_copy(records.at[k, pl.ds(begin, ROWS)], buf.at[k], sems.at[k])

    for k in range(segs):
        load(k).start()
    at = lax.broadcasted_iota(jnp.int32, (1, LENGTH), 1)
    count = jnp.minimum(at, SMOOTH) + jnp.minimum(LENGTH - 1 - at, SMOOTH) + 1
    share = 1.0 / count.astype(F32)
    make_tables(tab)

    def step(k, carry):
        load(k).wait()
        parts = range(ROWS // SUB)
        xs = [buf[k, pl.ds(n * SUB, SUB), :] for n in parts]
        levels = []
        first = tab[:REACHED, :BINS]
        second = tab[:REACHED, BINS:]
        for x in xs:
            ahi, alo = halves(jnp.abs(x))
            left = jnp.concatenate([ahi[:, :REACHED], alo[:, :REACHED]], axis=1)
            right = jnp.concatenate([ahi[:, LENGTH - REACHED :], alo[:, LENGTH - REACHED :]], axis=1)
            left = dot(left, jnp.concatenate([first, first], axis=0))
            right = dot(right, jnp.concatenate([second, second], axis=0))
            levels.append(jnp.concatenate([left, right], axis=1) * share)
        spectra = []
        products = []
        for at in (0, BINS):
            high = tab[LENGTH : LENGTH + BINS, at : at + BINS]
            products.append(jnp.concatenate([high, high, tab[LENGTH + BINS :, at : at + BINS]], axis=0))
        for x, level in zip(xs, levels):
            normed = x * pl.reciprocal(level + 1e-06, approx=True)
            left, right = normed[:, :BINS], normed[:, BINS:]
            pair = []
            for part, product in zip((left + right, left - right), products):
                high, low = halves(part)
                pair.append(dot(jnp.concatenate([high, low, high], axis=1), product))
            spectra.append(pair)
        same = jnp.concatenate([tab[REACHED:LENGTH, :BINS], tab[REACHED:LENGTH, BINS:]], axis=0)
        for n in parts:
            even, odd = spectra[n]
            re = jnp.concatenate([even[:, : BINS // 2], odd[:, : BINS // 2]], axis=1)
            im = jnp.concatenate([even[:, BINS // 2 :], odd[:, BINS // 2 :]], axis=1)
            power = dot((re * re + im * im).astype(BF), same)
            factor = lax.rsqrt(power + 1e-05)
            per = SUB // CHANS
            white[pl.ds(n * per, per), k, :, :BINS] = (re * factor).astype(BF).reshape(per, CHANS, BINS)
            white[pl.ds(n * per, per), k, :, BINS:] = (im * factor).astype(BF).reshape(per, CHANS, BINS)
        return carry

    lax.fori_loop(0, segs, step, 0)


def whiten(outer, records):
    segs = records.shape[0]
    return pl.pallas_call(
        functools.partial(whiten_body, outer),
        in_specs=[pl.BlockSpec(memory_space=pltpu.HBM)],
        out_specs=VMEM,
        out_shape=jax.ShapeDtypeStruct((HALF, segs, CHANS, LENGTH), BF),
        scratch_shapes=[
            pltpu.VMEM((segs, ROWS, LENGTH), F32),
            pltpu.VMEM((2 * LENGTH, LENGTH), BF),
            pltpu.SemaphoreType.DMA((segs,)),
        ],
        compiler_params=pltpu.CompilerParams(vmem_limit_bytes=50 * MIB),
        cost_estimate=TINY,
        name="whiten",
    )(records)


VISITS = [(p, d) for p in range(HALF) for d in range(1, REACH + 1) if p + d >= HALF] + [
    (p, d) for p in range(HALF, 12) for d in range(1, REACH + 1) if p < GROUP or p + d < 12
]
UPWARD = (
    ((0, 0), (1, 0), (1, 1), (2, 0), (2, 1), (3, 0), (3, 1)),
    ((2, 2), (3, 2), (3, 3)),
)


def seg_index():
    return lax.axis_index("seg").astype(jnp.int32)


def behind(owner):
    apart = jnp.bitwise_xor(seg_index(), owner)
    return 2 * jnp.bitwise_xor(apart, jnp.right_shift(apart, 1))


def list_pairs(own, before, codes, slots):
    s = seg_index()
    used = [jnp.int32(0)] * PLANES
    n = jnp.int32(0)
    for p, d in VISITS:
        row = p + HALF if p < HALF else p - HALF
        owner = row // 2
        live = (before if p < HALF else own)[behind(owner) + row % 2, d - 1]
        code = p + d * 16 + jnp.bitwise_xor(owner, s) * 256 + used[owner] * 4096
        slots[p * REACH + d - 1] = used[owner]
        used[owner] = used[owner] + live
        if p in (6, 7) and p + d in (12, 13):
            slots[96 + (p - 6) * 2 + p + d - 12] = used[0]
            code = code + (used[0] + 1) * 65536
            used[0] = used[0] + live
        codes[n] = code
        n = n + live
    return n


def plan_body(own, before, slots, plan):
    s = seg_index()
    n = jnp.int32(0)
    for owner in (0, 1):
        for k, (i, j) in enumerate(UPWARD[owner]):
            p, d = HALF + i, GROUP + j - i
            entry = p * REACH + d - 1 if i // 2 == owner else 96 + (i - 2) * 2 + j
            plan[MOVES + n] = slots[entry] + k * 4096
            n = n + jnp.where(s == owner, own[behind(i // 2) + i % 2, d - 1], 0)
    for r in range(1, PLANES):
        to = jnp.bitwise_xor(s, r)
        ahead = s < to
        for i in range(2):
            for j in range(2):
                row = 2 * s + i
                p = jnp.where(ahead, row + HALF, jnp.maximum(row - HALF, 0))
                d = 2 * to + j - row + jnp.where(ahead, 0, GROUP)
                live = jnp.where(ahead, own[i, d - 1], jnp.where(s >= 2, before[i, d - 1], 0))
                plan[MOVES + n] = slots[p * REACH + d - 1] + r * 256 + (2 * i + j) * 4096
                n = n + live
    plan[0] = n

    def write(n, i, d, base, size, slot):
        plan[WRITES + n] = base + slot * BODY + (base + size * BODY + slot) * 4096 + (i * 8 + d - 1) * 16777216

    n = jnp.int32(0)
    above = jnp.int32(0)
    for i in range(2):
        for d in range(1, REACH + 1):
            row = 2 * s + i
            live = own[i, d - 1]
            shift = (row + d >= GROUP) & (s >= 2)
            slot = jnp.where(shift, above, slots[(HALF + row) * REACH + d - 1])
            write(n, i, d, jnp.where(shift, TWO, 0), jnp.where(shift, SHIFTED, SLOTS), slot)
            n = n + live
            above = above + jnp.where(shift, live, 0)
    plan[1] = n
    for j in range(2):
        for d in range(1, REACH + 1):
            low = 2 * s + j - d
            crossing = low < 0
            row = jnp.where(crossing, low + GROUP, low)
            owner = jnp.right_shift(row, 1)
            at = behind(owner) + jnp.bitwise_and(row, 1)
            live = jnp.where(crossing, before[at, d - 1], own[at, d - 1])
            up = crossing & (owner < 2)
            mine = (owner == s) & jnp.logical_not(up)
            k0 = jnp.where(row == 0, 0, 2 * row - 1) + j
            k1 = jnp.where(row == 2, 0, 1) + j
            entry = jnp.maximum((HALF + low) * REACH + d - 1, 0)
            slot = jnp.where(mine, slots[entry], 2 * (row - 2 * owner) + j)
            slot = jnp.where(up, jnp.where(s == 0, k0, k1), slot)
            base = jnp.where(mine, 0, THREE + (jnp.bitwise_xor(s, owner) - 1) * SEND3)
            base = jnp.where(up, TWO, base)
            size = jnp.where(mine, SLOTS, jnp.where(up, SHIFTED, 4))
            write(n, j, d, base, size, slot)
            n = n + live
    plan[2] = n


def make_plan(*args):
    return pl.pallas_call(
        plan_body,
        in_specs=[SMEM] * 3,
        out_specs=SMEM,
        out_shape=jax.ShapeDtypeStruct((PLAN,), jnp.int32),
        compiler_params=pltpu.CompilerParams(vmem_limit_bytes=4 * MIB),
        cost_estimate=TINY,
        name="plan",
    )(*args)


def correlate_body(
    own, before, own_ext, own_int, got_ext, got_int, lag, keep, out1, out2, out3, slots, low, high, stk, pq, codes, last
):
    count = list_pairs(own, before, codes, slots)
    core = jnp.bitwise_and(lax.axis_index("blk"), 1)
    sources = (
        (own_ext, HALF * (1 + core)),
        (own_int, HALF * (2 - core)),
        (got_ext, 3 * HALF * core),
        (got_int, 3 * HALF * (1 - core)),
    )
    segs = low.shape[0]
    last[0] = -1

    def grab(dest, block):
        for ref, begin in sources:

            @pl.when((block >= begin) & (block < begin + HALF))
            def _(ref=ref, begin=begin):
                dest[...] = ref[block - begin]

    def put(r, n, stack):
        stk[r, pl.ds(pl.multiple_of(n * BODY, BODY), BODY), :] = stack[:BODY]
        stk[r, pl.ds(SLOTS * BODY + n, 1), :] = stack[BODY:LAGS]

    def pair(n, carry):
        code = codes[n]
        p = jnp.bitwise_and(code, 15)
        d = jnp.bitwise_and(jnp.right_shift(code, 4), 15)

        @pl.when(last[0] != p)
        def _():
            grab(low, p)
            last[0] = p

        grab(high, p + d)
        for chunk in range(CHANS // 16):
            rows = pl.ds(chunk * 16, 16)
            real = jnp.zeros((16, BINS), F32)
            imag = jnp.zeros((16, BINS), F32)
            for k in range(segs):
                are = low[k, rows, :BINS].astype(F32)
                aim = low[k, rows, BINS:].astype(F32)
                bre = high[k, rows, :BINS].astype(F32)
                bim = high[k, rows, BINS:].astype(F32)
                real += are * bre + aim * bim
                imag += are * bim - aim * bre
            rhi, rlo = halves(real)
            ihi, ilo = halves(imag)
            pq[0, rows, :BINS] = rhi
            pq[0, rows, BINS:] = ihi
            pq[1, rows, :BINS] = rlo
            pq[1, rows, BINS:] = ilo
        both = dot(pq[0], lag[...])
        stack = (both[:, :CHANS] + both[:, CHANS:] + dot(pq[1], lag[:, :CHANS])).T
        put(jnp.bitwise_and(jnp.right_shift(code, 8), 3), jnp.bitwise_and(jnp.right_shift(code, 12), 15), stack)
        second = jnp.right_shift(code, 16)

        @pl.when(second > 0)
        def _():
            put(seg_index(), second - 1, stack)

        return carry

    lax.fori_loop(0, count, pair, 0)
    keep[...] = stk[0]
    out1[...] = stk[1].astype(BF)
    out2[...] = stk[2].astype(BF)
    out3[...] = stk[3].astype(BF)


def correlate(own, before, whites, lag):
    segs = whites[0].shape[1]
    chunk = jax.ShapeDtypeStruct((CHUNK, CHANS), BF)
    return pl.pallas_call(
        correlate_body,
        in_specs=[SMEM] * 2 + [VMEM] * 5,
        out_specs=[VMEM] * 4 + [SMEM],
        out_shape=[
            jax.ShapeDtypeStruct((CHUNK, CHANS), F32),
            chunk,
            chunk,
            chunk,
            jax.ShapeDtypeStruct((128,), jnp.int32),
        ],
        scratch_shapes=[
            pltpu.VMEM((segs, CHANS, LENGTH), BF),
            pltpu.VMEM((segs, CHANS, LENGTH), BF),
            pltpu.VMEM((PLANES, CHUNK, CHANS), F32),
            pltpu.VMEM((2, CHANS, LENGTH), BF),
            pltpu.SMEM((PAIRS,), jnp.int32),
            pltpu.SMEM((1,), jnp.int32),
        ],
        compiler_params=pltpu.CompilerParams(vmem_limit_bytes=16 * MIB),
        cost_estimate=TINY,
        name="correlate",
    )(own, before, *whites, lag)


def combine_body(plan, keep, got2, got1, got3, full, send, out1, out2, out3, stage):
    full[...] = (keep[...] + got1[...].astype(F32)) + (got2[...].astype(F32) + got3[...].astype(F32))

    def move(n, carry):
        code = plan[MOVES + n]
        slot = jnp.bitwise_and(code, 255)
        message = jnp.bitwise_and(jnp.right_shift(code, 8), 15)
        k = jnp.right_shift(code, 12)
        size = jnp.where(message == 0, SHIFTED, 4)
        body = pl.ds(pl.multiple_of(slot * BODY, BODY), BODY)
        stage[message, pl.ds(pl.multiple_of(k * BODY, BODY), BODY), :] = full[body, :]
        stage[message, pl.ds(size * BODY + k, 1), :] = full[pl.ds(SLOTS * BODY + slot, 1), :]
        return carry

    lax.fori_loop(0, plan[0], move, 0)

    @pl.when(seg_index() >= 2)
    def _():
        send[: SHIFTED * BODY, :] = full[: SHIFTED * BODY, :].astype(BF)
        send[SHIFTED * BODY :, :] = full[SLOTS * BODY :, :].astype(BF)

    @pl.when(seg_index() < 2)
    def _():
        send[...] = stage[0].astype(BF)

    for r, out in ((1, out1), (2, out2), (3, out3)):
        out[...] = stage[r, :SEND3].astype(BF)


def combine(*args):
    third = jax.ShapeDtypeStruct((SEND3, CHANS), BF)
    return pl.pallas_call(
        combine_body,
        in_specs=[SMEM] + [VMEM] * 4,
        out_specs=[VMEM] * 5,
        out_shape=[
            jax.ShapeDtypeStruct((CHUNK, CHANS), F32),
            jax.ShapeDtypeStruct((SEND2, CHANS), BF),
            third,
            third,
            third,
        ],
        scratch_shapes=[pltpu.VMEM((PLANES, SEND2, CHANS), F32)],
        compiler_params=pltpu.CompilerParams(vmem_limit_bytes=8 * MIB),
        cost_estimate=TINY,
        name="combine",
    )(*args)


def finish_body(plan, full, got2, got1, got3, shifted, fwd, bwd, pool):
    pool[:TWO, :] = full[...]
    pool[TWO:THREE, :] = shifted[...].astype(F32)
    for r, got in ((1, got1), (2, got2), (3, got3)):
        pool[THREE + (r - 1) * SEND3 : THREE + r * SEND3, :] = got[...].astype(F32)
    fwd[...] = jnp.zeros(fwd.shape, F32)
    bwd[...] = jnp.zeros(bwd.shape, F32)

    def write(out, place, n):
        code = plan[WRITES + n]
        body = jnp.bitwise_and(code, 4095)
        i = jnp.right_shift(code, 27)
        at = pl.ds(jnp.bitwise_and(jnp.right_shift(code, 24), 7), 1)
        out[i, place(BODY), at, :] = pool[pl.ds(jnp.bitwise_and(jnp.right_shift(code, 12), 4095), 1), :]
        for m in range(BODY):
            out[i, place(m), at, :] = pool[pl.ds(body + m, 1), :]

    def ahead(n, carry):
        write(fwd, lambda m: m, n)
        return carry

    def behind(n, carry):
        write(bwd, lambda m: BODY - m, n)
        return carry

    lax.fori_loop(0, plan[1], ahead, 0)
    lax.fori_loop(plan[1], plan[2], behind, 0)


def finish(blocks, *args):
    out = jax.ShapeDtypeStruct((blocks, LAGS, REACH, CHANS), F32)
    return pl.pallas_call(
        finish_body,
        in_specs=[SMEM] + [VMEM] * 5,
        out_specs=[VMEM, VMEM],
        out_shape=[out, out],
        scratch_shapes=[pltpu.VMEM((POOL, CHANS), F32)],
        compiler_params=pltpu.CompilerParams(vmem_limit_bytes=8 * MIB),
        cost_estimate=TINY,
        name="finish",
    )(*args)


def shards(groups, planes, lag, records, pairs):
    def across(x, r):
        return lax.ppermute(x, "seg", [(z, z ^ r) for z in range(planes)])

    outer = [(g, g + 1 if g % 2 else g - 1) for g in range(1, groups - 1)]
    inner = [(g, g ^ 1) for g in range(groups)]
    upward = [(g, g + 1) for g in range(groups - 1)]
    shift = [
        (z * groups + g, z * groups + g + step)
        for z in range(planes)
        for g in range(groups)
        for step in (1 if z < 2 else -1,)
        if 0 <= g + step < groups
    ]
    own_ext = whiten(True, records)
    got_ext = lax.ppermute(own_ext, "blk", outer)
    own_int = whiten(False, records)
    got_int = lax.ppermute(own_int, "blk", inner)
    rows, _ = lax.optimization_barrier((pairs, own_int))
    own = jnp.concatenate([rows, across(rows, 1)])
    own = jnp.concatenate([own, across(own, 3)])
    before = lax.ppermute(own, "blk", upward)

    keep, out1, out2, out3, slots = correlate(own, before, (own_ext, own_int, got_ext, got_int), lag)
    plan = make_plan(own, before, slots)
    full, send, out1, out2, out3 = combine(plan, keep, across(out2, 2), across(out1, 1), across(out3, 3))
    shifted = lax.ppermute(send, ("seg", "blk"), shift)
    outs = finish(pairs.shape[0], plan, full, across(out2, 2), across(out1, 1), across(out3, 3), shifted)
    return tuple(jnp.transpose(out, (0, 2, 1, 3)) for out in outs)


def solution(mesh):
    groups = mesh.shape["blk"]
    planes = mesh.shape["seg"]

    def run(records, pairs):
        body = functools.partial(
            shards,
            groups,
            planes,
            jnp.asarray(lag_rows(records.shape[0])),
        )
        return jax.shard_map(
            body,
            mesh=mesh,
            in_specs=(P("seg", "blk", None), P(("blk", "seg"), None)),
            out_specs=(P(("blk", "seg"), None, None, None), P(("blk", "seg"), None, None, None)),
            check_vma=False,
        )(records, pairs)

    return run
```

```python
import functools

import jax
import jax.numpy as jnp
import ml_dtypes
import numpy as np
from jax import lax
from jax.experimental import pallas as pl
from jax.experimental.pallas import tpu as pltpu
from jax.sharding import PartitionSpec as P

BINS = 256
LENGTH = 512
CHANS = 128
MAXLAG = 32
LAGS = 2 * MAXLAG + 1
REACH = 8
SMOOTH = 32
BAND = 64
GROUP = 8
HALF = GROUP // 2
PLANES = 4
ROWS = HALF * CHANS
SUB = ROWS
REACHED = 384
SLOTS = 13
SHIFTED = 8
BODY = 64
CHUNK = SLOTS * BODY + 16
SEND2 = SHIFTED * BODY + 16
SEND3 = 4 * BODY + 16
PAIRS, MOVES, WRITES, PLAN = 48, 8, 40, 128
TWO = CHUNK
THREE = CHUNK + SEND2
POOL = THREE + 3 * SEND3
MIB = 1024 * 1024
TINY = pl.CostEstimate(flops=1, bytes_accessed=1, transcendentals=0)
BF = jnp.bfloat16
F32 = jnp.float32
SMEM = pl.BlockSpec(memory_space=pltpu.SMEM)
VMEM = pl.BlockSpec(memory_space=pltpu.VMEM)


def split(array):
    high = array.astype(ml_dtypes.bfloat16)
    low = (array - high.astype(np.float32)).astype(ml_dtypes.bfloat16)
    return high, low


def lag_rows(segments):
    freqs = np.concatenate([np.arange(0, BINS, 2), np.arange(1, BINS, 2)])
    shifts = np.arange(-MAXLAG, MAXLAG + 1)
    phase = (shifts[:, None] * freqs[None, :] % LENGTH) * (2.0 * np.pi / LENGTH)
    table = np.concatenate([np.cos(phase), -np.sin(phase)], axis=1) / np.sqrt(segments * BINS)
    table = np.concatenate([table, np.zeros((CHANS - LAGS, LENGTH))], axis=0).T.astype(np.float32)
    return np.concatenate(split(table), axis=1)


def dot(a, b):
    return jnp.dot(a, b, preferred_element_type=F32)


def halves(x):
    high = x.astype(BF)
    return high, (x - high.astype(F32)).astype(BF)


def make_tables(tab):
    at = lax.broadcasted_iota(jnp.int32, (REACHED, LENGTH), 0)
    col = lax.broadcasted_iota(jnp.int32, (REACHED, LENGTH), 1)
    apart = at - col + jnp.where(col < BINS, 0, LENGTH - REACHED)
    tab[:REACHED] = jnp.where(jnp.abs(apart) <= SMOOTH, 1.0, 0.0).astype(BF)
    half = BINS // 2
    row = lax.broadcasted_iota(jnp.int32, (CHANS, LENGTH), 0)
    col = lax.broadcasted_iota(jnp.int32, (CHANS, LENGTH), 1)
    row = jnp.bitwise_and(row, half - 1) // (BAND // 2)
    col = jnp.bitwise_and(col, half - 1) // (BAND // 2)
    tab[REACHED:LENGTH] = jnp.where(row == col, 0.5 / BAND, 0.0).astype(BF)

    def cosine(step, shift):
        col = lax.broadcasted_iota(jnp.int32, (16, BINS), 1)
        freq = 2 * jnp.bitwise_and(col, half - 1) + jnp.right_shift(col, 7)
        k = lax.broadcasted_iota(jnp.int32, (16, BINS), 0) * freq
        k = jnp.bitwise_and(k * step - shift + BINS, LENGTH - 1) - BINS
        square = jnp.square(k.astype(F32) * (2.0 * np.pi / LENGTH))
        value = jnp.ones_like(square)
        for n in range(20, 0, -2):
            value = 1.0 - value * square * (1.0 / (n * (n - 1)))
        return value

    quarter = LENGTH // 4
    fine_cos, fine_sin = cosine(1, 0), cosine(1, quarter)
    coarse_cos, coarse_sin = cosine(16, 0), cosine(16, quarter)
    for a in range(16):
        c, s = coarse_cos[a : a + 1], coarse_sin[a : a + 1]
        for k, part in enumerate((c * fine_cos - s * fine_sin, -(s * fine_cos) - c * fine_sin)):
            for n, rounded in enumerate(halves(part)):
                rows = pl.ds(LENGTH + n * BINS + 16 * a, 16)
                tab[rows, k * half : (k + 1) * half] = rounded[:, :half]
                tab[rows, BINS + k * half : BINS + (k + 1) * half] = rounded[:, half:]


def whiten_body(outer, records, white, buf, tab, sems):
    segs = records.shape[0]
    core = jnp.bitwise_and(lax.axis_index("blk"), 1)
    begin = pl.multiple_of((core if outer else 1 - core) * ROWS, ROWS)

    def load(k):
        return pltpu.make_async_copy(records.at[k, pl.ds(begin, ROWS)], buf.at[k], sems.at[k])

    for k in range(segs):
        load(k).start()
    at = lax.broadcasted_iota(jnp.int32, (1, LENGTH), 1)
    count = jnp.minimum(at, SMOOTH) + jnp.minimum(LENGTH - 1 - at, SMOOTH) + 1
    share = 1.0 / count.astype(F32)
    make_tables(tab)

    def step(k, carry):
        load(k).wait()
        parts = range(ROWS // SUB)
        xs = [buf[k, pl.ds(n * SUB, SUB), :] for n in parts]
        levels = []
        first = tab[:REACHED, :BINS]
        second = tab[:REACHED, BINS:]
        for x in xs:
            ahi, alo = halves(jnp.abs(x))
            left = jnp.concatenate([ahi[:, :REACHED], alo[:, :REACHED]], axis=1)
            right = jnp.concatenate([ahi[:, LENGTH - REACHED :], alo[:, LENGTH - REACHED :]], axis=1)
            left = dot(left, jnp.concatenate([first, first], axis=0))
            right = dot(right, jnp.concatenate([second, second], axis=0))
            levels.append(jnp.concatenate([left, right], axis=1) * share)
        spectra = []
        products = []
        for at in (0, BINS):
            high = tab[LENGTH : LENGTH + BINS, at : at + BINS]
            products.append(jnp.concatenate([high, high, tab[LENGTH + BINS :, at : at + BINS]], axis=0))
        for x, level in zip(xs, levels):
            normed = x * pl.reciprocal(level + 1e-06, approx=True)
            left, right = normed[:, :BINS], normed[:, BINS:]
            pair = []
            for part, product in zip((left + right, left - right), products):
                high, low = halves(part)
                pair.append(dot(jnp.concatenate([high, low, high], axis=1), product))
            spectra.append(pair)
        same = jnp.concatenate([tab[REACHED:LENGTH, :BINS], tab[REACHED:LENGTH, BINS:]], axis=0)
        for n in parts:
            even, odd = spectra[n]
            re = jnp.concatenate([even[:, : BINS // 2], odd[:, : BINS // 2]], axis=1)
            im = jnp.concatenate([even[:, BINS // 2 :], odd[:, BINS // 2 :]], axis=1)
            power = dot((re * re + im * im).astype(BF), same)
            factor = lax.rsqrt(power + 1e-05)
            per = SUB // CHANS
            white[pl.ds(n * per, per), k, :, :BINS] = (re * factor).astype(BF).reshape(per, CHANS, BINS)
            white[pl.ds(n * per, per), k, :, BINS:] = (im * factor).astype(BF).reshape(per, CHANS, BINS)
        return carry

    lax.fori_loop(0, segs, step, 0)


def whiten(outer, records):
    segs = records.shape[0]
    return pl.pallas_call(
        functools.partial(whiten_body, outer),
        in_specs=[pl.BlockSpec(memory_space=pltpu.HBM)],
        out_specs=VMEM,
        out_shape=jax.ShapeDtypeStruct((HALF, segs, CHANS, LENGTH), BF),
        scratch_shapes=[
            pltpu.VMEM((segs, ROWS, LENGTH), F32),
            pltpu.VMEM((2 * LENGTH, LENGTH), BF),
            pltpu.SemaphoreType.DMA((segs,)),
        ],
        compiler_params=pltpu.CompilerParams(vmem_limit_bytes=50 * MIB),
        cost_estimate=TINY,
        name="whiten",
    )(records)


VISITS = [(p, d) for p in range(HALF) for d in range(1, REACH + 1) if p + d >= HALF] + [
    (p, d) for p in range(HALF, 12) for d in range(1, REACH + 1) if p < GROUP or p + d < 12
]
UPWARD = (
    ((0, 0), (1, 0), (1, 1), (2, 0), (2, 1), (3, 0), (3, 1)),
    ((2, 2), (3, 2), (3, 3)),
)


def seg_index():
    return lax.axis_index("seg").astype(jnp.int32)


def behind(owner):
    apart = jnp.bitwise_xor(seg_index(), owner)
    return 2 * jnp.bitwise_xor(apart, jnp.right_shift(apart, 1))


def list_pairs(own, before, codes, slots):
    s = seg_index()
    used = [jnp.int32(0)] * PLANES
    n = jnp.int32(0)
    for p, d in VISITS:
        row = p + HALF if p < HALF else p - HALF
        owner = row // 2
        live = (before if p < HALF else own)[behind(owner) + row % 2, d - 1]
        code = p + d * 16 + jnp.bitwise_xor(owner, s) * 256 + used[owner] * 4096
        slots[p * REACH + d - 1] = used[owner]
        used[owner] = used[owner] + live
        if p in (6, 7) and p + d in (12, 13):
            slots[96 + (p - 6) * 2 + p + d - 12] = used[0]
            code = code + (used[0] + 1) * 65536
            used[0] = used[0] + live
        codes[n] = code
        n = n + live
    return n


def plan_body(own, before, slots, plan):
    s = seg_index()
    n = jnp.int32(0)
    for owner in (0, 1):
        for k, (i, j) in enumerate(UPWARD[owner]):
            p, d = HALF + i, GROUP + j - i
            entry = p * REACH + d - 1 if i // 2 == owner else 96 + (i - 2) * 2 + j
            plan[MOVES + n] = slots[entry] + k * 4096
            n = n + jnp.where(s == owner, own[behind(i // 2) + i % 2, d - 1], 0)
    for r in range(1, PLANES):
        to = jnp.bitwise_xor(s, r)
        ahead = s < to
        for i in range(2):
            for j in range(2):
                row = 2 * s + i
                p = jnp.where(ahead, row + HALF, jnp.maximum(row - HALF, 0))
                d = 2 * to + j - row + jnp.where(ahead, 0, GROUP)
                live = jnp.where(ahead, own[i, d - 1], jnp.where(s >= 2, before[i, d - 1], 0))
                plan[MOVES + n] = slots[p * REACH + d - 1] + r * 256 + (2 * i + j) * 4096
                n = n + live
    plan[0] = n

    def write(n, i, d, base, size, slot):
        plan[WRITES + n] = base + slot * BODY + (base + size * BODY + slot) * 4096 + (i * 8 + d - 1) * 16777216

    n = jnp.int32(0)
    above = jnp.int32(0)
    for i in range(2):
        for d in range(1, REACH + 1):
            row = 2 * s + i
            live = own[i, d - 1]
            shift = (row + d >= GROUP) & (s >= 2)
            slot = jnp.where(shift, above, slots[(HALF + row) * REACH + d - 1])
            write(n, i, d, jnp.where(shift, TWO, 0), jnp.where(shift, SHIFTED, SLOTS), slot)
            n = n + live
            above = above + jnp.where(shift, live, 0)
    plan[1] = n
    for j in range(2):
        for d in range(1, REACH + 1):
            low = 2 * s + j - d
            crossing = low < 0
            row = jnp.where(crossing, low + GROUP, low)
            owner = jnp.right_shift(row, 1)
            at = behind(owner) + jnp.bitwise_and(row, 1)
            live = jnp.where(crossing, before[at, d - 1], own[at, d - 1])
            up = crossing & (owner < 2)
            mine = (owner == s) & jnp.logical_not(up)
            k0 = jnp.where(row == 0, 0, 2 * row - 1) + j
            k1 = jnp.where(row == 2, 0, 1) + j
            entry = jnp.maximum((HALF + low) * REACH + d - 1, 0)
            slot = jnp.where(mine, slots[entry], 2 * (row - 2 * owner) + j)
            slot = jnp.where(up, jnp.where(s == 0, k0, k1), slot)
            base = jnp.where(mine, 0, THREE + (jnp.bitwise_xor(s, owner) - 1) * SEND3)
            base = jnp.where(up, TWO, base)
            size = jnp.where(mine, SLOTS, jnp.where(up, SHIFTED, 4))
            write(n, j, d, base, size, slot)
            n = n + live
    plan[2] = n


def make_plan(*args):
    return pl.pallas_call(
        plan_body,
        in_specs=[SMEM] * 3,
        out_specs=SMEM,
        out_shape=jax.ShapeDtypeStruct((PLAN,), jnp.int32),
        compiler_params=pltpu.CompilerParams(vmem_limit_bytes=4 * MIB),
        cost_estimate=TINY,
        name="plan",
    )(*args)


def correlate_body(
    own, before, own_ext, own_int, got_ext, got_int, lag, keep, out1, out2, out3, slots, low, high, stk, pq, codes, last
):
    count = list_pairs(own, before, codes, slots)
    core = jnp.bitwise_and(lax.axis_index("blk"), 1)
    sources = (
        (own_ext, HALF * (1 + core)),
        (own_int, HALF * (2 - core)),
        (got_ext, 3 * HALF * core),
        (got_int, 3 * HALF * (1 - core)),
    )
    segs = low.shape[0]
    last[0] = -1

    def grab(dest, block):
        for ref, begin in sources:

            @pl.when((block >= begin) & (block < begin + HALF))
            def _(ref=ref, begin=begin):
                dest[...] = ref[block - begin]

    def put(r, n, stack):
        stk[r, pl.ds(pl.multiple_of(n * BODY, BODY), BODY), :] = stack[:BODY]
        stk[r, pl.ds(SLOTS * BODY + n, 1), :] = stack[BODY:LAGS]

    def pair(n, carry):
        code = codes[n]
        p = jnp.bitwise_and(code, 15)
        d = jnp.bitwise_and(jnp.right_shift(code, 4), 15)

        @pl.when(last[0] != p)
        def _():
            grab(low, p)
            last[0] = p

        grab(high, p + d)
        for chunk in range(CHANS // 16):
            rows = pl.ds(chunk * 16, 16)
            real = jnp.zeros((16, BINS), F32)
            imag = jnp.zeros((16, BINS), F32)
            for k in range(segs):
                are = low[k, rows, :BINS].astype(F32)
                aim = low[k, rows, BINS:].astype(F32)
                bre = high[k, rows, :BINS].astype(F32)
                bim = high[k, rows, BINS:].astype(F32)
                real += are * bre + aim * bim
                imag += are * bim - aim * bre
            rhi, rlo = halves(real)
            ihi, ilo = halves(imag)
            pq[0, rows, :BINS] = rhi
            pq[0, rows, BINS:] = ihi
            pq[1, rows, :BINS] = rlo
            pq[1, rows, BINS:] = ilo
        both = dot(pq[0], lag[...])
        stack = (both[:, :CHANS] + both[:, CHANS:] + dot(pq[1], lag[:, :CHANS])).T
        put(jnp.bitwise_and(jnp.right_shift(code, 8), 3), jnp.bitwise_and(jnp.right_shift(code, 12), 15), stack)
        second = jnp.right_shift(code, 16)

        @pl.when(second > 0)
        def _():
            put(seg_index(), second - 1, stack)

        return carry

    lax.fori_loop(0, count, pair, 0)
    keep[...] = stk[0]
    out1[...] = stk[1].astype(BF)
    out2[...] = stk[2].astype(BF)
    out3[...] = stk[3].astype(BF)


def correlate(own, before, whites, lag):
    segs = whites[0].shape[1]
    chunk = jax.ShapeDtypeStruct((CHUNK, CHANS), BF)
    return pl.pallas_call(
        correlate_body,
        in_specs=[SMEM] * 2 + [VMEM] * 5,
        out_specs=[VMEM] * 4 + [SMEM],
        out_shape=[
            jax.ShapeDtypeStruct((CHUNK, CHANS), F32),
            chunk,
            chunk,
            chunk,
            jax.ShapeDtypeStruct((128,), jnp.int32),
        ],
        scratch_shapes=[
            pltpu.VMEM((segs, CHANS, LENGTH), BF),
            pltpu.VMEM((segs, CHANS, LENGTH), BF),
            pltpu.VMEM((PLANES, CHUNK, CHANS), F32),
            pltpu.VMEM((2, CHANS, LENGTH), BF),
            pltpu.SMEM((PAIRS,), jnp.int32),
            pltpu.SMEM((1,), jnp.int32),
        ],
        compiler_params=pltpu.CompilerParams(vmem_limit_bytes=16 * MIB),
        cost_estimate=TINY,
        name="correlate",
    )(own, before, *whites, lag)


def combine_body(plan, keep, got2, got1, got3, full, send, out1, out2, out3, stage):
    full[...] = (keep[...] + got1[...].astype(F32)) + (got2[...].astype(F32) + got3[...].astype(F32))

    def move(n, carry):
        code = plan[MOVES + n]
        slot = jnp.bitwise_and(code, 255)
        message = jnp.bitwise_and(jnp.right_shift(code, 8), 15)
        k = jnp.right_shift(code, 12)
        size = jnp.where(message == 0, SHIFTED, 4)
        body = pl.ds(pl.multiple_of(slot * BODY, BODY), BODY)
        stage[message, pl.ds(pl.multiple_of(k * BODY, BODY), BODY), :] = full[body, :]
        stage[message, pl.ds(size * BODY + k, 1), :] = full[pl.ds(SLOTS * BODY + slot, 1), :]
        return carry

    lax.fori_loop(0, plan[0], move, 0)

    @pl.when(seg_index() >= 2)
    def _():
        send[: SHIFTED * BODY, :] = full[: SHIFTED * BODY, :].astype(BF)
        send[SHIFTED * BODY :, :] = full[SLOTS * BODY :, :].astype(BF)

    @pl.when(seg_index() < 2)
    def _():
        send[...] = stage[0].astype(BF)

    for r, out in ((1, out1), (2, out2), (3, out3)):
        out[...] = stage[r, :SEND3].astype(BF)


def combine(*args):
    third = jax.ShapeDtypeStruct((SEND3, CHANS), BF)
    return pl.pallas_call(
        combine_body,
        in_specs=[SMEM] + [VMEM] * 4,
        out_specs=[VMEM] * 5,
        out_shape=[
            jax.ShapeDtypeStruct((CHUNK, CHANS), F32),
            jax.ShapeDtypeStruct((SEND2, CHANS), BF),
            third,
            third,
            third,
        ],
        scratch_shapes=[pltpu.VMEM((PLANES, SEND2, CHANS), F32)],
        compiler_params=pltpu.CompilerParams(vmem_limit_bytes=8 * MIB),
        cost_estimate=TINY,
        name="combine",
    )(*args)


def finish_body(plan, full, got2, got1, got3, shifted, fwd, bwd, pool):
    pool[:TWO, :] = full[...]
    pool[TWO:THREE, :] = shifted[...].astype(F32)
    for r, got in ((1, got1), (2, got2), (3, got3)):
        pool[THREE + (r - 1) * SEND3 : THREE + r * SEND3, :] = got[...].astype(F32)
    fwd[...] = jnp.zeros(fwd.shape, F32)
    bwd[...] = jnp.zeros(bwd.shape, F32)

    def write(out, place, n):
        code = plan[WRITES + n]
        body = jnp.bitwise_and(code, 4095)
        i = jnp.right_shift(code, 27)
        at = pl.ds(jnp.bitwise_and(jnp.right_shift(code, 24), 7), 1)
        out[i, place(BODY), at, :] = pool[pl.ds(jnp.bitwise_and(jnp.right_shift(code, 12), 4095), 1), :]
        for m in range(BODY):
            out[i, place(m), at, :] = pool[pl.ds(body + m, 1), :]

    def ahead(n, carry):
        write(fwd, lambda m: m, n)
        return carry

    def behind(n, carry):
        write(bwd, lambda m: BODY - m, n)
        return carry

    lax.fori_loop(0, plan[1], ahead, 0)
    lax.fori_loop(plan[1], plan[2], behind, 0)


def finish(blocks, *args):
    out = jax.ShapeDtypeStruct((blocks, LAGS, REACH, CHANS), F32)
    return pl.pallas_call(
        finish_body,
        in_specs=[SMEM] + [VMEM] * 5,
        out_specs=[VMEM, VMEM],
        out_shape=[out, out],
        scratch_shapes=[pltpu.VMEM((POOL, CHANS), F32)],
        compiler_params=pltpu.CompilerParams(vmem_limit_bytes=8 * MIB),
        cost_estimate=TINY,
        name="finish",
    )(*args)


def shards(groups, planes, lag, records, pairs):
    def across(x, r):
        return lax.ppermute(x, "seg", [(z, z ^ r) for z in range(planes)])

    outer = [(g, g + 1 if g % 2 else g - 1) for g in range(1, groups - 1)]
    inner = [(g, g ^ 1) for g in range(groups)]
    upward = [(g, g + 1) for g in range(groups - 1)]
    shift = [
        (z * groups + g, z * groups + g + step)
        for z in range(planes)
        for g in range(groups)
        for step in (1 if z < 2 else -1,)
        if 0 <= g + step < groups
    ]
    own_ext = whiten(True, records)
    got_ext = lax.ppermute(own_ext, "blk", outer)
    own_int = whiten(False, records)
    got_int = lax.ppermute(own_int, "blk", inner)
    rows, _ = lax.optimization_barrier((pairs, own_int))
    own = jnp.concatenate([rows, across(rows, 1), across(rows, 3), across(rows, 2)])
    before = lax.ppermute(own, "blk", upward)

    keep, out1, out2, out3, slots = correlate(own, before, (own_ext, own_int, got_ext, got_int), lag)
    plan = make_plan(own, before, slots)
    full, send, out1, out2, out3 = combine(plan, keep, across(out2, 2), across(out1, 1), across(out3, 3))
    shifted = lax.ppermute(send, ("seg", "blk"), shift)
    outs = finish(pairs.shape[0], plan, full, across(out2, 2), across(out1, 1), across(out3, 3), shifted)
    return tuple(jnp.transpose(out, (0, 2, 1, 3)) for out in outs)


def solution(mesh):
    groups = mesh.shape["blk"]
    planes = mesh.shape["seg"]

    def run(records, pairs):
        body = functools.partial(
            shards,
            groups,
            planes,
            jnp.asarray(lag_rows(records.shape[0])),
        )
        return jax.shard_map(
            body,
            mesh=mesh,
            in_specs=(P("seg", "blk", None), P(("blk", "seg"), None)),
            out_specs=(P(("blk", "seg"), None, None, None), P(("blk", "seg"), None, None, None)),
            check_vma=False,
        )(records, pairs)

    return run
```

```python
import functools

import jax
import jax.numpy as jnp
import ml_dtypes
import numpy as np
from jax import lax
from jax.experimental import pallas as pl
from jax.experimental.pallas import tpu as pltpu
from jax.sharding import PartitionSpec as P

BINS = 256
LENGTH = 512
CHANS = 128
MAXLAG = 32
LAGS = 2 * MAXLAG + 1
REACH = 8
SMOOTH = 32
BAND = 64
GROUP = 8
HALF = GROUP // 2
PLANES = 4
ROWS = HALF * CHANS
SUB = ROWS
REACHED = 384
SLOTS = 13
SHIFTED = 8
BODY = 64
CHUNK = SLOTS * BODY + 16
SEND2 = SHIFTED * BODY + 16
SEND3 = 4 * BODY + 16
PAIRS, MOVES, WRITES, PLAN = 48, 8, 40, 128
TWO = CHUNK
THREE = CHUNK + SEND2
POOL = THREE + 3 * SEND3
MIB = 1024 * 1024
TINY = pl.CostEstimate(flops=1, bytes_accessed=1, transcendentals=0)
BF = jnp.bfloat16
F32 = jnp.float32
SMEM = pl.BlockSpec(memory_space=pltpu.SMEM)
VMEM = pl.BlockSpec(memory_space=pltpu.VMEM)


def split(array):
    high = array.astype(ml_dtypes.bfloat16)
    low = (array - high.astype(np.float32)).astype(ml_dtypes.bfloat16)
    return high, low


def lag_rows(segments):
    freqs = np.concatenate([np.arange(0, BINS, 2), np.arange(1, BINS, 2)])
    shifts = np.arange(-MAXLAG, MAXLAG + 1)
    phase = (shifts[:, None] * freqs[None, :] % LENGTH) * (2.0 * np.pi / LENGTH)
    table = np.concatenate([np.cos(phase), -np.sin(phase)], axis=1) / np.sqrt(segments * BINS)
    table = np.concatenate([table, np.zeros((CHANS - LAGS, LENGTH))], axis=0).T.astype(np.float32)
    return np.concatenate(split(table), axis=1)


def dot(a, b):
    return jnp.dot(a, b, preferred_element_type=F32)


def halves(x):
    high = x.astype(BF)
    return high, (x - high.astype(F32)).astype(BF)


def make_tables(tab):
    at = lax.broadcasted_iota(jnp.int32, (REACHED, LENGTH), 0)
    col = lax.broadcasted_iota(jnp.int32, (REACHED, LENGTH), 1)
    apart = at - col + jnp.where(col < BINS, 0, LENGTH - REACHED)
    tab[:REACHED] = jnp.where(jnp.abs(apart) <= SMOOTH, 1.0, 0.0).astype(BF)
    half = BINS // 2
    row = lax.broadcasted_iota(jnp.int32, (CHANS, LENGTH), 0)
    col = lax.broadcasted_iota(jnp.int32, (CHANS, LENGTH), 1)
    row = jnp.bitwise_and(row, half - 1) // (BAND // 2)
    col = jnp.bitwise_and(col, half - 1) // (BAND // 2)
    tab[REACHED:LENGTH] = jnp.where(row == col, 0.5 / BAND, 0.0).astype(BF)

    def cosine(step, shift):
        col = lax.broadcasted_iota(jnp.int32, (16, BINS), 1)
        freq = 2 * jnp.bitwise_and(col, half - 1) + jnp.right_shift(col, 7)
        k = lax.broadcasted_iota(jnp.int32, (16, BINS), 0) * freq
        k = jnp.bitwise_and(k * step - shift + BINS, LENGTH - 1) - BINS
        square = jnp.square(k.astype(F32) * (2.0 * np.pi / LENGTH))
        value = jnp.ones_like(square)
        for n in range(20, 0, -2):
            value = 1.0 - value * square * (1.0 / (n * (n - 1)))
        return value

    quarter = LENGTH // 4
    fine_cos, fine_sin = cosine(1, 0), cosine(1, quarter)
    coarse_cos, coarse_sin = cosine(16, 0), cosine(16, quarter)
    for a in range(16):
        c, s = coarse_cos[a : a + 1], coarse_sin[a : a + 1]
        for k, part in enumerate((c * fine_cos - s * fine_sin, -(s * fine_cos) - c * fine_sin)):
            for n, rounded in enumerate(halves(part)):
                rows = pl.ds(LENGTH + n * BINS + 16 * a, 16)
                tab[rows, k * half : (k + 1) * half] = rounded[:, :half]
                tab[rows, BINS + k * half : BINS + (k + 1) * half] = rounded[:, half:]


def whiten_body(outer, records, white, buf, tab, sems):
    segs = records.shape[0]
    core = jnp.bitwise_and(lax.axis_index("blk"), 1)
    begin = pl.multiple_of((core if outer else 1 - core) * ROWS, ROWS)

    def load(k):
        return pltpu.make_async_copy(records.at[k, pl.ds(begin, ROWS)], buf.at[k], sems.at[k])

    for k in range(segs):
        load(k).start()
    at = lax.broadcasted_iota(jnp.int32, (1, LENGTH), 1)
    count = jnp.minimum(at, SMOOTH) + jnp.minimum(LENGTH - 1 - at, SMOOTH) + 1
    share = 1.0 / count.astype(F32)
    make_tables(tab)

    def step(k, carry):
        load(k).wait()
        parts = range(ROWS // SUB)
        xs = [buf[k, pl.ds(n * SUB, SUB), :] for n in parts]
        levels = []
        first = tab[:REACHED, :BINS]
        second = tab[:REACHED, BINS:]
        for x in xs:
            ahi, alo = halves(jnp.abs(x))
            left = jnp.concatenate([ahi[:, :REACHED], alo[:, :REACHED]], axis=1)
            right = jnp.concatenate([ahi[:, LENGTH - REACHED :], alo[:, LENGTH - REACHED :]], axis=1)
            left = dot(left, jnp.concatenate([first, first], axis=0))
            right = dot(right, jnp.concatenate([second, second], axis=0))
            levels.append(jnp.concatenate([left, right], axis=1) * share)
        spectra = []
        products = []
        for at in (0, BINS):
            high = tab[LENGTH : LENGTH + BINS, at : at + BINS]
            products.append(jnp.concatenate([high, high, tab[LENGTH + BINS :, at : at + BINS]], axis=0))
        for x, level in zip(xs, levels):
            normed = x * pl.reciprocal(level + 1e-06, approx=True)
            left, right = normed[:, :BINS], normed[:, BINS:]
            pair = []
            for part, product in zip((left + right, left - right), products):
                high, low = halves(part)
                pair.append(dot(jnp.concatenate([high, low, high], axis=1), product))
            spectra.append(pair)
        same = jnp.concatenate([tab[REACHED:LENGTH, :BINS], tab[REACHED:LENGTH, BINS:]], axis=0)
        for n in parts:
            even, odd = spectra[n]
            re = jnp.concatenate([even[:, : BINS // 2], odd[:, : BINS // 2]], axis=1)
            im = jnp.concatenate([even[:, BINS // 2 :], odd[:, BINS // 2 :]], axis=1)
            power = dot((re * re + im * im).astype(BF), same)
            factor = lax.rsqrt(power + 1e-05)
            per = SUB // CHANS
            white[pl.ds(n * per, per), k, :, :BINS] = (re * factor).astype(BF).reshape(per, CHANS, BINS)
            white[pl.ds(n * per, per), k, :, BINS:] = (im * factor).astype(BF).reshape(per, CHANS, BINS)
        return carry

    lax.fori_loop(0, segs, step, 0)


def whiten(outer, records):
    segs = records.shape[0]
    return pl.pallas_call(
        functools.partial(whiten_body, outer),
        in_specs=[pl.BlockSpec(memory_space=pltpu.HBM)],
        out_specs=VMEM,
        out_shape=jax.ShapeDtypeStruct((HALF, segs, CHANS, LENGTH), BF),
        scratch_shapes=[
            pltpu.VMEM((segs, ROWS, LENGTH), F32),
            pltpu.VMEM((2 * LENGTH, LENGTH), BF),
            pltpu.SemaphoreType.DMA((segs,)),
        ],
        compiler_params=pltpu.CompilerParams(vmem_limit_bytes=50 * MIB),
        cost_estimate=TINY,
        name="whiten",
    )(records)


VISITS = [(p, d) for p in range(HALF) for d in range(1, REACH + 1) if p + d >= HALF] + [
    (p, d) for p in range(HALF, 12) for d in range(1, REACH + 1) if p < GROUP or p + d < 12
]
UPWARD = (
    ((0, 0), (1, 0), (1, 1), (2, 0), (2, 1), (3, 0), (3, 1)),
    ((2, 2), (3, 2), (3, 3)),
)


def seg_index():
    return lax.axis_index("seg").astype(jnp.int32)


def behind(owner):
    apart = jnp.bitwise_xor(seg_index(), owner)
    return 2 * jnp.bitwise_xor(apart, jnp.right_shift(apart, 1))


def list_pairs(own, before, codes, slots):
    s = seg_index()
    used = [jnp.int32(0)] * PLANES
    n = jnp.int32(0)
    for p, d in VISITS:
        row = p + HALF if p < HALF else p - HALF
        owner = row // 2
        live = (before if p < HALF else own)[behind(owner) + row % 2, d - 1]
        code = p + d * 16 + jnp.bitwise_xor(owner, s) * 256 + used[owner] * 4096
        slots[p * REACH + d - 1] = used[owner]
        used[owner] = used[owner] + live
        if p in (6, 7) and p + d in (12, 13):
            slots[96 + (p - 6) * 2 + p + d - 12] = used[0]
            code = code + (used[0] + 1) * 65536
            used[0] = used[0] + live
        codes[n] = code
        n = n + live
    return n


def plan_body(own, before, slots, plan):
    s = seg_index()
    n = jnp.int32(0)
    for owner in (0, 1):
        for k, (i, j) in enumerate(UPWARD[owner]):
            p, d = HALF + i, GROUP + j - i
            entry = p * REACH + d - 1 if i // 2 == owner else 96 + (i - 2) * 2 + j
            plan[MOVES + n] = slots[entry] + k * 4096
            n = n + jnp.where(s == owner, own[behind(i // 2) + i % 2, d - 1], 0)
    for r in range(1, PLANES):
        to = jnp.bitwise_xor(s, r)
        ahead = s < to
        for i in range(2):
            for j in range(2):
                row = 2 * s + i
                p = jnp.where(ahead, row + HALF, jnp.maximum(row - HALF, 0))
                d = 2 * to + j - row + jnp.where(ahead, 0, GROUP)
                live = jnp.where(ahead, own[i, d - 1], jnp.where(s >= 2, before[i, d - 1], 0))
                plan[MOVES + n] = slots[p * REACH + d - 1] + r * 256 + (2 * i + j) * 4096
                n = n + live
    plan[0] = n

    def write(n, i, d, base, size, slot):
        plan[WRITES + n] = base + slot * BODY + (base + size * BODY + slot) * 4096 + (i * 8 + d - 1) * 16777216

    n = jnp.int32(0)
    above = jnp.int32(0)
    for i in range(2):
        for d in range(1, REACH + 1):
            row = 2 * s + i
            live = own[i, d - 1]
            shift = (row + d >= GROUP) & (s >= 2)
            slot = jnp.where(shift, above, slots[(HALF + row) * REACH + d - 1])
            write(n, i, d, jnp.where(shift, TWO, 0), jnp.where(shift, SHIFTED, SLOTS), slot)
            n = n + live
            above = above + jnp.where(shift, live, 0)
    plan[1] = n
    for j in range(2):
        for d in range(1, REACH + 1):
            low = 2 * s + j - d
            crossing = low < 0
            row = jnp.where(crossing, low + GROUP, low)
            owner = jnp.right_shift(row, 1)
            at = behind(owner) + jnp.bitwise_and(row, 1)
            live = jnp.where(crossing, before[at, d - 1], own[at, d - 1])
            up = crossing & (owner < 2)
            mine = (owner == s) & jnp.logical_not(up)
            k0 = jnp.where(row == 0, 0, 2 * row - 1) + j
            k1 = jnp.where(row == 2, 0, 1) + j
            entry = jnp.maximum((HALF + low) * REACH + d - 1, 0)
            slot = jnp.where(mine, slots[entry], 2 * (row - 2 * owner) + j)
            slot = jnp.where(up, jnp.where(s == 0, k0, k1), slot)
            base = jnp.where(mine, 0, THREE + (jnp.bitwise_xor(s, owner) - 1) * SEND3)
            base = jnp.where(up, TWO, base)
            size = jnp.where(mine, SLOTS, jnp.where(up, SHIFTED, 4))
            write(n, j, d, base, size, slot)
            n = n + live
    plan[2] = n


def make_plan(*args):
    return pl.pallas_call(
        plan_body,
        in_specs=[SMEM] * 3,
        out_specs=SMEM,
        out_shape=jax.ShapeDtypeStruct((PLAN,), jnp.int32),
        compiler_params=pltpu.CompilerParams(vmem_limit_bytes=4 * MIB),
        cost_estimate=TINY,
        name="plan",
    )(*args)


def correlate_body(
    own, before, own_ext, own_int, got_ext, got_int, lag, keep, out1, out2, out3, slots, low, high, stk, pq, codes, last
):
    count = list_pairs(own, before, codes, slots)
    core = jnp.bitwise_and(lax.axis_index("blk"), 1)
    sources = (
        (own_ext, HALF * (1 + core)),
        (own_int, HALF * (2 - core)),
        (got_ext, 3 * HALF * core),
        (got_int, 3 * HALF * (1 - core)),
    )
    segs = low.shape[0]
    last[0] = -1

    def grab(dest, block):
        for ref, begin in sources:

            @pl.when((block >= begin) & (block < begin + HALF))
            def _(ref=ref, begin=begin):
                dest[...] = ref[block - begin]

    def put(r, n, stack):
        stk[r, pl.ds(pl.multiple_of(n * BODY, BODY), BODY), :] = stack[:BODY]
        stk[r, pl.ds(SLOTS * BODY + n, 1), :] = stack[BODY:LAGS]

    def pair(n, carry):
        code = codes[n]
        p = jnp.bitwise_and(code, 15)
        d = jnp.bitwise_and(jnp.right_shift(code, 4), 15)

        @pl.when(last[0] != p)
        def _():
            grab(low, p)
            last[0] = p

        grab(high, p + d)
        for chunk in range(CHANS // 16):
            rows = pl.ds(chunk * 16, 16)
            real = jnp.zeros((16, BINS), F32)
            imag = jnp.zeros((16, BINS), F32)
            for k in range(segs):
                are = low[k, rows, :BINS].astype(F32)
                aim = low[k, rows, BINS:].astype(F32)
                bre = high[k, rows, :BINS].astype(F32)
                bim = high[k, rows, BINS:].astype(F32)
                real += are * bre + aim * bim
                imag += are * bim - aim * bre
            rhi, rlo = halves(real)
            ihi, ilo = halves(imag)
            pq[0, rows, :BINS] = rhi
            pq[0, rows, BINS:] = ihi
            pq[1, rows, :BINS] = rlo
            pq[1, rows, BINS:] = ilo
        both = dot(pq[0], lag[...])
        stack = (both[:, :CHANS] + both[:, CHANS:] + dot(pq[1], lag[:, :CHANS])).T
        put(jnp.bitwise_and(jnp.right_shift(code, 8), 3), jnp.bitwise_and(jnp.right_shift(code, 12), 15), stack)
        second = jnp.right_shift(code, 16)

        @pl.when(second > 0)
        def _():
            put(seg_index(), second - 1, stack)

        return carry

    lax.fori_loop(0, count, pair, 0)
    keep[...] = stk[0]
    out1[...] = stk[1].astype(BF)
    out2[...] = stk[2].astype(BF)
    out3[...] = stk[3].astype(BF)


def correlate(own, before, whites, lag):
    segs = whites[0].shape[1]
    chunk = jax.ShapeDtypeStruct((CHUNK, CHANS), BF)
    return pl.pallas_call(
        correlate_body,
        in_specs=[SMEM] * 2 + [VMEM] * 5,
        out_specs=[VMEM] * 4 + [SMEM],
        out_shape=[
            jax.ShapeDtypeStruct((CHUNK, CHANS), F32),
            chunk,
            chunk,
            chunk,
            jax.ShapeDtypeStruct((128,), jnp.int32),
        ],
        scratch_shapes=[
            pltpu.VMEM((segs, CHANS, LENGTH), BF),
            pltpu.VMEM((segs, CHANS, LENGTH), BF),
            pltpu.VMEM((PLANES, CHUNK, CHANS), F32),
            pltpu.VMEM((2, CHANS, LENGTH), BF),
            pltpu.SMEM((PAIRS,), jnp.int32),
            pltpu.SMEM((1,), jnp.int32),
        ],
        compiler_params=pltpu.CompilerParams(vmem_limit_bytes=16 * MIB),
        cost_estimate=TINY,
        name="correlate",
    )(own, before, *whites, lag)


def combine_body(plan, keep, got1, got3, got2, full, send, out1, out2, out3, stage):
    full[...] = (keep[...] + got1[...].astype(F32)) + (got2[...].astype(F32) + got3[...].astype(F32))

    def move(n, carry):
        code = plan[MOVES + n]
        slot = jnp.bitwise_and(code, 255)
        message = jnp.bitwise_and(jnp.right_shift(code, 8), 15)
        k = jnp.right_shift(code, 12)
        size = jnp.where(message == 0, SHIFTED, 4)
        body = pl.ds(pl.multiple_of(slot * BODY, BODY), BODY)
        stage[message, pl.ds(pl.multiple_of(k * BODY, BODY), BODY), :] = full[body, :]
        stage[message, pl.ds(size * BODY + k, 1), :] = full[pl.ds(SLOTS * BODY + slot, 1), :]
        return carry

    lax.fori_loop(0, plan[0], move, 0)

    @pl.when(seg_index() >= 2)
    def _():
        send[: SHIFTED * BODY, :] = full[: SHIFTED * BODY, :].astype(BF)
        send[SHIFTED * BODY :, :] = full[SLOTS * BODY :, :].astype(BF)

    @pl.when(seg_index() < 2)
    def _():
        send[...] = stage[0].astype(BF)

    for r, out in ((1, out1), (2, out2), (3, out3)):
        out[...] = stage[r, :SEND3].astype(BF)


def combine(*args):
    third = jax.ShapeDtypeStruct((SEND3, CHANS), BF)
    return pl.pallas_call(
        combine_body,
        in_specs=[SMEM] + [VMEM] * 4,
        out_specs=[VMEM] * 5,
        out_shape=[
            jax.ShapeDtypeStruct((CHUNK, CHANS), F32),
            jax.ShapeDtypeStruct((SEND2, CHANS), BF),
            third,
            third,
            third,
        ],
        scratch_shapes=[pltpu.VMEM((PLANES, SEND2, CHANS), F32)],
        compiler_params=pltpu.CompilerParams(vmem_limit_bytes=8 * MIB),
        cost_estimate=TINY,
        name="combine",
    )(*args)


def finish_body(plan, full, got2, got1, got3, shifted, fwd, bwd, pool):
    pool[:TWO, :] = full[...]
    pool[TWO:THREE, :] = shifted[...].astype(F32)
    for r, got in ((1, got1), (2, got2), (3, got3)):
        pool[THREE + (r - 1) * SEND3 : THREE + r * SEND3, :] = got[...].astype(F32)
    fwd[...] = jnp.zeros(fwd.shape, F32)
    bwd[...] = jnp.zeros(bwd.shape, F32)

    def write(out, place, n):
        code = plan[WRITES + n]
        body = jnp.bitwise_and(code, 4095)
        i = jnp.right_shift(code, 27)
        at = pl.ds(jnp.bitwise_and(jnp.right_shift(code, 24), 7), 1)
        out[i, place(BODY), at, :] = pool[pl.ds(jnp.bitwise_and(jnp.right_shift(code, 12), 4095), 1), :]
        for m in range(BODY):
            out[i, place(m), at, :] = pool[pl.ds(body + m, 1), :]

    def ahead(n, carry):
        write(fwd, lambda m: m, n)
        return carry

    def behind(n, carry):
        write(bwd, lambda m: BODY - m, n)
        return carry

    lax.fori_loop(0, plan[1], ahead, 0)
    lax.fori_loop(plan[1], plan[2], behind, 0)


def finish(blocks, *args):
    out = jax.ShapeDtypeStruct((blocks, LAGS, REACH, CHANS), F32)
    return pl.pallas_call(
        finish_body,
        in_specs=[SMEM] + [VMEM] * 5,
        out_specs=[VMEM, VMEM],
        out_shape=[out, out],
        scratch_shapes=[pltpu.VMEM((POOL, CHANS), F32)],
        compiler_params=pltpu.CompilerParams(vmem_limit_bytes=8 * MIB),
        cost_estimate=TINY,
        name="finish",
    )(*args)


def shards(groups, planes, lag, records, pairs):
    def across(x, r):
        return lax.ppermute(x, "seg", [(z, z ^ r) for z in range(planes)])

    outer = [(g, g + 1 if g % 2 else g - 1) for g in range(1, groups - 1)]
    inner = [(g, g ^ 1) for g in range(groups)]
    upward = [(g, g + 1) for g in range(groups - 1)]
    shift = [
        (z * groups + g, z * groups + g + step)
        for z in range(planes)
        for g in range(groups)
        for step in (1 if z < 2 else -1,)
        if 0 <= g + step < groups
    ]
    own_ext = whiten(True, records)
    got_ext = lax.ppermute(own_ext, "blk", outer)
    own_int = whiten(False, records)
    got_int = lax.ppermute(own_int, "blk", inner)
    rows, _ = lax.optimization_barrier((pairs, own_int))
    own = jnp.concatenate([rows, across(rows, 1), across(rows, 3), across(rows, 2)])
    before = lax.ppermute(own, "blk", upward)

    keep, out1, out2, out3, slots = correlate(own, before, (own_ext, own_int, got_ext, got_int), lag)
    plan = make_plan(own, before, slots)
    full, send, out1, out2, out3 = combine(plan, keep, across(out1, 1), across(out3, 3), across(out2, 2))
    shifted = lax.ppermute(send, ("seg", "blk"), shift)
    outs = finish(pairs.shape[0], plan, full, across(out2, 2), across(out1, 1), across(out3, 3), shifted)
    return tuple(jnp.transpose(out, (0, 2, 1, 3)) for out in outs)


def solution(mesh):
    groups = mesh.shape["blk"]
    planes = mesh.shape["seg"]

    def run(records, pairs):
        body = functools.partial(
            shards,
            groups,
            planes,
            jnp.asarray(lag_rows(records.shape[0])),
        )
        return jax.shard_map(
            body,
            mesh=mesh,
            in_specs=(P("seg", "blk", None), P(("blk", "seg"), None)),
            out_specs=(P(("blk", "seg"), None, None, None), P(("blk", "seg"), None, None, None)),
            check_vma=False,
        )(records, pairs)

    return run
```

```python
import functools

import jax
import jax.numpy as jnp
import ml_dtypes
import numpy as np
from jax import lax
from jax.experimental import pallas as pl
from jax.experimental.pallas import tpu as pltpu
from jax.sharding import PartitionSpec as P

BINS = 256
LENGTH = 512
CHANS = 128
MAXLAG = 32
LAGS = 2 * MAXLAG + 1
REACH = 8
SMOOTH = 32
BAND = 64
GROUP = 8
HALF = GROUP // 2
PLANES = 4
ROWS = HALF * CHANS
SUB = ROWS
REACHED = 384
SLOTS = 13
SHIFTED = 8
BODY = 64
CHUNK = SLOTS * BODY + 16
SEND2 = SHIFTED * BODY + 16
SEND3 = 4 * BODY + 16
PAIRS, MOVES, WRITES, PLAN = 48, 8, 40, 128
TWO = CHUNK
THREE = CHUNK + SEND2
POOL = THREE + 3 * SEND3
MIB = 1024 * 1024
TINY = pl.CostEstimate(flops=1, bytes_accessed=1, transcendentals=0)
BF = jnp.bfloat16
F32 = jnp.float32
SMEM = pl.BlockSpec(memory_space=pltpu.SMEM)
VMEM = pl.BlockSpec(memory_space=pltpu.VMEM)


def split(array):
    high = array.astype(ml_dtypes.bfloat16)
    low = (array - high.astype(np.float32)).astype(ml_dtypes.bfloat16)
    return high, low


def lag_rows(segments):
    freqs = np.concatenate([np.arange(0, BINS, 2), np.arange(1, BINS, 2)])
    shifts = np.arange(-MAXLAG, MAXLAG + 1)
    phase = (shifts[:, None] * freqs[None, :] % LENGTH) * (2.0 * np.pi / LENGTH)
    table = np.concatenate([np.cos(phase), -np.sin(phase)], axis=1) / np.sqrt(segments * BINS)
    table = np.concatenate([table, np.zeros((CHANS - LAGS, LENGTH))], axis=0).T.astype(np.float32)
    return np.concatenate(split(table), axis=1)


def dot(a, b):
    return jnp.dot(a, b, preferred_element_type=F32)


def halves(x):
    high = x.astype(BF)
    return high, (x - high.astype(F32)).astype(BF)


def make_tables(tab):
    at = lax.broadcasted_iota(jnp.int32, (REACHED, LENGTH), 0)
    col = lax.broadcasted_iota(jnp.int32, (REACHED, LENGTH), 1)
    apart = at - col + jnp.where(col < BINS, 0, LENGTH - REACHED)
    tab[:REACHED] = jnp.where(jnp.abs(apart) <= SMOOTH, 1.0, 0.0).astype(BF)
    half = BINS // 2
    row = lax.broadcasted_iota(jnp.int32, (CHANS, LENGTH), 0)
    col = lax.broadcasted_iota(jnp.int32, (CHANS, LENGTH), 1)
    row = jnp.bitwise_and(row, half - 1) // (BAND // 2)
    col = jnp.bitwise_and(col, half - 1) // (BAND // 2)
    tab[REACHED:LENGTH] = jnp.where(row == col, 0.5 / BAND, 0.0).astype(BF)

    def cosine(step, shift):
        col = lax.broadcasted_iota(jnp.int32, (16, BINS), 1)
        freq = 2 * jnp.bitwise_and(col, half - 1) + jnp.right_shift(col, 7)
        k = lax.broadcasted_iota(jnp.int32, (16, BINS), 0) * freq
        k = jnp.bitwise_and(k * step - shift + BINS, LENGTH - 1) - BINS
        square = jnp.square(k.astype(F32) * (2.0 * np.pi / LENGTH))
        value = jnp.ones_like(square)
        for n in range(20, 0, -2):
            value = 1.0 - value * square * (1.0 / (n * (n - 1)))
        return value

    quarter = LENGTH // 4
    fine_cos, fine_sin = cosine(1, 0), cosine(1, quarter)
    coarse_cos, coarse_sin = cosine(16, 0), cosine(16, quarter)
    for a in range(16):
        c, s = coarse_cos[a : a + 1], coarse_sin[a : a + 1]
        for k, part in enumerate((c * fine_cos - s * fine_sin, -(s * fine_cos) - c * fine_sin)):
            for n, rounded in enumerate(halves(part)):
                rows = pl.ds(LENGTH + n * BINS + 16 * a, 16)
                tab[rows, k * half : (k + 1) * half] = rounded[:, :half]
                tab[rows, BINS + k * half : BINS + (k + 1) * half] = rounded[:, half:]


def whiten_body(outer, records, white, buf, tab, sems):
    segs = records.shape[0]
    core = jnp.bitwise_and(lax.axis_index("blk"), 1)
    begin = pl.multiple_of((core if outer else 1 - core) * ROWS, ROWS)

    def load(k):
        return pltpu.make_async_copy(records.at[k, pl.ds(begin, ROWS)], buf.at[k], sems.at[k])

    for k in range(segs):
        load(k).start()
    at = lax.broadcasted_iota(jnp.int32, (1, LENGTH), 1)
    count = jnp.minimum(at, SMOOTH) + jnp.minimum(LENGTH - 1 - at, SMOOTH) + 1
    share = 1.0 / count.astype(F32)
    make_tables(tab)

    def step(k, carry):
        load(k).wait()
        parts = range(ROWS // SUB)
        xs = [buf[k, pl.ds(n * SUB, SUB), :] for n in parts]
        levels = []
        first = tab[:REACHED, :BINS]
        second = tab[:REACHED, BINS:]
        for x in xs:
            ahi, alo = halves(jnp.abs(x))
            left = jnp.concatenate([ahi[:, :REACHED], alo[:, :REACHED]], axis=1)
            right = jnp.concatenate([ahi[:, LENGTH - REACHED :], alo[:, LENGTH - REACHED :]], axis=1)
            left = dot(left, jnp.concatenate([first, first], axis=0))
            right = dot(right, jnp.concatenate([second, second], axis=0))
            levels.append(jnp.concatenate([left, right], axis=1) * share)
        spectra = []
        products = []
        for at in (0, BINS):
            high = tab[LENGTH : LENGTH + BINS, at : at + BINS]
            products.append(jnp.concatenate([high, high, tab[LENGTH + BINS :, at : at + BINS]], axis=0))
        for x, level in zip(xs, levels):
            normed = x * pl.reciprocal(level + 1e-06, approx=True)
            left, right = normed[:, :BINS], normed[:, BINS:]
            pair = []
            for part, product in zip((left + right, left - right), products):
                high, low = halves(part)
                pair.append(dot(jnp.concatenate([high, low, high], axis=1), product))
            spectra.append(pair)
        same = jnp.concatenate([tab[REACHED:LENGTH, :BINS], tab[REACHED:LENGTH, BINS:]], axis=0)
        for n in parts:
            even, odd = spectra[n]
            re = jnp.concatenate([even[:, : BINS // 2], odd[:, : BINS // 2]], axis=1)
            im = jnp.concatenate([even[:, BINS // 2 :], odd[:, BINS // 2 :]], axis=1)
            power = dot((re * re + im * im).astype(BF), same)
            factor = lax.rsqrt(power + 1e-05)
            per = SUB // CHANS
            white[pl.ds(n * per, per), k, :, :BINS] = (re * factor).astype(BF).reshape(per, CHANS, BINS)
            white[pl.ds(n * per, per), k, :, BINS:] = (im * factor).astype(BF).reshape(per, CHANS, BINS)
        return carry

    lax.fori_loop(0, segs, step, 0)


def whiten(outer, records):
    segs = records.shape[0]
    return pl.pallas_call(
        functools.partial(whiten_body, outer),
        in_specs=[pl.BlockSpec(memory_space=pltpu.HBM)],
        out_specs=VMEM,
        out_shape=jax.ShapeDtypeStruct((HALF, segs, CHANS, LENGTH), BF),
        scratch_shapes=[
            pltpu.VMEM((segs, ROWS, LENGTH), F32),
            pltpu.VMEM((2 * LENGTH, LENGTH), BF),
            pltpu.SemaphoreType.DMA((segs,)),
        ],
        compiler_params=pltpu.CompilerParams(vmem_limit_bytes=50 * MIB),
        cost_estimate=TINY,
        name="whiten",
    )(records)


VISITS = [(p, d) for p in range(HALF) for d in range(1, REACH + 1) if p + d >= HALF] + [
    (p, d) for p in range(HALF, 12) for d in range(1, REACH + 1) if p < GROUP or p + d < 12
]
UPWARD = (
    ((0, 0), (1, 0), (1, 1), (2, 0), (2, 1), (3, 0), (3, 1)),
    ((2, 2), (3, 2), (3, 3)),
)


def seg_index():
    return lax.axis_index("seg").astype(jnp.int32)


def behind(owner):
    apart = jnp.bitwise_xor(seg_index(), owner)
    return 2 * jnp.bitwise_xor(apart, jnp.right_shift(apart, 1))


def list_pairs(own, before, codes, slots):
    s = seg_index()
    used = [jnp.int32(0)] * PLANES
    n = jnp.int32(0)
    for p, d in VISITS:
        row = p + HALF if p < HALF else p - HALF
        owner = row // 2
        live = (before if p < HALF else own)[behind(owner) + row % 2, d - 1]
        code = p + d * 16 + jnp.bitwise_xor(owner, s) * 256 + used[owner] * 4096
        slots[p * REACH + d - 1] = used[owner]
        used[owner] = used[owner] + live
        if p in (6, 7) and p + d in (12, 13):
            slots[96 + (p - 6) * 2 + p + d - 12] = used[0]
            code = code + (used[0] + 1) * 65536
            used[0] = used[0] + live
        codes[n] = code
        n = n + live
    return n


def plan_body(own, before, slots, plan):
    s = seg_index()
    n = jnp.int32(0)
    for owner in (0, 1):
        for k, (i, j) in enumerate(UPWARD[owner]):
            p, d = HALF + i, GROUP + j - i
            entry = p * REACH + d - 1 if i // 2 == owner else 96 + (i - 2) * 2 + j
            plan[MOVES + n] = slots[entry] + k * 4096
            n = n + jnp.where(s == owner, own[behind(i // 2) + i % 2, d - 1], 0)
    for r in range(1, PLANES):
        to = jnp.bitwise_xor(s, r)
        ahead = s < to
        for i in range(2):
            for j in range(2):
                row = 2 * s + i
                p = jnp.where(ahead, row + HALF, jnp.maximum(row - HALF, 0))
                d = 2 * to + j - row + jnp.where(ahead, 0, GROUP)
                live = jnp.where(ahead, own[i, d - 1], jnp.where(s >= 2, before[i, d - 1], 0))
                plan[MOVES + n] = slots[p * REACH + d - 1] + r * 256 + (2 * i + j) * 4096
                n = n + live
    plan[0] = n

    def write(n, i, d, base, size, slot):
        plan[WRITES + n] = base + slot * BODY + (base + size * BODY + slot) * 4096 + (i * 8 + d - 1) * 16777216

    n = jnp.int32(0)
    above = jnp.int32(0)
    for i in range(2):
        for d in range(1, REACH + 1):
            row = 2 * s + i
            live = own[i, d - 1]
            shift = (row + d >= GROUP) & (s >= 2)
            slot = jnp.where(shift, above, slots[(HALF + row) * REACH + d - 1])
            write(n, i, d, jnp.where(shift, TWO, 0), jnp.where(shift, SHIFTED, SLOTS), slot)
            n = n + live
            above = above + jnp.where(shift, live, 0)
    plan[1] = n
    for j in range(2):
        for d in range(1, REACH + 1):
            low = 2 * s + j - d
            crossing = low < 0
            row = jnp.where(crossing, low + GROUP, low)
            owner = jnp.right_shift(row, 1)
            at = behind(owner) + jnp.bitwise_and(row, 1)
            live = jnp.where(crossing, before[at, d - 1], own[at, d - 1])
            up = crossing & (owner < 2)
            mine = (owner == s) & jnp.logical_not(up)
            k0 = jnp.where(row == 0, 0, 2 * row - 1) + j
            k1 = jnp.where(row == 2, 0, 1) + j
            entry = jnp.maximum((HALF + low) * REACH + d - 1, 0)
            slot = jnp.where(mine, slots[entry], 2 * (row - 2 * owner) + j)
            slot = jnp.where(up, jnp.where(s == 0, k0, k1), slot)
            base = jnp.where(mine, 0, THREE + (jnp.bitwise_xor(s, owner) - 1) * SEND3)
            base = jnp.where(up, TWO, base)
            size = jnp.where(mine, SLOTS, jnp.where(up, SHIFTED, 4))
            write(n, j, d, base, size, slot)
            n = n + live
    plan[2] = n


def make_plan(*args):
    return pl.pallas_call(
        plan_body,
        in_specs=[SMEM] * 3,
        out_specs=SMEM,
        out_shape=jax.ShapeDtypeStruct((PLAN,), jnp.int32),
        compiler_params=pltpu.CompilerParams(vmem_limit_bytes=4 * MIB),
        cost_estimate=TINY,
        name="plan",
    )(*args)


def correlate_body(
    own, before, own_ext, own_int, got_ext, got_int, lag, keep, out1, out2, out3, slots, low, high, stk, pq, codes, last
):
    count = list_pairs(own, before, codes, slots)
    core = jnp.bitwise_and(lax.axis_index("blk"), 1)
    sources = (
        (own_ext, HALF * (1 + core)),
        (own_int, HALF * (2 - core)),
        (got_ext, 3 * HALF * core),
        (got_int, 3 * HALF * (1 - core)),
    )
    segs = low.shape[0]
    last[0] = -1

    def grab(dest, block):
        for ref, begin in sources:

            @pl.when((block >= begin) & (block < begin + HALF))
            def _(ref=ref, begin=begin):
                dest[...] = ref[block - begin]

    def put(r, n, stack):
        stk[r, pl.ds(pl.multiple_of(n * BODY, BODY), BODY), :] = stack[:BODY]
        stk[r, pl.ds(SLOTS * BODY + n, 1), :] = stack[BODY:LAGS]

    def pair(n, carry):
        code = codes[n]
        p = jnp.bitwise_and(code, 15)
        d = jnp.bitwise_and(jnp.right_shift(code, 4), 15)

        @pl.when(last[0] != p)
        def _():
            grab(low, p)
            last[0] = p

        grab(high, p + d)
        for chunk in range(CHANS // 16):
            rows = pl.ds(chunk * 16, 16)
            real = jnp.zeros((16, BINS), F32)
            imag = jnp.zeros((16, BINS), F32)
            for k in range(segs):
                are = low[k, rows, :BINS].astype(F32)
                aim = low[k, rows, BINS:].astype(F32)
                bre = high[k, rows, :BINS].astype(F32)
                bim = high[k, rows, BINS:].astype(F32)
                real += are * bre + aim * bim
                imag += are * bim - aim * bre
            rhi, rlo = halves(real)
            ihi, ilo = halves(imag)
            pq[0, rows, :BINS] = rhi
            pq[0, rows, BINS:] = ihi
            pq[1, rows, :BINS] = rlo
            pq[1, rows, BINS:] = ilo
        both = dot(pq[0], lag[...])
        stack = (both[:, :CHANS] + both[:, CHANS:] + dot(pq[1], lag[:, :CHANS])).T
        put(jnp.bitwise_and(jnp.right_shift(code, 8), 3), jnp.bitwise_and(jnp.right_shift(code, 12), 15), stack)
        second = jnp.right_shift(code, 16)

        @pl.when(second > 0)
        def _():
            put(seg_index(), second - 1, stack)

        return carry

    lax.fori_loop(0, count, pair, 0)
    keep[...] = stk[0]
    out1[...] = stk[1].astype(BF)
    out2[...] = stk[2].astype(BF)
    out3[...] = stk[3].astype(BF)


def correlate(own, before, whites, lag):
    segs = whites[0].shape[1]
    chunk = jax.ShapeDtypeStruct((CHUNK, CHANS), BF)
    return pl.pallas_call(
        correlate_body,
        in_specs=[SMEM] * 2 + [VMEM] * 5,
        out_specs=[VMEM] * 4 + [SMEM],
        out_shape=[
            jax.ShapeDtypeStruct((CHUNK, CHANS), F32),
            chunk,
            chunk,
            chunk,
            jax.ShapeDtypeStruct((128,), jnp.int32),
        ],
        scratch_shapes=[
            pltpu.VMEM((segs, CHANS, LENGTH), BF),
            pltpu.VMEM((segs, CHANS, LENGTH), BF),
            pltpu.VMEM((PLANES, CHUNK, CHANS), F32),
            pltpu.VMEM((2, CHANS, LENGTH), BF),
            pltpu.SMEM((PAIRS,), jnp.int32),
            pltpu.SMEM((1,), jnp.int32),
        ],
        compiler_params=pltpu.CompilerParams(vmem_limit_bytes=16 * MIB),
        cost_estimate=TINY,
        name="correlate",
    )(own, before, *whites, lag)


def combine_body(plan, keep, got1, got3, got2, full, send, out1, out2, out3, stage):
    full[...] = (keep[...] + got1[...].astype(F32)) + (got2[...].astype(F32) + got3[...].astype(F32))

    def move(n, carry):
        code = plan[MOVES + n]
        slot = jnp.bitwise_and(code, 255)
        message = jnp.bitwise_and(jnp.right_shift(code, 8), 15)
        k = jnp.right_shift(code, 12)
        size = jnp.where(message == 0, SHIFTED, 4)
        body = pl.ds(pl.multiple_of(slot * BODY, BODY), BODY)
        stage[message, pl.ds(pl.multiple_of(k * BODY, BODY), BODY), :] = full[body, :]
        stage[message, pl.ds(size * BODY + k, 1), :] = full[pl.ds(SLOTS * BODY + slot, 1), :]
        return carry

    lax.fori_loop(0, plan[0], move, 0)

    @pl.when(seg_index() >= 2)
    def _():
        send[: SHIFTED * BODY, :] = full[: SHIFTED * BODY, :].astype(BF)
        send[SHIFTED * BODY :, :] = full[SLOTS * BODY :, :].astype(BF)

    @pl.when(seg_index() < 2)
    def _():
        send[...] = stage[0].astype(BF)

    for r, out in ((1, out1), (2, out2), (3, out3)):
        out[:SEND3, :] = stage[r, :SEND3].astype(BF)


def combine(*args):
    third = jax.ShapeDtypeStruct((SEND3, CHANS), BF)
    return pl.pallas_call(
        combine_body,
        in_specs=[SMEM] + [VMEM] * 4,
        out_specs=[VMEM] * 5,
        out_shape=[
            jax.ShapeDtypeStruct((CHUNK, CHANS), F32),
            jax.ShapeDtypeStruct((SEND2, CHANS), BF),
            third,
            jax.ShapeDtypeStruct((SEND2, CHANS), BF),
            third,
        ],
        scratch_shapes=[pltpu.VMEM((PLANES, SEND2, CHANS), F32)],
        compiler_params=pltpu.CompilerParams(vmem_limit_bytes=8 * MIB),
        cost_estimate=TINY,
        name="combine",
    )(*args)


def finish_body(plan, full, got2, shifted, got1, got3, fwd, bwd, pool):
    pool[:TWO, :] = full[...]
    pool[TWO:THREE, :] = shifted[...].astype(F32)
    for r, got in ((1, got1), (2, got2), (3, got3)):
        pool[THREE + (r - 1) * SEND3 : THREE + r * SEND3, :] = got[:SEND3, :].astype(F32)
    fwd[...] = jnp.zeros(fwd.shape, F32)
    bwd[...] = jnp.zeros(bwd.shape, F32)

    def write(out, place, n):
        code = plan[WRITES + n]
        body = jnp.bitwise_and(code, 4095)
        i = jnp.right_shift(code, 27)
        at = pl.ds(jnp.bitwise_and(jnp.right_shift(code, 24), 7), 1)
        out[i, place(BODY), at, :] = pool[pl.ds(jnp.bitwise_and(jnp.right_shift(code, 12), 4095), 1), :]
        for m in range(BODY):
            out[i, place(m), at, :] = pool[pl.ds(body + m, 1), :]

    def ahead(n, carry):
        write(fwd, lambda m: m, n)
        return carry

    def behind(n, carry):
        write(bwd, lambda m: BODY - m, n)
        return carry

    lax.fori_loop(0, plan[1], ahead, 0)
    lax.fori_loop(plan[1], plan[2], behind, 0)


def finish(blocks, *args):
    out = jax.ShapeDtypeStruct((blocks, LAGS, REACH, CHANS), F32)
    return pl.pallas_call(
        finish_body,
        in_specs=[SMEM] + [VMEM] * 5,
        out_specs=[VMEM, VMEM],
        out_shape=[out, out],
        scratch_shapes=[pltpu.VMEM((POOL, CHANS), F32)],
        compiler_params=pltpu.CompilerParams(vmem_limit_bytes=8 * MIB),
        cost_estimate=TINY,
        name="finish",
    )(*args)


def shards(groups, planes, lag, records, pairs):
    def across(x, r):
        return lax.ppermute(x, "seg", [(z, z ^ r) for z in range(planes)])

    outer = [(g, g + 1 if g % 2 else g - 1) for g in range(1, groups - 1)]
    inner = [(g, g ^ 1) for g in range(groups)]
    upward = [(g, g + 1) for g in range(groups - 1)]
    shift = [
        (z * groups + g, z * groups + g + step)
        for z in range(planes)
        for g in range(groups)
        for step in (1 if z < 2 else -1,)
        if 0 <= g + step < groups
    ]
    own_ext = whiten(True, records)
    got_ext = lax.ppermute(own_ext, "blk", outer)
    own_int = whiten(False, records)
    got_int = lax.ppermute(own_int, "blk", inner)
    rows, _ = lax.optimization_barrier((pairs, own_int))
    own = jnp.concatenate([rows, across(rows, 1), across(rows, 3), across(rows, 2)])
    before = lax.ppermute(own, "blk", upward)

    keep, out1, out2, out3, slots = correlate(own, before, (own_ext, own_int, got_ext, got_int), lag)
    plan = make_plan(own, before, slots)
    full, send, out1, out2, out3 = combine(plan, keep, across(out1, 1), across(out3, 3), across(out2, 2))
    shifted = lax.ppermute(send, ("seg", "blk"), shift)
    outs = finish(pairs.shape[0], plan, full, across(out2, 2), shifted, across(out1, 1), across(out3, 3))
    return tuple(jnp.transpose(out, (0, 2, 1, 3)) for out in outs)


def solution(mesh):
    groups = mesh.shape["blk"]
    planes = mesh.shape["seg"]

    def run(records, pairs):
        body = functools.partial(
            shards,
            groups,
            planes,
            jnp.asarray(lag_rows(records.shape[0])),
        )
        return jax.shard_map(
            body,
            mesh=mesh,
            in_specs=(P("seg", "blk", None), P(("blk", "seg"), None)),
            out_specs=(P(("blk", "seg"), None, None, None), P(("blk", "seg"), None, None, None)),
            check_vma=False,
        )(records, pairs)

    return run
```

```python
import functools

import jax
import jax.numpy as jnp
import ml_dtypes
import numpy as np
from jax import lax
from jax.experimental import pallas as pl
from jax.experimental.pallas import tpu as pltpu
from jax.sharding import PartitionSpec as P

BINS = 256
LENGTH = 512
CHANS = 128
MAXLAG = 32
LAGS = 2 * MAXLAG + 1
REACH = 8
SMOOTH = 32
BAND = 64
GROUP = 8
HALF = GROUP // 2
PLANES = 4
ROWS = HALF * CHANS
SUB = ROWS
REACHED = 384
SLOTS = 13
SHIFTED = 8
BODY = 64
CHUNK = SLOTS * BODY + 16
SEND2 = SHIFTED * BODY + 16
SEND3 = 4 * BODY + 16
PAIRS, MOVES, WRITES, PLAN = 48, 8, 40, 128
TWO = CHUNK
THREE = CHUNK + SEND2
POOL = THREE + 3 * SEND3
MIB = 1024 * 1024
TINY = pl.CostEstimate(flops=1, bytes_accessed=1, transcendentals=0)
BF = jnp.bfloat16
F32 = jnp.float32
SMEM = pl.BlockSpec(memory_space=pltpu.SMEM)
VMEM = pl.BlockSpec(memory_space=pltpu.VMEM)


def split(array):
    high = array.astype(ml_dtypes.bfloat16)
    low = (array - high.astype(np.float32)).astype(ml_dtypes.bfloat16)
    return high, low


def lag_rows(segments):
    freqs = np.concatenate([np.arange(0, BINS, 2), np.arange(1, BINS, 2)])
    shifts = np.arange(-MAXLAG, MAXLAG + 1)
    phase = (shifts[:, None] * freqs[None, :] % LENGTH) * (2.0 * np.pi / LENGTH)
    table = np.concatenate([np.cos(phase), -np.sin(phase)], axis=1) / np.sqrt(segments * BINS)
    table = np.concatenate([table, np.zeros((CHANS - LAGS, LENGTH))], axis=0).T.astype(np.float32)
    return np.concatenate(split(table), axis=1)


def dot(a, b):
    return jnp.dot(a, b, preferred_element_type=F32)


def halves(x):
    high = x.astype(BF)
    return high, (x - high.astype(F32)).astype(BF)


def make_tables(tab):
    at = lax.broadcasted_iota(jnp.int32, (REACHED, LENGTH), 0)
    col = lax.broadcasted_iota(jnp.int32, (REACHED, LENGTH), 1)
    apart = at - col + jnp.where(col < BINS, 0, LENGTH - REACHED)
    tab[:REACHED] = jnp.where(jnp.abs(apart) <= SMOOTH, 1.0, 0.0).astype(BF)
    half = BINS // 2
    row = lax.broadcasted_iota(jnp.int32, (CHANS, LENGTH), 0)
    col = lax.broadcasted_iota(jnp.int32, (CHANS, LENGTH), 1)
    row = jnp.bitwise_and(row, half - 1) // (BAND // 2)
    col = jnp.bitwise_and(col, half - 1) // (BAND // 2)
    tab[REACHED:LENGTH] = jnp.where(row == col, 0.5 / BAND, 0.0).astype(BF)

    def cosine(step, shift):
        col = lax.broadcasted_iota(jnp.int32, (16, BINS), 1)
        freq = 2 * jnp.bitwise_and(col, half - 1) + jnp.right_shift(col, 7)
        k = lax.broadcasted_iota(jnp.int32, (16, BINS), 0) * freq
        k = jnp.bitwise_and(k * step - shift + BINS, LENGTH - 1) - BINS
        square = jnp.square(k.astype(F32) * (2.0 * np.pi / LENGTH))
        value = jnp.ones_like(square)
        for n in range(20, 0, -2):
            value = 1.0 - value * square * (1.0 / (n * (n - 1)))
        return value

    quarter = LENGTH // 4
    fine_cos, fine_sin = cosine(1, 0), cosine(1, quarter)
    coarse_cos, coarse_sin = cosine(16, 0), cosine(16, quarter)
    for a in range(16):
        c, s = coarse_cos[a : a + 1], coarse_sin[a : a + 1]
        for k, part in enumerate((c * fine_cos - s * fine_sin, -(s * fine_cos) - c * fine_sin)):
            for n, rounded in enumerate(halves(part)):
                rows = pl.ds(LENGTH + n * BINS + 16 * a, 16)
                tab[rows, k * half : (k + 1) * half] = rounded[:, :half]
                tab[rows, BINS + k * half : BINS + (k + 1) * half] = rounded[:, half:]


def whiten_body(outer, records, white, buf, tab, sems):
    segs = records.shape[0]
    core = jnp.bitwise_and(lax.axis_index("blk"), 1)
    begin = pl.multiple_of((core if outer else 1 - core) * ROWS, ROWS)

    def load(k):
        return pltpu.make_async_copy(records.at[k, pl.ds(begin, ROWS)], buf.at[k], sems.at[k])

    load(0).start()
    at = lax.broadcasted_iota(jnp.int32, (1, LENGTH), 1)
    count = jnp.minimum(at, SMOOTH) + jnp.minimum(LENGTH - 1 - at, SMOOTH) + 1
    share = 1.0 / count.astype(F32)
    make_tables(tab)
    for k in range(1, segs):
        load(k).start()

    def step(k, carry):
        load(k).wait()
        parts = range(ROWS // SUB)
        xs = [buf[k, pl.ds(n * SUB, SUB), :] for n in parts]
        levels = []
        first = tab[:REACHED, :BINS]
        second = tab[:REACHED, BINS:]
        for x in xs:
            ahi, alo = halves(jnp.abs(x))
            left = jnp.concatenate([ahi[:, :REACHED], alo[:, :REACHED]], axis=1)
            right = jnp.concatenate([ahi[:, LENGTH - REACHED :], alo[:, LENGTH - REACHED :]], axis=1)
            left = dot(left, jnp.concatenate([first, first], axis=0))
            right = dot(right, jnp.concatenate([second, second], axis=0))
            levels.append(jnp.concatenate([left, right], axis=1) * share)
        spectra = []
        products = []
        for at in (0, BINS):
            high = tab[LENGTH : LENGTH + BINS, at : at + BINS]
            products.append(jnp.concatenate([high, high, tab[LENGTH + BINS :, at : at + BINS]], axis=0))
        for x, level in zip(xs, levels):
            normed = x * pl.reciprocal(level + 1e-06, approx=True)
            left, right = normed[:, :BINS], normed[:, BINS:]
            pair = []
            for part, product in zip((left + right, left - right), products):
                high, low = halves(part)
                pair.append(dot(jnp.concatenate([high, low, high], axis=1), product))
            spectra.append(pair)
        same = jnp.concatenate([tab[REACHED:LENGTH, :BINS], tab[REACHED:LENGTH, BINS:]], axis=0)
        for n in parts:
            even, odd = spectra[n]
            re = jnp.concatenate([even[:, : BINS // 2], odd[:, : BINS // 2]], axis=1)
            im = jnp.concatenate([even[:, BINS // 2 :], odd[:, BINS // 2 :]], axis=1)
            power = dot((re * re + im * im).astype(BF), same)
            factor = lax.rsqrt(power + 1e-05)
            per = SUB // CHANS
            white[pl.ds(n * per, per), k, :, :BINS] = (re * factor).astype(BF).reshape(per, CHANS, BINS)
            white[pl.ds(n * per, per), k, :, BINS:] = (im * factor).astype(BF).reshape(per, CHANS, BINS)
        return carry

    lax.fori_loop(0, segs, step, 0)


def whiten(outer, records):
    segs = records.shape[0]
    return pl.pallas_call(
        functools.partial(whiten_body, outer),
        in_specs=[pl.BlockSpec(memory_space=pltpu.HBM)],
        out_specs=VMEM,
        out_shape=jax.ShapeDtypeStruct((HALF, segs, CHANS, LENGTH), BF),
        scratch_shapes=[
            pltpu.VMEM((segs, ROWS, LENGTH), F32),
            pltpu.VMEM((2 * LENGTH, LENGTH), BF),
            pltpu.SemaphoreType.DMA((segs,)),
        ],
        compiler_params=pltpu.CompilerParams(vmem_limit_bytes=50 * MIB),
        cost_estimate=TINY,
        name="whiten",
    )(records)


VISITS = [(p, d) for p in range(HALF) for d in range(1, REACH + 1) if p + d >= HALF] + [
    (p, d) for p in range(HALF, 12) for d in range(1, REACH + 1) if p < GROUP or p + d < 12
]
UPWARD = (
    ((0, 0), (1, 0), (1, 1), (2, 0), (2, 1), (3, 0), (3, 1)),
    ((2, 2), (3, 2), (3, 3)),
)


def seg_index():
    return lax.axis_index("seg").astype(jnp.int32)


def behind(owner):
    apart = jnp.bitwise_xor(seg_index(), owner)
    return 2 * jnp.bitwise_xor(apart, jnp.right_shift(apart, 1))


def list_pairs(own, before, codes, slots):
    s = seg_index()
    used = [jnp.int32(0)] * PLANES
    n = jnp.int32(0)
    for p, d in VISITS:
        row = p + HALF if p < HALF else p - HALF
        owner = row // 2
        live = (before if p < HALF else own)[behind(owner) + row % 2, d - 1]
        code = p + d * 16 + jnp.bitwise_xor(owner, s) * 256 + used[owner] * 4096
        slots[p * REACH + d - 1] = used[owner]
        used[owner] = used[owner] + live
        if p in (6, 7) and p + d in (12, 13):
            slots[96 + (p - 6) * 2 + p + d - 12] = used[0]
            code = code + (used[0] + 1) * 65536
            used[0] = used[0] + live
        codes[n] = code
        n = n + live
    return n


def plan_body(own, before, slots, plan):
    s = seg_index()
    n = jnp.int32(0)
    for owner in (0, 1):
        for k, (i, j) in enumerate(UPWARD[owner]):
            p, d = HALF + i, GROUP + j - i
            entry = p * REACH + d - 1 if i // 2 == owner else 96 + (i - 2) * 2 + j
            plan[MOVES + n] = slots[entry] + k * 4096
            n = n + jnp.where(s == owner, own[behind(i // 2) + i % 2, d - 1], 0)
    for r in range(1, PLANES):
        to = jnp.bitwise_xor(s, r)
        ahead = s < to
        for i in range(2):
            for j in range(2):
                row = 2 * s + i
                p = jnp.where(ahead, row + HALF, jnp.maximum(row - HALF, 0))
                d = 2 * to + j - row + jnp.where(ahead, 0, GROUP)
                live = jnp.where(ahead, own[i, d - 1], jnp.where(s >= 2, before[i, d - 1], 0))
                plan[MOVES + n] = slots[p * REACH + d - 1] + r * 256 + (2 * i + j) * 4096
                n = n + live
    plan[0] = n

    def write(n, i, d, base, size, slot):
        plan[WRITES + n] = base + slot * BODY + (base + size * BODY + slot) * 4096 + (i * 8 + d - 1) * 16777216

    n = jnp.int32(0)
    above = jnp.int32(0)
    for i in range(2):
        for d in range(1, REACH + 1):
            row = 2 * s + i
            live = own[i, d - 1]
            shift = (row + d >= GROUP) & (s >= 2)
            slot = jnp.where(shift, above, slots[(HALF + row) * REACH + d - 1])
            write(n, i, d, jnp.where(shift, TWO, 0), jnp.where(shift, SHIFTED, SLOTS), slot)
            n = n + live
            above = above + jnp.where(shift, live, 0)
    plan[1] = n
    for j in range(2):
        for d in range(1, REACH + 1):
            low = 2 * s + j - d
            crossing = low < 0
            row = jnp.where(crossing, low + GROUP, low)
            owner = jnp.right_shift(row, 1)
            at = behind(owner) + jnp.bitwise_and(row, 1)
            live = jnp.where(crossing, before[at, d - 1], own[at, d - 1])
            up = crossing & (owner < 2)
            mine = (owner == s) & jnp.logical_not(up)
            k0 = jnp.where(row == 0, 0, 2 * row - 1) + j
            k1 = jnp.where(row == 2, 0, 1) + j
            entry = jnp.maximum((HALF + low) * REACH + d - 1, 0)
            slot = jnp.where(mine, slots[entry], 2 * (row - 2 * owner) + j)
            slot = jnp.where(up, jnp.where(s == 0, k0, k1), slot)
            base = jnp.where(mine, 0, THREE + (jnp.bitwise_xor(s, owner) - 1) * SEND3)
            base = jnp.where(up, TWO, base)
            size = jnp.where(mine, SLOTS, jnp.where(up, SHIFTED, 4))
            write(n, j, d, base, size, slot)
            n = n + live
    plan[2] = n


def make_plan(*args):
    return pl.pallas_call(
        plan_body,
        in_specs=[SMEM] * 3,
        out_specs=SMEM,
        out_shape=jax.ShapeDtypeStruct((PLAN,), jnp.int32),
        compiler_params=pltpu.CompilerParams(vmem_limit_bytes=4 * MIB),
        cost_estimate=TINY,
        name="plan",
    )(*args)


def correlate_body(
    own, before, own_ext, own_int, got_ext, got_int, lag, keep, out1, out2, out3, slots, low, high, stk, pq, codes, last
):
    count = list_pairs(own, before, codes, slots)
    core = jnp.bitwise_and(lax.axis_index("blk"), 1)
    sources = (
        (own_ext, HALF * (1 + core)),
        (own_int, HALF * (2 - core)),
        (got_ext, 3 * HALF * core),
        (got_int, 3 * HALF * (1 - core)),
    )
    segs = low.shape[0]
    last[0] = -1

    def grab(dest, block):
        for ref, begin in sources:

            @pl.when((block >= begin) & (block < begin + HALF))
            def _(ref=ref, begin=begin):
                dest[...] = ref[block - begin]

    def put(r, n, stack):
        stk[r, pl.ds(pl.multiple_of(n * BODY, BODY), BODY), :] = stack[:BODY]
        stk[r, pl.ds(SLOTS * BODY + n, 1), :] = stack[BODY:LAGS]

    def pair(n, carry):
        code = codes[n]
        p = jnp.bitwise_and(code, 15)
        d = jnp.bitwise_and(jnp.right_shift(code, 4), 15)

        @pl.when(last[0] != p)
        def _():
            grab(low, p)
            last[0] = p

        grab(high, p + d)
        for chunk in range(CHANS // 16):
            rows = pl.ds(chunk * 16, 16)
            real = jnp.zeros((16, BINS), F32)
            imag = jnp.zeros((16, BINS), F32)
            for k in range(segs):
                are = low[k, rows, :BINS].astype(F32)
                aim = low[k, rows, BINS:].astype(F32)
                bre = high[k, rows, :BINS].astype(F32)
                bim = high[k, rows, BINS:].astype(F32)
                real += are * bre + aim * bim
                imag += are * bim - aim * bre
            rhi, rlo = halves(real)
            ihi, ilo = halves(imag)
            pq[0, rows, :BINS] = rhi
            pq[0, rows, BINS:] = ihi
            pq[1, rows, :BINS] = rlo
            pq[1, rows, BINS:] = ilo
        both = dot(pq[0], lag[...])
        stack = (both[:, :CHANS] + both[:, CHANS:] + dot(pq[1], lag[:, :CHANS])).T
        put(jnp.bitwise_and(jnp.right_shift(code, 8), 3), jnp.bitwise_and(jnp.right_shift(code, 12), 15), stack)
        second = jnp.right_shift(code, 16)

        @pl.when(second > 0)
        def _():
            put(seg_index(), second - 1, stack)

        return carry

    lax.fori_loop(0, count, pair, 0)
    keep[...] = stk[0]
    out1[...] = stk[1].astype(BF)
    out2[...] = stk[2].astype(BF)
    out3[...] = stk[3].astype(BF)


def correlate(own, before, whites, lag):
    segs = whites[0].shape[1]
    chunk = jax.ShapeDtypeStruct((CHUNK, CHANS), BF)
    return pl.pallas_call(
        correlate_body,
        in_specs=[SMEM] * 2 + [VMEM] * 5,
        out_specs=[VMEM] * 4 + [SMEM],
        out_shape=[
            jax.ShapeDtypeStruct((CHUNK, CHANS), F32),
            chunk,
            chunk,
            chunk,
            jax.ShapeDtypeStruct((128,), jnp.int32),
        ],
        scratch_shapes=[
            pltpu.VMEM((segs, CHANS, LENGTH), BF),
            pltpu.VMEM((segs, CHANS, LENGTH), BF),
            pltpu.VMEM((PLANES, CHUNK, CHANS), F32),
            pltpu.VMEM((2, CHANS, LENGTH), BF),
            pltpu.SMEM((PAIRS,), jnp.int32),
            pltpu.SMEM((1,), jnp.int32),
        ],
        compiler_params=pltpu.CompilerParams(vmem_limit_bytes=16 * MIB),
        cost_estimate=TINY,
        name="correlate",
    )(own, before, *whites, lag)


def combine_body(plan, keep, got1, got3, got2, full, send, out1, out2, out3, stage):
    full[...] = (keep[...] + got1[...].astype(F32)) + (got2[...].astype(F32) + got3[...].astype(F32))

    def move(n, carry):
        code = plan[MOVES + n]
        slot = jnp.bitwise_and(code, 255)
        message = jnp.bitwise_and(jnp.right_shift(code, 8), 15)
        k = jnp.right_shift(code, 12)
        size = jnp.where(message == 0, SHIFTED, 4)
        body = pl.ds(pl.multiple_of(slot * BODY, BODY), BODY)
        stage[message, pl.ds(pl.multiple_of(k * BODY, BODY), BODY), :] = full[body, :]
        stage[message, pl.ds(size * BODY + k, 1), :] = full[pl.ds(SLOTS * BODY + slot, 1), :]
        return carry

    lax.fori_loop(0, plan[0], move, 0)

    @pl.when(seg_index() >= 2)
    def _():
        send[: SHIFTED * BODY, :] = full[: SHIFTED * BODY, :].astype(BF)
        send[SHIFTED * BODY :, :] = full[SLOTS * BODY :, :].astype(BF)

    @pl.when(seg_index() < 2)
    def _():
        send[...] = stage[0].astype(BF)

    for r, out in ((1, out1), (2, out2), (3, out3)):
        out[:SEND3, :] = stage[r, :SEND3].astype(BF)


def combine(*args):
    third = jax.ShapeDtypeStruct((SEND3, CHANS), BF)
    return pl.pallas_call(
        combine_body,
        in_specs=[SMEM] + [VMEM] * 4,
        out_specs=[VMEM] * 5,
        out_shape=[
            jax.ShapeDtypeStruct((CHUNK, CHANS), F32),
            jax.ShapeDtypeStruct((SEND2, CHANS), BF),
            third,
            jax.ShapeDtypeStruct((SEND2, CHANS), BF),
            third,
        ],
        scratch_shapes=[pltpu.VMEM((PLANES, SEND2, CHANS), F32)],
        compiler_params=pltpu.CompilerParams(vmem_limit_bytes=8 * MIB),
        cost_estimate=TINY,
        name="combine",
    )(*args)


def finish_body(plan, full, got2, shifted, got1, got3, fwd, bwd, pool):
    pool[:TWO, :] = full[...]
    pool[TWO:THREE, :] = shifted[...].astype(F32)
    for r, got in ((1, got1), (2, got2), (3, got3)):
        pool[THREE + (r - 1) * SEND3 : THREE + r * SEND3, :] = got[:SEND3, :].astype(F32)
    fwd[...] = jnp.zeros(fwd.shape, F32)
    bwd[...] = jnp.zeros(bwd.shape, F32)

    def write(out, place, n):
        code = plan[WRITES + n]
        body = jnp.bitwise_and(code, 4095)
        i = jnp.right_shift(code, 27)
        at = pl.ds(jnp.bitwise_and(jnp.right_shift(code, 24), 7), 1)
        out[i, place(BODY), at, :] = pool[pl.ds(jnp.bitwise_and(jnp.right_shift(code, 12), 4095), 1), :]
        for m in range(BODY):
            out[i, place(m), at, :] = pool[pl.ds(body + m, 1), :]

    def ahead(n, carry):
        write(fwd, lambda m: m, n)
        return carry

    def behind(n, carry):
        write(bwd, lambda m: BODY - m, n)
        return carry

    lax.fori_loop(0, plan[1], ahead, 0)
    lax.fori_loop(plan[1], plan[2], behind, 0)


def finish(blocks, *args):
    out = jax.ShapeDtypeStruct((blocks, LAGS, REACH, CHANS), F32)
    return pl.pallas_call(
        finish_body,
        in_specs=[SMEM] + [VMEM] * 5,
        out_specs=[VMEM, VMEM],
        out_shape=[out, out],
        scratch_shapes=[pltpu.VMEM((POOL, CHANS), F32)],
        compiler_params=pltpu.CompilerParams(vmem_limit_bytes=8 * MIB),
        cost_estimate=TINY,
        name="finish",
    )(*args)


def shards(groups, planes, lag, records, pairs):
    def across(x, r):
        return lax.ppermute(x, "seg", [(z, z ^ r) for z in range(planes)])

    outer = [(g, g + 1 if g % 2 else g - 1) for g in range(1, groups - 1)]
    inner = [(g, g ^ 1) for g in range(groups)]
    upward = [(g, g + 1) for g in range(groups - 1)]
    shift = [
        (z * groups + g, z * groups + g + step)
        for z in range(planes)
        for g in range(groups)
        for step in (1 if z < 2 else -1,)
        if 0 <= g + step < groups
    ]
    own_ext = whiten(True, records)
    got_ext = lax.ppermute(own_ext, "blk", outer)
    own_int = whiten(False, records)
    got_int = lax.ppermute(own_int, "blk", inner)
    rows, _ = lax.optimization_barrier((pairs, own_int))
    own = jnp.concatenate([rows, across(rows, 1), across(rows, 3), across(rows, 2)])
    before = lax.ppermute(own, "blk", upward)

    keep, out1, out2, out3, slots = correlate(own, before, (own_ext, own_int, got_ext, got_int), lag)
    plan = make_plan(own, before, slots)
    full, send, out1, out2, out3 = combine(plan, keep, across(out1, 1), across(out3, 3), across(out2, 2))
    shifted = lax.ppermute(send, ("seg", "blk"), shift)
    outs = finish(pairs.shape[0], plan, full, across(out2, 2), shifted, across(out1, 1), across(out3, 3))
    return tuple(jnp.transpose(out, (0, 2, 1, 3)) for out in outs)


def solution(mesh):
    groups = mesh.shape["blk"]
    planes = mesh.shape["seg"]

    def run(records, pairs):
        body = functools.partial(
            shards,
            groups,
            planes,
            jnp.asarray(lag_rows(records.shape[0])),
        )
        return jax.shard_map(
            body,
            mesh=mesh,
            in_specs=(P("seg", "blk", None), P(("blk", "seg"), None)),
            out_specs=(P(("blk", "seg"), None, None, None), P(("blk", "seg"), None, None, None)),
            check_vma=False,
        )(records, pairs)

    return run
```
